32 devices in a mesh: head: 4 (over y, x), seq: 8 (over z, core).
Axes of the slice: x: 2, y: 2, z: 4, core: 2. Of those that a mesh axis runs over, the one named last changes fastest.
Arguments:
- inputs: bfloat16 [2, 2048, 2048], P(None, ('seq', 'head')), may hold values from -6 to 6
- cotangent: bfloat16 [2, 2048, 2048], P(None, ('seq', 'head')), may hold values from -6 to 6
- routes: int32 [2, 2048, 6], P(None, 'seq'), may hold values from 0 to 15, all different within a row; in each aligned block of 256 rows (0 to 255, 256 to 511, ..., all dimensions but the last counted through in order) at most 128 rows name the same one
- gate_weights: float32 [2, 2048, 6], P(None, 'seq'), may hold values from 0.2 to 0.8
- attn_gain: bfloat16 [2048], P('seq'), may hold values from 0.099609375 to 1.8984375
- latent_gain: bfloat16 [512], P('seq'), may hold values from 0.099609375 to 1.8984375
- ffn_gain: bfloat16 [2048], P('seq'), may hold values from 0.099609375 to 1.8984375
- query_proj: bfloat16 [2048, 3072], P('seq', 'head'), may hold values from -0.125 to 0.125
- latent_proj: bfloat16 [2048, 576], P('seq'), may hold values from -0.125 to 0.125
- expand_proj: bfloat16 [512, 4096], P('seq', 'head'), may hold values from -0.25 to 0.25
- out_proj: bfloat16 [2048, 2048], P('head', 'seq'), may hold values from -3 to 3
- shared_gate: bfloat16 [2048, 2816], P('seq', 'head'), may hold values from -0.125 to 0.125
- shared_up: bfloat16 [2048, 2816], P('seq', 'head'), may hold values from -0.125 to 0.125
- shared_down: bfloat16 [2816, 2048], P('head', 'seq'), may hold values from -0.109375 to 0.109375
- expert_gate: bfloat16 [32, 2048, 704], P(('seq', 'head')), may hold values from -0.125 to 0.125
- expert_up_weight: bfloat16 [32, 2048, 704], P(('seq', 'head')), may hold values from -0.125 to 0.125
- expert_down: bfloat16 [32, 704, 2048], P(('seq', 'head')), may hold values from -0.15625 to 0.15625
Outputs:
- output: bfloat16 [2, 2048, 2048], P(None, ('seq', 'head'))
- inputs_grad: bfloat16 [2, 2048, 2048], P(None, ('seq', 'head'))
- query_grad: float32 [2048, 3072], P('seq', 'head')
- latent_grad: float32 [2048, 576], P('seq')
- expand_grad: float32 [512, 4096], P('seq', 'head')
- outproj_grad: float32 [2048, 2048], P('head', 'seq')
- shgate_grad: float32 [2048, 2816], P('seq', 'head')
- shup_grad: float32 [2048, 2816], P('seq', 'head')
- shdown_grad: float32 [2816, 2048], P('head', 'seq')
- exgate_grad: float32 [32, 2048, 704], P(('seq', 'head'))
- exup_grad: float32 [32, 2048, 704], P(('seq', 'head'))
- exdown_grad: float32 [32, 704, 2048], P(('seq', 'head'))
- attngain_grad: float32 [2048], P('seq')
- latgain_grad: float32 [512], P('seq')
- ffngain_grad: float32 [2048], P('seq')
The draws below stay inside these ranges and needn't reach their ends.
Inputs may be any that keep to these rules, and one draw needn't show every extreme that they name: `routes`: in each aligned block of 256 rows along a sequence, no expert is named by more than 128 rows, and in some block one expert is named by exactly 128.
All inputs are finite; a program needn't handle non-finite values.
Results may differ from the reference program's by a relative error of at most 0.03.
Values may be sent and summed in bfloat16 or wider, within the bound.
No kernel may reach another device: no remote copies, remote signals or barrier semaphores. Data moves between devices by JAX's collectives and lax.ppermute only.
A program may use at most 320 MiB of HBM per device.

```python
import math
import jax
import jax.numpy as jnp
import numpy as np
from jax import lax

D = 2048
HEADS = 16
HDIM = 128
RDIM = 64
RANK = 512
FF = 1408
SHARED = 2816
TOPK = 6
BLOCK = 256
BATCH = 2
QDIM = 192
CH = 256
SEQ_LEN = 2048
EXPERTS = 16
MOST = 128


def shard_levels(rng, dims, split, low, high):
    level = 1.0
    for position, blocks in split:
        steps = jax.random.uniform(jax.random.fold_in(jax.random.fold_in(rng, 6), position), (blocks,), jnp.float32, low / len(split), high / len(split))
        level = level * jnp.repeat(jnp.exp(steps), dims[position] // blocks).reshape((-1,) + (1,) * (len(dims) - 1 - position))
    return level


def routed_block(own_key, own, number, rows, number_of, top, limit, skew):
    sequence = jax.random.permutation(own_key, number_of)
    crowded, ordinary = load_shares(number_of, rows * top, limit, skew, True), load_shares(number_of, rows * top, limit, skew, False)
    places = jnp.arange(number_of)

    def named(lengths, turn):
        used = int((lengths > 0).sum())
        fixed = max(1, used // 4)
        moved = fixed + (places - fixed + turn * (used - fixed)) % max(1, number_of - fixed)
        return jnp.zeros((number_of,), jnp.int32).at[sequence[jnp.where(places < fixed, places, moved)]].set(jnp.asarray(lengths, jnp.int32))

    lengths = jnp.where(number % 4 == 0, named(crowded, number // 4), named(ordinary, number - number // 4 - 1))
    mixed = jax.random.permutation(jax.random.fold_in(own, 3), number_of)
    donor, receiver = mixed[0:number_of // 2 * 2:2], mixed[1:number_of // 2 * 2:2]
    slack = jnp.minimum(lengths[donor] - 1, limit - lengths[receiver]) // 2
    slack = jnp.where((donor == sequence[0]) | (receiver == sequence[0]) | (lengths[receiver] == 0), 0, jnp.maximum(slack, 0))
    moved = jax.random.randint(jax.random.fold_in(own, 4), (number_of // 2,), 0, 1 << 20) % (slack + 1)
    lengths = lengths.at[donor].add(-moved).at[receiver].add(moved)
    members = jnp.searchsorted(jnp.cumsum(lengths), jnp.arange(rows * top), side="right").astype(jnp.int32)
    grid = members.reshape(top, rows).T
    grid = grid[jax.random.permutation(jax.random.fold_in(own, 1), rows)]
    turn = jax.random.randint(jax.random.fold_in(own, 2), (rows, 1), 0, top)
    return jnp.take_along_axis(grid, (jnp.arange(top)[None, :] + turn) % top, axis=1)


def load_shares(count, total, bound, lean, full):
    loads = [(1 << 20) // math.isqrt(standing ** lean) + 1 for standing in range(1, count + 1)]
    largest = bound if full else min(bound, max(-(-total // count), total * loads[0] // sum(loads)))
    least = 1 if total - largest >= count - 1 else 0
    holding, rest = [largest] + [least] * (count - 1), total - largest - least * (count - 1)
    while rest > 0:
        candidates = [i for i in range(1, count) if holding[i] < largest] or [i for i in range(1, count) if holding[i] < bound]
        whole, budget = sum([loads[i] for i in candidates]), rest
        for i in candidates:
            addition = min(bound - holding[i], max(1, budget * loads[i] // whole), rest)
            holding[i] = holding[i] + addition
            rest = rest - addition
    return np.array(holding)


def scatter_about(rng, extent, deviation, bound, split=(), kind=jnp.bfloat16):
    values = deviation * jax.random.normal(rng, extent, jnp.float32)
    if split:
        values = values * shard_levels(rng, extent, split, -0.22, 0.18)
    return jnp.clip(values, -bound, bound).astype(kind)


def setup_inputs(seed: int = 0) -> dict:
    key_list = jax.random.split(jax.random.key(seed), 18)
    inputs = scatter_about(key_list[0], (BATCH, SEQ_LEN, D), 1.0, 6.0, ((1, 32),))
    cotangent = scatter_about(key_list[1], (BATCH, SEQ_LEN, D), 1.0, 6.0, ((1, 32),))
    routes_keys = jax.random.split(jax.random.fold_in(key_list[2], 1), BATCH * SEQ_LEN // CH)
    routes_turns = jax.random.permutation(jax.random.fold_in(key_list[2], 3), BATCH * SEQ_LEN // CH)
    routes = jax.vmap(lambda own, number: routed_block(jax.random.fold_in(key_list[2], 2), own, number, CH, EXPERTS, TOPK, MOST, 1))(routes_keys, routes_turns).reshape((BATCH, SEQ_LEN, TOPK))
    gate_weights = jnp.clip(jnp.exp(math.log(0.8) - 1.3862944 * jax.random.uniform(key_list[3], (BATCH, SEQ_LEN, TOPK), jnp.float32) ** shard_levels(key_list[3], (BATCH, SEQ_LEN, TOPK), ((1, 8),), -0.2, 0.2)), 0.2, 0.8)
    attn_gain = jnp.clip(1.0 + 0.18 * jax.random.normal(key_list[4], (D,), jnp.float32), 0.099609375, 1.8984375).astype(jnp.bfloat16)
    latent_gain = jnp.clip(1.0 + 0.18 * jax.random.normal(key_list[5], (RANK,), jnp.float32), 0.099609375, 1.8984375).astype(jnp.bfloat16)
    ffn_gain = jnp.clip(1.0 + 0.18 * jax.random.normal(key_list[6], (D,), jnp.float32), 0.099609375, 1.8984375).astype(jnp.bfloat16)
    query_proj = scatter_about(key_list[7], (D, HEADS * QDIM), D ** -0.5, 0.125, ((0, 8), (1, 4)))
    latent_proj = scatter_about(key_list[8], (D, RANK + RDIM), D ** -0.5, 0.125, ((0, 8),))
    expand_proj = scatter_about(key_list[9], (RANK, HEADS * 2 * HDIM), RANK ** -0.5, 0.25, ((0, 8), (1, 4)))
    out_proj = scatter_about(key_list[10], (HEADS * HDIM, D), (max(1, 4 * D // SEQ_LEN)) ** -0.5, 3.0, ((0, 4), (1, 8)))
    shared_gate = scatter_about(key_list[11], (D, SHARED), D ** -0.5, 0.125, ((0, 8), (1, 4)))
    shared_up = scatter_about(key_list[12], (D, SHARED), D ** -0.5, 0.125, ((0, 8), (1, 4)))
    shared_down = scatter_about(key_list[13], (SHARED, D), SHARED ** -0.5, 0.109375, ((0, 4), (1, 8)))
    expert_gate = scatter_about(key_list[14], (2 * EXPERTS, D, FF // 2), D ** -0.5, 0.125, ((0, 32),))
    expert_up_weight = scatter_about(key_list[15], (2 * EXPERTS, D, FF // 2), D ** -0.5, 0.125, ((0, 32),))
    expert_down = scatter_about(key_list[16], (2 * EXPERTS, FF // 2, D), FF ** -0.5, 0.15625, ((0, 32),))
    return {"inputs": inputs, "cotangent": cotangent, "routes": routes, "gate_weights": gate_weights, "attn_gain": attn_gain, "latent_gain": latent_gain, "ffn_gain": ffn_gain, "query_proj": query_proj, "latent_proj": latent_proj, "expand_proj": expand_proj, "out_proj": out_proj, "shared_gate": shared_gate, "shared_up": shared_up, "shared_down": shared_down, "expert_gate": expert_gate, "expert_up_weight": expert_up_weight, "expert_down": expert_down}


EPSILON = 1e-06
ROPE_BASE = 10000.0
NEG_LARGE = -1e+30
PRECISE = lax.Precision.HIGHEST

@jax.custom_vjp
def low(v):
    return lax.optimization_barrier(v.astype(jnp.bfloat16)).astype(jnp.float32)

@jax.custom_vjp
def low_back(v):
    return v

def low_keep(v):
    return (low(v), None)

def low_pass(kept, grad):
    return (grad,)

def back_keep(v):
    return (v, None)

def back_low(kept, grad):
    return (low(grad),)
low.defvjp(low_keep, low_pass)
low_back.defvjp(back_keep, back_low)

def rms_norm(values, gain_vec):
    return values * lax.rsqrt(lax.optimization_barrier(jnp.mean(values * values, axis=-1, keepdims=True)) + EPSILON) * gain_vec

def silu_value(values):
    return values * jax.nn.sigmoid(values)

def rope_tables(positions, half_dim):
    frequency = ROPE_BASE ** (-jnp.arange(half_dim, dtype=jnp.float32) / half_dim)
    angles = positions.astype(jnp.float32)[:, None] * frequency[None, :]
    return (jnp.cos(angles), jnp.sin(angles))

def rope_turn(values, cosine_table, sine_table):
    half_dim = values.shape[-1] // 2
    first_half = values[..., :half_dim]
    second_half = values[..., half_dim:]
    return jnp.concatenate([first_half * cosine_table - second_half * sine_table, first_half * sine_table + second_half * cosine_table], axis=-1)

def attend_all(query_rows, key_rows, value_rows, score_scale):
    block_rows = min(512, SEQ_LEN)
    block_count = SEQ_LEN // block_rows
    key_block = jnp.arange(SEQ_LEN, dtype=jnp.int32) // BLOCK

    def one_block(flat_index):
        batch_index = flat_index // block_count
        first_row = flat_index % block_count * block_rows
        queries = lax.dynamic_slice_in_dim(query_rows[batch_index], first_row, block_rows, 0)
        scores = jnp.einsum('qhd,khd->hqk', queries, key_rows[batch_index], precision=PRECISE) * score_scale
        scores = low_back(scores)
        query_block = (first_row + jnp.arange(block_rows, dtype=jnp.int32)) // BLOCK
        allowed = key_block[None, :] <= query_block[:, None]
        scores = jnp.where(allowed[None, :, :], scores, NEG_LARGE)
        shifted = scores - lax.optimization_barrier(jnp.max(scores, axis=-1, keepdims=True))
        expo = jnp.exp(shifted)
        probs = expo / lax.optimization_barrier(jnp.sum(expo, axis=-1, keepdims=True))
        return jnp.einsum('hqk,khd->qhd', low(probs), value_rows[batch_index], precision=PRECISE)
    pieces = lax.map(jax.checkpoint(one_block), jnp.arange(BATCH * block_count, dtype=jnp.int32))
    return pieces.reshape(BATCH, SEQ_LEN, HEADS, HDIM)

def reference(inputs, cotangent, routes, gate_weights, attn_gain, latent_gain, ffn_gain, query_proj, latent_proj, expand_proj, out_proj, shared_gate, shared_up, shared_down, expert_gate, expert_up_weight, expert_down):
    token_total = BATCH * SEQ_LEN
    picked = routes.reshape(token_total, TOPK, 1) == jnp.arange(EXPERTS, dtype=jnp.int32).reshape(1, 1, EXPERTS)
    coefficients = lax.optimization_barrier(jnp.sum(jnp.where(picked, gate_weights.reshape(token_total, TOPK, 1), 0.0), axis=1))
    cosine_table, sine_table = rope_tables(jnp.arange(SEQ_LEN, dtype=jnp.int32), RDIM // 2)
    score_scale = QDIM ** (-0.5)

    def forward_pass(complete_input, attention_norm_gain, latent_norm_gain, feedforward_gain, query_matrix, latent_matrix, expansion_matrix, output_projection_matrix, shared_gate_matrix, shared_up_matrix, shared_down_matrix, expert_gate_stack, expert_up_stack, expert_down_stack):
        input_rows = complete_input.reshape(token_total, D)
        normed = low(rms_norm(input_rows, attention_norm_gain))
        query_lin = low_back(jnp.dot(normed, query_matrix, precision=PRECISE)).reshape(BATCH, SEQ_LEN, HEADS, QDIM)
        query_rows = low(jnp.concatenate([query_lin[..., :HDIM], rope_turn(query_lin[..., HDIM:], cosine_table[:, None, :], sine_table[:, None, :])], axis=-1))
        latent = low_back(low(jnp.dot(normed, latent_matrix, precision=PRECISE)))
        comp_normed = low(rms_norm(latent[:, :RANK], latent_norm_gain))
        rope_key = rope_turn(latent[:, RANK:].reshape(BATCH, SEQ_LEN, RDIM), cosine_table, sine_table)
        expanded = low_back(jnp.dot(comp_normed, expansion_matrix, precision=PRECISE)).reshape(BATCH, SEQ_LEN, HEADS, 2 * HDIM)
        key_rows = low(jnp.concatenate([expanded[..., :HDIM], jnp.broadcast_to(rope_key[:, :, None, :], (BATCH, SEQ_LEN, HEADS, RDIM))], axis=-1))
        value_rows = low(expanded[..., HDIM:])
        attended = attend_all(query_rows, key_rows, value_rows, score_scale)
        attended = low_back(low(attended)).reshape(token_total, HEADS * HDIM)
        attention = low_back(jnp.dot(attended, output_projection_matrix, precision=PRECISE))
        residual = input_rows + attention
        ffn_in = low(rms_norm(residual, feedforward_gain))
        shared_pre = low_back(jnp.dot(ffn_in, shared_gate_matrix, precision=PRECISE))
        shared_upp = low_back(jnp.dot(ffn_in, shared_up_matrix, precision=PRECISE))
        shared_act = low(silu_value(shared_pre) * shared_upp)
        shared_out = jnp.dot(shared_act, shared_down_matrix, precision=PRECISE)

        def expert_step(running, expert_slot_index):
            gate_mat = jnp.concatenate([expert_gate_stack[2 * expert_slot_index], expert_gate_stack[2 * expert_slot_index + 1]], axis=1)
            up_projection_matrix = jnp.concatenate([expert_up_stack[2 * expert_slot_index], expert_up_stack[2 * expert_slot_index + 1]], axis=1)
            down_mat = jnp.concatenate([expert_down_stack[2 * expert_slot_index], expert_down_stack[2 * expert_slot_index + 1]], axis=0)
            expert_pre = low_back(jnp.dot(ffn_in, gate_mat, precision=PRECISE))
            expert_up_product = low_back(jnp.dot(ffn_in, up_projection_matrix, precision=PRECISE))
            expert_act = low(silu_value(expert_pre) * expert_up_product)
            expert_out = low_back(jnp.dot(expert_act, down_mat, precision=PRECISE))
            column = lax.dynamic_slice_in_dim(coefficients, expert_slot_index, 1, 1)
            return (running + column * expert_out, None)
        routed, _ = lax.scan(jax.checkpoint(expert_step), jnp.zeros((token_total, D), jnp.float32), jnp.arange(EXPERTS, dtype=jnp.int32))
        return residual + shared_out + routed
    float_args = tuple((array_arg.astype(jnp.float32) for array_arg in (inputs, attn_gain, latent_gain, ffn_gain, query_proj, latent_proj, expand_proj, out_proj, shared_gate, shared_up, shared_down, expert_gate, expert_up_weight, expert_down)))
    result, pull_back = jax.vjp(forward_pass, *float_args)
    gradients = pull_back(cotangent.astype(jnp.float32).reshape(token_total, D))
    return (result.astype(jnp.bfloat16).reshape(BATCH, SEQ_LEN, D), gradients[0].astype(jnp.bfloat16), gradients[4], gradients[5], gradients[6], gradients[7], gradients[8], gradients[9], gradients[10], gradients[11], gradients[12], gradients[13], gradients[1], gradients[2], gradients[3])
```

```python
import functools

import jax
import jax.numpy as jnp
from jax import lax
from jax.experimental import pallas as pl
from jax.experimental.pallas import tpu as pltpu
from jax.sharding import PartitionSpec as P

HDIM = 128
RDIM = 64
RANK = 512
TOPK = 6
BLOCK = 256
QDIM = 192
HALF = RDIM // 2
EPSILON = 1e-06
ROPE_BASE = 10000.0
NEG_LARGE = -1e30
LOG2E = 1.4426950408889634
SCALE = QDIM ** (-0.5)
F32 = jnp.float32
BF16 = jnp.bfloat16
MIB = 1024 * 1024


def dot(a, b):
    return lax.dot_general(a, b, (((1,), (0,)), ((), ())), preferred_element_type=F32)


def dot_nt(a, b):
    return lax.dot_general(a, b, (((1,), (1,)), ((), ())), preferred_element_type=F32)


def dot_tn(a, b):
    return lax.dot_general(a, b, (((0,), (0,)), ((), ())), preferred_element_type=F32)


def rms_inverse(values):
    return lax.rsqrt(jnp.mean(values * values, axis=-1, keepdims=True) + EPSILON)


def rope_tables(positions):
    frequency = ROPE_BASE ** (-jnp.arange(HALF, dtype=F32) / HALF)
    angles = positions.astype(F32)[:, None] * frequency[None, :]
    return (jnp.cos(angles), jnp.sin(angles))


def norm_back(grad_normed, hat_rows, inverse, gain_vec):
    scaled = grad_normed * gain_vec
    gain_term = jnp.sum(grad_normed * hat_rows, axis=(0, 1))
    grad_rows = inverse * (scaled - hat_rows * jnp.mean(scaled * hat_rows, axis=-1, keepdims=True))
    return (grad_rows, gain_term)


def swap(value, axis, mask):
    size = lax.axis_size(axis)
    return lax.ppermute(value, axis, [(i, i ^ mask) for i in range(size)])


def after(value, *others):
    seen = sum(other[(0,) * other.ndim].astype(F32) for other in others)
    return jnp.where(seen == seen, value, jnp.zeros((), value.dtype))


def bits_of(size):
    return [1 << i for i in range(size.bit_length() - 1)]


def depth():
    return lax.axis_size("seq") // 2


def plane_order(flip):
    bits = bits_of(lax.axis_size("head"))
    order = [0]
    for bit in bits[::-1] if flip else bits:
        order = order + [i | bit for i in order]
    return order


def spread_line(value):
    held = [value[None]]
    for bit in bits_of(depth())[::-1]:
        last = held[-1]
        got = swap(last, "seq", 2 * bit)
        held.append(jnp.stack([last, got], axis=1).reshape((-1,) + value.shape))
    return held


def collect_line(value):
    for bit in bits_of(depth()):
        pairs = value.reshape((-1, 2) + value.shape[1:])
        value = pairs[:, 0].astype(F32) + swap(pairs[:, 1], "seq", 2 * bit).astype(F32)
        if value.shape[0] > 1:
            value = value.astype(BF16)
    return value[0]


def spread_plane(value, flip):
    bits = bits_of(lax.axis_size("head"))
    value = value[None]
    for bit in bits[::-1] if flip else bits:
        value = jnp.concatenate([value, swap(value, "head", bit)], axis=0)
    return value


def collect_plane(value, flip):
    bits = bits_of(lax.axis_size("head"))
    for bit in bits if flip else bits[::-1]:
        half = value.shape[0] // 2
        value = (
            value[:half].astype(F32) + swap(value[half:], "head", bit).astype(F32)
        ).astype(BF16)
    return value[0]


def spread_all(value, flip):
    own = spread_plane(value, flip)
    return (own, swap(own, "seq", 1))


def collect_all(own, other, flip):
    both = (own.astype(F32) + swap(other, "seq", 1).astype(F32)).astype(BF16)
    return collect_plane(both, flip)


def pick(value, index, axis=0):
    return lax.dynamic_index_in_dim(value, index, axis, keepdims=False)


def gather_seq(steps):
    return (steps[-1], swap(steps[-1], "seq", 1))


def scatter_seq(own, other):
    both = (own.astype(F32) + swap(other, "seq", 1).astype(F32)).astype(BF16)
    return collect_line(both)


def load_block(ref, line):
    block = ref[:, line]
    return block.reshape(block.shape[0] * block.shape[1], block.shape[2])


def parts_of(here, own, other, size):
    out = []
    for core, ref in enumerate((own, other)):
        for line in range(own.shape[0]):
            place = pl.multiple_of((here ^ (2 * line + core)) * size, size)
            out.append((ref, line, place))
    return out


def latent_kernel(
    s_ref, x_ref, cos, sin, own, other, keys_out, lat_out, gattn_out, gffn_out, wide_out
):
    here = s_ref[0]
    rows = RANK + RDIM
    size = own.shape[2]
    x = x_ref[...].astype(F32)
    inverse = rms_inverse(x)
    acc = jnp.zeros((x.shape[0], rows), F32)
    glat = jnp.zeros((RANK // size, size), F32)
    for ref, line, place in parts_of(here, own, other, size):
        gains = ref[line, rows:, :].astype(F32)
        block = x_ref[:, pl.ds(place, size)].astype(F32)
        normed = (block * inverse * gains[0:1]).astype(BF16)
        acc = acc + dot_nt(normed, ref[line, :rows, :])
        gattn_out[:, pl.ds(place, size)] = gains[0:1]
        gffn_out[:, pl.ds(place, size)] = gains[1:2]
        glat = glat + gains[2 : 2 + RANK // size]
        wide_out[:, pl.ds(place, size)] = ref[line, :rows, :]
    low = acc.astype(BF16)
    lat_out[...] = low
    low = low.astype(F32)
    comp = low[:, :RANK]
    glat = jnp.concatenate([glat[i : i + 1] for i in range(RANK // size)], axis=1)
    normed = comp * rms_inverse(comp) * glat
    first, second = low[:, RANK : RANK + HALF], low[:, RANK + HALF :]
    keys_out[...] = jnp.concatenate(
        [normed, first * cos[...] - second * sin[...], first * sin[...] + second * cos[...]],
        axis=1,
    ).astype(BF16)


def block_scores(query, keys, masks):
    scores = dot_nt(query, keys)
    if masks is not None:
        scores = jnp.where(masks, scores, NEG_LARGE)
    return scores


def fill_expand(here, own, other, wexp, rank_each):
    for ref, line, place in parts_of(here, own, other, rank_each):
        wexp[pl.ds(place, rank_each), :] = ref[line, :rank_each, :]


def attend_kernel(heads, masked, *refs):
    if masked:
        s_ref, qblk_ref, kblk_ref, *refs = refs
    else:
        s_ref, *refs = refs
    (
        x, gain, cos, sin, own, other, q_own, q_other, e_own, e_other, o_own, o_other,
        normed_out, q_out, att_out, lse_out, part_out, acc, mx, sm, wexp,
    ) = refs
    group = x.shape[0]
    lines = own.shape[1]
    nope = heads * HDIM
    wide = heads * HALF
    here = s_ref[0]
    fill_expand(here, e_own, e_other, wexp, RANK // (2 * lines))
    rows = x[...].astype(F32)
    normed_out[...] = (rows * rms_inverse(rows) * gain[...]).astype(BF16)
    qlin = jnp.zeros((group, heads * QDIM), F32)
    size = q_own.shape[1]
    for ref, line, place in parts_of(here, q_own, q_other, size):
        qlin = qlin + dot(normed_out[:, pl.ds(place, size)], ref[line])
    first = qlin[:, nope : nope + wide]
    second = qlin[:, nope + wide :]
    turned_a = first * cos[...] - second * sin[...]
    turned_b = first * sin[...] + second * cos[...]
    for h in range(heads):
        q_out[h] = jnp.concatenate(
            [
                qlin[:, h * HDIM : (h + 1) * HDIM],
                turned_a[:, h * HALF : (h + 1) * HALF],
                turned_b[:, h * HALF : (h + 1) * HALF],
            ],
            axis=1,
        ).astype(BF16)
    acc[...] = jnp.zeros_like(acc)
    mx[...] = jnp.full_like(mx, NEG_LARGE)
    sm[...] = jnp.zeros_like(sm)

    for core, ref in enumerate((own, other)):

        def step(line, carry, core=core, ref=ref):
            @pl.when((here ^ (2 * line + core)) <= here)
            def _():
                latent = load_block(ref, line)
                expanded = dot(latent[:, :RANK], wexp[...]).astype(BF16)
                rope_key = latent[:, RANK:]
                allowed = None
                if masked:
                    allowed = kblk_ref[pl.ds(2 * line + core, 1), :] <= qblk_ref[...]
                for h in range(heads):
                    keys = jnp.concatenate(
                        [expanded[:, 2 * h * HDIM : (2 * h + 1) * HDIM], rope_key], axis=1
                    )
                    vals = expanded[:, (2 * h + 1) * HDIM : (2 * h + 2) * HDIM]
                    scores = block_scores(q_out[h], keys, allowed)
                    old = mx[h][:, :1]
                    new = jnp.maximum(old, jnp.max(scores, axis=1, keepdims=True))
                    weights = jnp.exp2((scores - new) * (SCALE * LOG2E))
                    if masked:
                        weights = jnp.where(allowed, weights, 0.0)
                    rescale = jnp.exp2((old - new) * (SCALE * LOG2E))
                    sm[h] = sm[h] * rescale + jnp.sum(weights, axis=1, keepdims=True)
                    acc[h] = acc[h] * rescale + dot(weights.astype(BF16), vals)
                    mx[h] = jnp.broadcast_to(new, (group, HDIM))

            return carry

        lax.fori_loop(0, lines, step, 0)
    for h in range(heads):
        att_out[:, h * HDIM : (h + 1) * HDIM] = (acc[h] / sm[h]).astype(BF16)
        lse_out[h] = mx[h] * (SCALE * LOG2E) + jnp.log2(sm[h])
    size = o_own.shape[2]
    for ref, line, place in parts_of(here, o_own, o_other, size):
        part_out[:, pl.ds(place, size)] = dot(att_out[...], ref[line]).astype(BF16)


def attend_back_kernel(heads, masked, batches, *refs):
    s_ref, *refs = refs
    take = lambda count: [refs.pop(0) for _ in range(count)]
    marks = [take(2) if masked else None for _ in range(batches)]
    per_batch = [take(9) for _ in range(batches)]
    q_own, q_other, e_own, e_other, o_own, o_other = take(6)
    outs = [take(3) for _ in range(batches)]
    dq_own, dq_other, de_own, de_other, do_own, do_other = take(6)
    gq_acc, gqlin, gatt, wexp, dwexp, dwq, dwo = refs
    group = per_batch[0][0].shape[0]
    lines = q_own.shape[0]
    nope = heads * HDIM
    wide = heads * HALF
    here = s_ref[0]
    fill_expand(here, e_own, e_other, wexp, RANK // (2 * lines))
    dwexp[...] = jnp.zeros_like(dwexp)
    out_parts = parts_of(here, o_own, o_other, o_own.shape[2])
    query_parts = parts_of(here, q_own, q_other, q_own.shape[1])
    for b in range(batches):
        gres, normed, q_ref, att, lse, cos, sin, own, other = per_batch[b]
        gpart_out, own_out, other_out = outs[b]
        plane, each = own.shape[0], own.shape[2]
        total = jnp.zeros((group, heads * HDIM), F32)
        for i, (ref, line, place) in enumerate(out_parts):
            block = gres[:, pl.ds(place, ref.shape[2])]
            total = total + dot_nt(block, ref[line])
            term = dot_tn(att[...], block)
            dwo[i] = term if b == 0 else dwo[i] + term
        gatt[...] = total.astype(BF16)
        gq_acc[...] = jnp.zeros_like(gq_acc)
        deltas = [
            jnp.sum(
                gatt[:, h * HDIM : (h + 1) * HDIM].astype(F32)
                * att[:, h * HDIM : (h + 1) * HDIM].astype(F32),
                axis=1,
                keepdims=True,
            )
            for h in range(heads)
        ]
        for core, (ref, out) in enumerate(((own, own_out), (other, other_out))):

            def step(line, carry, core=core, ref=ref, out=out, b=b, q_ref=q_ref, lse=lse):
                live = (here ^ (2 * line + core)) <= here

                @pl.when(jnp.logical_not(live))
                def _():
                    out[:, line] = jnp.zeros((plane, each, RANK + RDIM), BF16)

                @pl.when(live)
                def _():
                    latent = load_block(ref, line)
                    expanded = dot(latent[:, :RANK], wexp[...]).astype(BF16)
                    rope_key = latent[:, RANK:]
                    allowed = None
                    if masked:
                        qblk_ref, kblk_ref = marks[b]
                        allowed = kblk_ref[pl.ds(2 * line + core, 1), :] <= qblk_ref[...]
                    grads = []
                    grad_rope = jnp.zeros((group, RDIM), F32)
                    for h in range(heads):
                        keys = jnp.concatenate(
                            [expanded[:, 2 * h * HDIM : (2 * h + 1) * HDIM], rope_key], axis=1
                        )
                        vals = expanded[:, (2 * h + 1) * HDIM : (2 * h + 2) * HDIM]
                        query = q_ref[h]
                        gout = gatt[:, h * HDIM : (h + 1) * HDIM]
                        scores = block_scores(query, keys, allowed)
                        probs = jnp.exp2(scores * (SCALE * LOG2E) - lse[h][:, :1])
                        if masked:
                            probs = jnp.where(allowed, probs, 0.0)
                        gprobs = dot_nt(gout, vals)
                        gscores = (probs * (gprobs - deltas[h])).astype(BF16)
                        gq_acc[h] = gq_acc[h] + dot(gscores, keys)
                        gkeys = dot_tn(gscores, query) * SCALE
                        gvals = dot_tn(probs.astype(BF16), gout)
                        grads.append(gkeys[:, :HDIM].astype(BF16))
                        grads.append(gvals.astype(BF16))
                        grad_rope = grad_rope + gkeys[:, HDIM:]
                    gexp = jnp.concatenate(grads, axis=1)
                    dwexp[...] = dwexp[...] + dot_tn(latent[:, :RANK], gexp)
                    gcomp = dot_nt(gexp, wexp[...])
                    packed = jnp.concatenate([gcomp, grad_rope], axis=1).astype(BF16)
                    out[:, line] = packed.reshape(plane, each, RANK + RDIM)

                return carry

            lax.fori_loop(0, lines, step, 0)
        firsts, seconds = [], []
        for h in range(heads):
            value = gq_acc[h] * SCALE
            gqlin[:, h * HDIM : (h + 1) * HDIM] = value[:, :HDIM].astype(BF16)
            firsts.append(value[:, HDIM : HDIM + HALF])
            seconds.append(value[:, HDIM + HALF :])
        first = jnp.concatenate(firsts, axis=1)
        second = jnp.concatenate(seconds, axis=1)
        gqlin[:, nope : nope + wide] = (first * cos[...] + second * sin[...]).astype(BF16)
        gqlin[:, nope + wide :] = (second * cos[...] - first * sin[...]).astype(BF16)
        for i, (ref, line, place) in enumerate(query_parts):
            size = ref.shape[1]
            gpart_out[:, pl.ds(place, size)] = dot_nt(gqlin[...], ref[line]).astype(BF16)
            term = dot_tn(normed[:, pl.ds(place, size)], gqlin[...])
            dwq[i] = term if b == 0 else dwq[i] + term
    for line in range(lines):
        dq_own[line] = dwq[line].astype(BF16)
        dq_other[line] = dwq[lines + line].astype(BF16)
        do_own[line] = dwo[line].astype(BF16)
        do_other[line] = dwo[lines + line].astype(BF16)
    each = RANK // (2 * lines)
    for core, out in enumerate((de_own, de_other)):
        for line in range(lines):
            place = pl.multiple_of((here ^ (2 * line + core)) * each, each)
            out[line] = dwexp[pl.ds(place, each), :].astype(BF16)


def vmem_specs(count):
    return [pl.BlockSpec(memory_space=pltpu.VMEM)] * count


def smem_spec():
    return [pl.BlockSpec(memory_space=pltpu.SMEM)]


def own_latents(here, x, cos, sin, parts):
    rows, width = x.shape
    return pl.pallas_call(
        latent_kernel,
        out_shape=(
            jax.ShapeDtypeStruct((rows, RANK + RDIM), BF16),
            jax.ShapeDtypeStruct((rows, RANK + RDIM), BF16),
            jax.ShapeDtypeStruct((1, width), F32),
            jax.ShapeDtypeStruct((1, width), F32),
            jax.ShapeDtypeStruct((RANK + RDIM, width), BF16),
        ),
        in_specs=smem_spec() + vmem_specs(5),
        out_specs=tuple(vmem_specs(5)),
        compiler_params=pltpu.CompilerParams(vmem_limit_bytes=40 * MIB),
        cost_estimate=pl.CostEstimate(
            flops=1_000_000_000, bytes_accessed=6_000_000, transcendentals=1_000
        ),
        name="own_latents",
    )(here, x, cos, sin, *parts)


def attend(here, marks, x, gain, cos, sin, keys, weights, heads):
    group, width = x.shape
    return pl.pallas_call(
        functools.partial(attend_kernel, heads, bool(marks)),
        out_shape=(
            jax.ShapeDtypeStruct((group, width), BF16),
            jax.ShapeDtypeStruct((heads, group, QDIM), BF16),
            jax.ShapeDtypeStruct((group, heads * HDIM), BF16),
            jax.ShapeDtypeStruct((heads, group, HDIM), F32),
            jax.ShapeDtypeStruct((group, width), BF16),
        ),
        in_specs=smem_spec() + vmem_specs(len(marks) + 12),
        out_specs=tuple(vmem_specs(5)),
        scratch_shapes=[pltpu.VMEM((heads, group, HDIM), F32)] * 3
        + [pltpu.VMEM((RANK, 2 * heads * HDIM), BF16)],
        compiler_params=pltpu.CompilerParams(vmem_limit_bytes=56 * MIB),
        cost_estimate=pl.CostEstimate(
            flops=8_000_000_000, bytes_accessed=12_000_000, transcendentals=4_000_000
        ),
        name="attend",
    )(here, *marks, x, gain, cos, sin, *keys, *weights)


def attend_back(here, marks, per_batch, weights):
    batches = len(per_batch)
    heads, group = per_batch[0][2].shape[:2]
    width = per_batch[0][0].shape[1]
    q_own, _, e_own, _, o_own, _ = weights
    lines = q_own.shape[0]
    rank_each = RANK // (2 * lines)
    outs = []
    for args in per_batch:
        outs.append(jax.ShapeDtypeStruct((group, width), BF16))
        outs += [jax.ShapeDtypeStruct(args[7].shape, BF16)] * 2
    outs += [jax.ShapeDtypeStruct(q_own.shape, BF16)] * 2
    outs += [jax.ShapeDtypeStruct((lines, rank_each, e_own.shape[2]), BF16)] * 2
    outs += [jax.ShapeDtypeStruct(o_own.shape, BF16)] * 2
    inputs = [m for mark in marks for m in mark] + [v for args in per_batch for v in args]
    inputs += list(weights)
    return pl.pallas_call(
        functools.partial(attend_back_kernel, heads, bool(marks[0]), batches),
        out_shape=tuple(outs),
        in_specs=smem_spec() + vmem_specs(len(inputs)),
        out_specs=tuple(vmem_specs(len(outs))),
        scratch_shapes=[
            pltpu.VMEM((heads, group, QDIM), F32),
            pltpu.VMEM((group, heads * QDIM), BF16),
            pltpu.VMEM((group, heads * HDIM), BF16),
            pltpu.VMEM((RANK, 2 * heads * HDIM), BF16),
            pltpu.VMEM((RANK, 2 * heads * HDIM), F32),
            pltpu.VMEM((2 * lines,) + q_own.shape[1:], F32),
            pltpu.VMEM((2 * lines,) + o_own.shape[1:], F32),
        ],
        compiler_params=pltpu.CompilerParams(vmem_limit_bytes=62 * MIB),
        cost_estimate=pl.CostEstimate(
            flops=24_000_000_000, bytes_accessed=30_000_000, transcendentals=8_000_000
        ),
        name="attend_back",
    )(here, *inputs)


def feed_kernel(batch, order, aliased, *refs):
    slot, gate, xa, xb, c, wg, wu, wd, sgu, sgut, sd = refs[:11]
    refs = refs[11 + aliased :]
    o, ga, gb, rows_out, grows_out, act_out, gpre_out, gup_out, dsgut, dsd = refs
    plane, per, half, width = xa.shape
    group = 2 * plane * half
    cap = rows_out.shape[2]
    pad = sd.shape[0]

    @pl.when(pl.program_id(0) == 0)
    def _():
        dsgut[...] = jnp.zeros_like(dsgut)
        dsd[...] = jnp.zeros_like(dsd)

    xs, cs, picks, gates = [], [], [], []
    for i in range(per):
        xs += [xa[:, i].reshape(group // 2, width), xb[:, i].reshape(group // 2, width)]
        for side in range(2):
            for j in range(plane):
                place = order[j] if (side != batch) else j
                cs.append(c[place, i, side * half : (side + 1) * half])
        chosen = lax.broadcasted_iota(jnp.int32, (cap, group), 0) == slot[i]
        gates.append(jnp.sum(jnp.where(chosen, gate[i], 0.0), axis=1, keepdims=True))
        picks.append(chosen.astype(F32))
    x = jnp.concatenate(xs, axis=0)
    cot = jnp.concatenate(cs, axis=0)
    gates = jnp.concatenate(gates, axis=0)
    rows = jnp.concatenate(
        [
            dot(picks[i].astype(BF16), x[i * group : (i + 1) * group]).astype(BF16)
            for i in range(per)
        ],
        axis=0,
    )
    grows = jnp.concatenate(
        [dot(picks[i].astype(BF16), cot[i * group : (i + 1) * group]) for i in range(per)],
        axis=0,
    )
    grows = (grows * gates).astype(BF16)
    pre = dot_nt(rows, wg[...])
    upp = dot_nt(rows, wu[...])
    sig = 1.0 / (1.0 + jnp.exp(-pre))
    silu = pre * sig
    act = (silu * upp).astype(BF16)
    geact = dot_nt(grows, wd[...])
    gpre = (geact * upp * (sig * (1.0 + pre * (1.0 - sig)))).astype(BF16)
    gup = (geact * silu).astype(BF16)
    for i in range(per):
        part = slice(i * cap, (i + 1) * cap)
        rows_out[0, i] = rows[part]
        grows_out[0, i] = grows[part]
        act_out[0, i] = act[part]
        gpre_out[0, i] = gpre[part]
        gup_out[0, i] = gup[part]
    made = (dot(act, wd[...]) * gates).astype(BF16)
    gmade = (dot(gpre, wg[...]) + dot(gup, wu[...])).astype(BF16)
    both = dot(x, sgu[...])
    spre, supp = both[:, :pad], both[:, pad:]
    ssig = 1.0 / (1.0 + jnp.exp(-spre))
    ssilu = spre * ssig
    sact = (ssilu * supp).astype(BF16)
    gsact = dot_nt(cot, sd[...])
    gspre = (gsact * supp * (ssig * (1.0 + spre * (1.0 - ssig)))).astype(BF16)
    gsupp = (gsact * ssilu).astype(BF16)
    gsboth = jnp.concatenate([gspre, gsupp], axis=1)
    dsgut[...] = dsgut[...] + dot_tn(gsboth, x)
    dsd[...] = dsd[...] + dot_tn(sact, cot)
    for i in range(per):
        back = picks[i].T.astype(BF16)
        toks = slice(i * group, (i + 1) * group)
        part = slice(i * cap, (i + 1) * cap)
        out = dot(
            jnp.concatenate([back, sact[toks]], axis=1),
            jnp.concatenate([made[part], sd[...]], axis=0),
        ).astype(BF16)
        for side in range(2):
            for j in range(plane):
                place = order[j] if (side != batch) else j
                at = (side * plane + j) * half
                o[place, i, side * half : (side + 1) * half] = out[at : at + half]
        gx = dot(
            jnp.concatenate([back, gsboth[toks]], axis=1),
            jnp.concatenate([gmade[part], sgut[...]], axis=0),
        ).astype(BF16)
        ga[:, i] = gx[: group // 2].reshape(plane, half, width)
        gb[:, i] = gx[group // 2 :].reshape(plane, half, width)


def feed(batch, core, batches, cap, slot, gate, xa, xb, cot, weights, earlier):
    plane, lines, half, width = xa.shape
    group = 2 * plane * half
    per = 2 if group <= 256 and lines % 2 == 0 else 1
    steps = lines // per
    hidden = weights[0].shape[0]
    pad = weights[-1].shape[0]

    def block(size):
        return pl.BlockSpec((plane, per, size, width), lambda i: (0, i, 0, 0))

    def fixed(shape):
        return pl.BlockSpec(shape, lambda i: (0,) * len(shape), pipeline_mode=pl.Buffered(1))

    def saved(size):
        return pl.BlockSpec((1, per, cap, size), lambda i: (batch, core * steps + i, 0, 0))

    mark = pl.BlockSpec((per, 1, group), lambda i: (i, 0, 0))
    full = jax.ShapeDtypeStruct(xa.shape, BF16)
    keep = [width, width, hidden, hidden, hidden]
    kept_shapes = [jax.ShapeDtypeStruct((batches, 2 * lines, cap, size), BF16) for size in keep]
    aliased = len(earlier)
    return pl.pallas_call(
        functools.partial(feed_kernel, batch, plane_order(True), aliased),
        grid=(steps,),
        out_shape=tuple(
            [jax.ShapeDtypeStruct(cot.shape, BF16), full, full]
            + kept_shapes
            + [
                jax.ShapeDtypeStruct((2 * pad, width), F32),
                jax.ShapeDtypeStruct((pad, width), F32),
            ]
        ),
        in_specs=[mark, mark, block(half), block(half), block(2 * half)]
        + [fixed(w.shape) for w in weights]
        + [pl.BlockSpec(memory_space=pl.ANY)] * aliased,
        out_specs=tuple(
            [block(2 * half), block(half), block(half)]
            + [saved(size) for size in keep]
            + [fixed((2 * pad, width)), fixed((pad, width))]
        ),
        input_output_aliases={11 + i: 3 + i for i in range(aliased)},
        compiler_params=pltpu.CompilerParams(vmem_limit_bytes=62 * MIB),
        cost_estimate=pl.CostEstimate(
            flops=16_000_000_000, bytes_accessed=30_000_000, transcendentals=1_000_000
        ),
        name="feed",
    )(slot, gate, xa, xb, cot, *weights, *earlier)


def local(
    inputs,
    cotangent,
    routes,
    gate_weights,
    attn_gain,
    latent_gain,
    ffn_gain,
    query_proj,
    latent_proj,
    expand_proj,
    out_proj,
    shared_gate,
    shared_up,
    shared_down,
    expert_gate,
    expert_up_weight,
    expert_down,
):
    seq_count = lax.axis_size("seq")
    head_count = lax.axis_size("head")
    seq_index = lax.axis_index("seq")
    head_index = lax.axis_index("head")
    lines = depth()
    line, core = seq_index // 2, seq_index % 2
    batches, each, width = inputs.shape
    group = each * head_count
    heads = out_proj.shape[0] // HDIM
    half = each // 2
    orders = [plane_order(False), plane_order(True)]
    serial = group > BLOCK

    here = seq_index.reshape(1)
    positions = seq_index * group + jnp.arange(group, dtype=jnp.int32)

    shard = latent_proj.shape[0]
    n_lat = latent_gain.shape[0]
    lat_gain = lax.dynamic_update_slice_in_dim(
        jnp.zeros((RANK,), BF16), latent_gain, seq_index * n_lat, 0
    )
    gain_rows = 16
    gain_part = jnp.concatenate(
        [attn_gain[None], ffn_gain[None], lat_gain.reshape(RANK // shard, shard)], axis=0
    )
    gain_part = jnp.pad(gain_part, ((0, gain_rows - gain_part.shape[0]), (0, 0)))
    lat_mine = jnp.concatenate([jnp.transpose(latent_proj), gain_part], axis=0)
    with jax.named_scope("latent_weights"):
        lat_steps = spread_line(lat_mine)
        lat_parts = gather_seq(lat_steps)
    with jax.named_scope("inputs"):
        group_rows = [
            spread_plane(inputs[b], bool(b)).reshape(group, width) for b in range(batches)
        ]

    pair = head_count // 2
    expert_ids = jnp.arange(seq_count, dtype=jnp.int32) * pair + head_index // 2
    hits = routes[None] == expert_ids[:, None, None, None]
    gate_of = jnp.sum(jnp.where(hits, gate_weights[None], 0.0), axis=-1)
    named = jnp.any(hits, axis=-1)

    def block_order(value):
        value = value.reshape(value.shape[:-1] + (head_count, 2, half))
        sides = []
        for side in range(2):
            ids = jnp.array(orders[side], jnp.int32) ^ head_index
            sides.append(jnp.take(value[..., side, :], ids, axis=-2))
        value = jnp.stack(sides, axis=-3)
        return value.reshape(value.shape[:-3] + (group,))

    gate_of, named = block_order(gate_of), block_order(named)
    ahead = jnp.arange(group)[:, None] < jnp.arange(group)[None, :]
    rank = lax.dot_general(
        named.astype(BF16), ahead.astype(BF16), (((2,), (0,)), ((), ())), preferred_element_type=F32
    )
    gate_high = gate_of.astype(BF16)
    mark_mine = jnp.stack(
        [
            jnp.where(named, jnp.minimum(rank, 255.0), -1.0).astype(BF16),
            gate_high,
            (gate_of - gate_high.astype(F32)).astype(BF16),
        ],
        axis=1,
    )
    expand_rows, expand_cols = expand_proj.shape
    mark_rows = -(-mark_mine.size // expand_cols)
    mark_pad = -(-mark_rows // 16) * 16
    mark_mine = jnp.pad(
        mark_mine.reshape(-1), (0, mark_pad * expand_cols - mark_mine.size)
    ).reshape(mark_pad, expand_cols)
    with jax.named_scope("expand_weights"):
        expand_mine = after(jnp.concatenate([expand_proj, mark_mine], axis=0), lat_steps[1])
        expand_steps = spread_line(expand_mine)
        expand_parts = gather_seq(expand_steps)
    mark_size = seq_count * 3 * batches * group

    def marks_from(parts):
        flat = parts[:, expand_rows:].reshape(lines, -1)[:, :mark_size]
        return pick(flat.reshape(lines, seq_count, 3, batches, 1, group), seq_index, 1).astype(F32)

    marks_mine = [marks_from(parts) for parts in expand_parts]
    slots = [m[:, 0].astype(jnp.int32) for m in marks_mine]
    gates = [m[:, 1] + m[:, 2] for m in marks_mine]

    cos_all, sin_all = rope_tables(positions)
    own_cos, own_sin = [
        lax.dynamic_slice_in_dim(t, head_index * each, each, 0) for t in (cos_all, sin_all)
    ]
    own_keys, own_latent, gain_attn, gain_ffn, latent_t = own_latents(
        here,
        inputs.reshape(batches * each, width),
        jnp.tile(own_cos, (batches, 1)),
        jnp.tile(own_sin, (batches, 1)),
        lat_parts,
    )
    own_keys = own_keys.reshape(batches, each, RANK + RDIM)
    with jax.named_scope("keys"):
        key_steps = spread_line(own_keys)
        keys = [spread_all(key_steps[-1][:, b], bool(b)) for b in range(batches)]

    cols = query_proj.reshape(query_proj.shape[0], heads, QDIM)
    query_mine = jnp.concatenate(
        [
            cols[..., :HDIM].reshape(-1, heads * HDIM),
            cols[..., HDIM : HDIM + HALF].reshape(-1, heads * HALF),
            cols[..., HDIM + HALF :].reshape(-1, heads * HALF),
        ],
        axis=1,
    )
    with jax.named_scope("query_weights"):
        query_mine = after(query_mine, expand_steps[1])
        query_steps = spread_line(query_mine)
        query_parts = gather_seq(query_steps)
    with jax.named_scope("output_weights"):
        out_mine = after(out_proj, query_steps[1], key_steps[1])
        out_steps = spread_line(out_mine)
        out_parts = gather_seq(out_steps)
    attn_weights = (*query_parts, *expand_parts, *out_parts)

    hidden_each = shared_gate.shape[1] // seq_count
    hidden_pad = -(-hidden_each // 128) * 128
    dshard = shared_gate.shape[0]
    shared_mine = jnp.stack(
        [
            jnp.transpose(shared_gate).reshape(seq_count, hidden_each, dshard),
            jnp.transpose(shared_up).reshape(seq_count, hidden_each, dshard),
            shared_down.reshape(seq_count, hidden_each, dshard),
        ],
        axis=1,
    ).reshape(lines, 2, 3, hidden_each, dshard)
    with jax.named_scope("shared_weights"):
        kept = pick(shared_mine, core, 1)
        came = swap(pick(shared_mine, core ^ 1, 1), "seq", 1)
        paired = jnp.where(core == 0, jnp.stack([kept, came], 1), jnp.stack([came, kept], 1))
        paired = after(paired, out_steps[1])
        shared_pieces = [pick(paired, line)]
        shared_pieces += [swap(pick(paired, line ^ k), "seq", 2 * k) for k in range(1, lines)]
    shared_t = jnp.zeros((lines, 2, 3, hidden_each, dshard), BF16)
    for k in range(lines):
        shared_t = lax.dynamic_update_slice_in_dim(
            shared_t, shared_pieces[k][None], line ^ k, 0
        )
    shared_t = jnp.transpose(shared_t, (2, 3, 0, 1, 4)).reshape(3, hidden_each, width)
    shared_t = jnp.pad(shared_t, ((0, 0), (0, hidden_pad - hidden_each), (0, 0)))
    sgut = shared_t[:2].reshape(2 * hidden_pad, width)
    weights = (
        jnp.transpose(expert_gate[0]),
        jnp.transpose(expert_up_weight[0]),
        expert_down[0],
        jnp.transpose(sgut),
        sgut,
        shared_t[2],
    )

    with jax.named_scope("cotangents"):
        cot_steps = spread_line(after(cotangent, out_steps[1]))
        cot_line = after(cot_steps[-1], keys[0][0], keys[1][0])

    own_rows = inputs.astype(F32)
    own_inverse = rms_inverse(own_rows)
    own_hat = own_rows * own_inverse
    normed, queries, attended, lses, tables, marks = [], [], [], [], [], []
    residual, ffn_hat, ffn_inverse, ffn_rows = [], [], [], []
    for b in range(batches):
        away = jnp.array(orders[b], jnp.int32) ^ head_index
        place = (away[:, None] * each + jnp.arange(each, dtype=jnp.int32)[None, :]).reshape(group)
        cos_b, sin_b = [
            jnp.tile(
                jnp.take(t.reshape(head_count, each, HALF), away, axis=0).reshape(group, HALF),
                (1, heads),
            )
            for t in (cos_all, sin_all)
        ]
        tables.append((cos_b, sin_b))
        marks_b = ()
        if group > BLOCK:
            own_block = (seq_index * group + place) // BLOCK
            offsets = jnp.arange(seq_count, dtype=jnp.int32) ^ seq_index
            key_block = (offsets[:, None] * group + place[None, :]) // BLOCK
            marks_b = (jnp.broadcast_to(own_block[:, None], (group, group)), key_block)
        marks.append(marks_b)
        normed_b, q_b, att_b, lse_b, part = attend(
            here, marks_b, group_rows[b], gain_attn, cos_b, sin_b, keys[b], attn_weights, heads
        )
        normed.append(normed_b)
        queries.append(q_b)
        attended.append(att_b)
        lses.append(lse_b)
        part = part.reshape(head_count, each, width)
        total = part[0].astype(F32)
        with jax.named_scope("attention_sum"):
            for j in range(1, head_count):
                total = total + swap(part[j], "head", orders[b][j]).astype(F32)
        residual_b = own_rows[b] + total
        inverse_b = rms_inverse(residual_b)
        hat_b = residual_b * inverse_b
        ffn_b = (hat_b * gain_ffn).astype(BF16)
        residual.append(residual_b)
        ffn_inverse.append(inverse_b)
        ffn_hat.append(hat_b)
        ffn_rows.append(ffn_b)

    most_rows = 4 * group * TOPK // (3 * seq_count * pair)
    kept_rows, outs, grad_ffn, dsgut, dsd = (), [], [], 0.0, 0.0
    spread_ffn, cots = [], []
    for b in range(batches):
        with jax.named_scope("ffn_rows"):
            if serial and b:
                ffn_rows[b] = after(ffn_rows[b], grad_ffn[b - 1], outs[b - 1])
                cot_line = after(cot_line, grad_ffn[b - 1], outs[b - 1])
            rows_b = spread_line(ffn_rows[b])[-1]
            spread_ffn.append(
                (spread_all(rows_b[:, :half], False), spread_all(rows_b[:, half:], True))
            )
        with jax.named_scope("cotangents"):
            cots.append(spread_all(cot_line[:, b], bool(b)))
        made = [None, None]
        for side in (1, 0):
            res = feed(
                b, side, batches, most_rows, slots[side][:, b], gates[side][:, b],
                spread_ffn[b][0][side], spread_ffn[b][1][side], cots[b][side], weights, kept_rows,
            )
            made[side] = res[:3]
            kept_rows = tuple(res[3:8])
            dsgut = dsgut + res[8]
            dsd = dsd + res[9]
        with jax.named_scope("ffn_grads"):
            first = collect_all(made[0][1], made[1][1], False)
            second = collect_all(made[0][2], made[1][2], True)
            grad_ffn.append(collect_line(jnp.concatenate([first, second], axis=1)))
        with jax.named_scope("outputs"):
            outs.append(collect_all(made[0][0], made[1][0], bool(b)))

    ffn_hat, ffn_inverse = jnp.stack(ffn_hat), jnp.stack(ffn_inverse)
    grad_two, ffngain_term = norm_back(jnp.stack(grad_ffn), ffn_hat, ffn_inverse, gain_ffn)
    grad_residual = cotangent.astype(F32) + grad_two
    grad_attention = grad_residual.astype(BF16)
    with jax.named_scope("attention_grads"):
        gatt_rows = [
            spread_plane(grad_attention[b], bool(b)).reshape(group, width)
            for b in range(batches)
        ]
    per_batch = [
        (gatt_rows[b], normed[b], queries[b], attended[b], lses[b], *tables[b], *keys[b])
        for b in range(batches)
    ]
    if serial:
        calls = [
            attend_back(here, marks[b : b + 1], per_batch[b : b + 1], attn_weights)
            for b in range(batches)
        ]
        sums = [sum(v.astype(F32) for v in t).astype(BF16) for t in zip(*[c[3:] for c in calls])]
        res = [v for c in calls for v in c[:3]] + sums
    else:
        res = attend_back(here, marks, per_batch, attn_weights)
    gparts = [res[3 * b] for b in range(batches)]
    gkeys = [res[3 * b + 1 : 3 * b + 3] for b in range(batches)]
    dq_own, dq_other, de_own, de_other, do_own, do_other = res[3 * batches :]
    with jax.named_scope("key_grads"):
        grad_key = [collect_all(*gkeys[b], bool(b)) for b in range(batches)]
        grad_key = collect_line(jnp.stack(grad_key, axis=1))
    latent_rows = own_latent.astype(F32).reshape(batches, each, RANK + RDIM)
    compressed = latent_rows[..., :RANK]
    comp_inverse = rms_inverse(compressed)
    comp_hat = compressed * comp_inverse
    lat_gains = sum(
        part[:, RANK + RDIM + 2 : RANK + RDIM + 2 + RANK // shard].astype(F32).sum(axis=0)
        for part in lat_parts
    ).reshape(RANK)
    grad_comp = grad_key[..., :RANK]
    grad_a, grad_b = grad_key[..., RANK : RANK + HALF], grad_key[..., RANK + HALF :]
    grad_rope = jnp.concatenate(
        [grad_a * own_cos + grad_b * own_sin, grad_b * own_cos - grad_a * own_sin], axis=-1
    )
    grad_compressed, latgain_term = norm_back(grad_comp, comp_hat, comp_inverse, lat_gains)
    grad_latent = jnp.concatenate([grad_compressed, grad_rope], axis=-1).astype(BF16)

    grad_normed = []
    for b in range(batches):
        part = gparts[b].reshape(head_count, each, width)
        total = part[0].astype(F32)
        with jax.named_scope("normed_grads"):
            for j in range(1, head_count):
                total = total + swap(part[j], "head", orders[b][j]).astype(F32)
        grad_normed.append(total)
    grad_normed = jnp.stack(grad_normed) + dot(
        grad_latent.reshape(batches * each, RANK + RDIM), latent_t
    ).reshape(batches, each, width)
    grad_input, attngain_term = norm_back(grad_normed, own_hat, own_inverse, gain_attn)
    inputs_grad = (grad_input + grad_residual).astype(BF16)

    with jax.named_scope("query_grads"):
        query_grad = scatter_seq(dq_own, dq_other)
    nope = heads * HDIM
    query_grad = jnp.concatenate(
        [
            query_grad[:, :nope].reshape(-1, heads, HDIM),
            query_grad[:, nope : nope + heads * HALF].reshape(-1, heads, HALF),
            query_grad[:, nope + heads * HALF :].reshape(-1, heads, HALF),
        ],
        axis=-1,
    ).reshape(-1, heads * QDIM)
    with jax.named_scope("expand_grads"):
        expand_grad = scatter_seq(de_own, de_other)
    with jax.named_scope("output_grads"):
        outproj_grad = scatter_seq(do_own, do_other)
    share = (RANK + RDIM) // head_count
    with jax.named_scope("latent_grads"):
        latent_rows = [
            spread_plane(grad_latent[b], bool(b)).reshape(group, -1) for b in range(batches)
        ]
    latent_term = 0.0
    for b in range(batches):
        mine = lax.dynamic_slice_in_dim(latent_rows[b], head_index * share, share, 1)
        latent_term = latent_term + dot_tn(mine, normed[b])
    latent_term = latent_term.astype(BF16)
    gain_term = jnp.concatenate(
        [
            attngain_term.reshape(seq_count, 1, shard),
            ffngain_term.reshape(seq_count, 1, shard),
            jnp.pad(
                latgain_term.reshape(seq_count, 1, n_lat), ((0, 0), (0, 0), (0, shard - n_lat))
            ),
            jnp.zeros((seq_count, gain_rows - 3, shard), F32),
        ],
        axis=1,
    ).astype(BF16)
    latent_term = jnp.concatenate(
        [
            jnp.stack([latent_term[:, i * shard : (i + 1) * shard] for i in range(seq_count)]),
            gain_term,
        ],
        axis=1,
    )
    latent_own, latent_other = [
        jnp.stack([pick(latent_term, seq_index ^ (2 * k + c)) for k in range(lines)])
        for c in range(2)
    ]
    with jax.named_scope("latent_grads"):
        latent_mine = scatter_seq(latent_own, latent_other).astype(BF16)
        latent_parts = [latent_mine]
        latent_parts += [swap(latent_mine, "head", k) for k in range(1, head_count)]
    latent_grad = jnp.zeros((head_count, share, shard), BF16)
    gain_grad = 0.0
    for k in range(head_count):
        latent_grad = lax.dynamic_update_slice_in_dim(
            latent_grad, latent_parts[k][None, :share], head_index ^ k, 0
        )
        gain_grad = gain_grad + latent_parts[k][share:].astype(F32)
    latent_grad = jnp.transpose(latent_grad.reshape(RANK + RDIM, shard)).astype(F32)
    attngain_grad = gain_grad[0]
    ffngain_grad = gain_grad[1]
    latgain_grad = gain_grad[2, :n_lat]

    shared_term = jnp.concatenate(
        [dsgut.reshape(2, hidden_pad, width), dsd[None]], axis=0
    )[:, :hidden_each].astype(BF16)
    shared_term = jnp.transpose(
        shared_term.reshape(3, hidden_each, lines, 2, dshard), (2, 3, 0, 1, 4)
    )
    with jax.named_scope("shared_grads"):
        held = [pick(shared_term, line)]
        held += [swap(pick(shared_term, line ^ k), "seq", 2 * k) for k in range(1, lines)]
        held = jnp.stack(held)
        kept = pick(held, core, 1)
        came = swap(pick(held, core ^ 1, 1), "seq", 1)
    paired = jnp.where(core == 0, jnp.stack([kept, came], 1), jnp.stack([came, kept], 1))
    shared_grad = jnp.zeros(paired.shape, BF16)
    for k in range(lines):
        shared_grad = lax.dynamic_update_slice_in_dim(shared_grad, paired[k : k + 1], line ^ k, 0)
    shared_grad = jnp.transpose(shared_grad, (2, 0, 1, 3, 4)).reshape(3, -1, dshard).astype(F32)
    shgate_grad = jnp.transpose(shared_grad[0])
    shup_grad = jnp.transpose(shared_grad[1])
    shdown_grad = shared_grad[2]

    rows, grows, act, gpre, gup = [v.reshape(-1, v.shape[-1]) for v in kept_rows]
    exgate_grad = jnp.transpose(dot_tn(gpre, rows))[None]
    exup_grad = jnp.transpose(dot_tn(gup, rows))[None]
    exdown_grad = dot_tn(act, grows)[None]

    with jax.named_scope("outputs"):
        ffn_own = collect_line(jnp.stack(outs, axis=1))
    output = (jnp.stack(residual) + ffn_own).astype(BF16)

    return (
        output,
        inputs_grad,
        query_grad,
        latent_grad,
        expand_grad,
        outproj_grad,
        shgate_grad,
        shup_grad,
        shdown_grad,
        exgate_grad,
        exup_grad,
        exdown_grad,
        attngain_grad,
        latgain_grad,
        ffngain_grad,
    )


def solution(mesh):
    own = P(None, ("seq", "head"), None)
    stack = P(("seq", "head"), None, None)
    return jax.shard_map(
        local,
        mesh=mesh,
        in_specs=(
            own,
            own,
            P(None, "seq", None),
            P(None, "seq", None),
            P("seq"),
            P("seq"),
            P("seq"),
            P("seq", "head"),
            P("seq", None),
            P("seq", "head"),
            P("head", "seq"),
            P("seq", "head"),
            P("seq", "head"),
            P("head", "seq"),
            stack,
            stack,
            stack,
        ),
        out_specs=(
            own,
            own,
            P("seq", "head"),
            P("seq", None),
            P("seq", "head"),
            P("head", "seq"),
            P("seq", "head"),
            P("seq", "head"),
            P("head", "seq"),
            stack,
            stack,
            stack,
            P("seq"),
            P("seq"),
            P("seq"),
        ),
        check_vma=False,
    )
```

```python
import functools

import jax
import jax.numpy as jnp
from jax import lax
from jax.experimental import pallas as pl
from jax.experimental.pallas import tpu as pltpu
from jax.sharding import PartitionSpec as P

HDIM = 128
RDIM = 64
RANK = 512
TOPK = 6
BLOCK = 256
QDIM = 192
HALF = RDIM // 2
EPSILON = 1e-06
ROPE_BASE = 10000.0
NEG_LARGE = -1e30
LOG2E = 1.4426950408889634
SCALE = QDIM ** (-0.5)
WIDE = -(-(RANK + RDIM) // 128) * 128
F32 = jnp.float32
BF16 = jnp.bfloat16
MIB = 1024 * 1024


def dot(a, b):
    return lax.dot_general(a, b, (((1,), (0,)), ((), ())), preferred_element_type=F32)


def dot_nt(a, b):
    return lax.dot_general(a, b, (((1,), (1,)), ((), ())), preferred_element_type=F32)


def dot_tn(a, b):
    return lax.dot_general(a, b, (((0,), (0,)), ((), ())), preferred_element_type=F32)


def rms_inverse(values):
    return lax.rsqrt(jnp.mean(values * values, axis=-1, keepdims=True) + EPSILON)


def rope_tables(positions):
    frequency = ROPE_BASE ** (-jnp.arange(HALF, dtype=F32) / HALF)
    angles = positions.astype(F32)[:, None] * frequency[None, :]
    return (jnp.cos(angles), jnp.sin(angles))


def norm_back(grad_normed, hat_rows, inverse, gain_vec):
    scaled = grad_normed * gain_vec
    gain_term = jnp.sum(grad_normed * hat_rows, axis=(0, 1))
    grad_rows = inverse * (scaled - hat_rows * jnp.mean(scaled * hat_rows, axis=-1, keepdims=True))
    return (grad_rows, gain_term)


def swap(value, axis, mask):
    size = lax.axis_size(axis)
    return lax.ppermute(value, axis, [(i, i ^ mask) for i in range(size)])


def depth():
    return lax.axis_size("seq") // 2


def line_pieces(value):
    return [value] + [swap(value, "seq", 2 * k) for k in range(1, depth())]


def plane_pieces(value):
    return [value] + [swap(value, "head", r) for r in range(1, lax.axis_size("head"))]


def core_pieces(values):
    return values, [swap(v, "seq", 1) for v in values]


def line_sum(values):
    total = values[0].astype(F32)
    for k in range(1, depth()):
        total = total + swap(values[k], "seq", 2 * k).astype(F32)
    return total


def plane_sum(values):
    total = values[0].astype(F32)
    for r in range(1, lax.axis_size("head")):
        total = total + swap(values[r], "head", r).astype(F32)
    return total


def pick(value, index, axis=0):
    return lax.dynamic_index_in_dim(value, index, axis, keepdims=False)


def any_spec():
    return [pl.BlockSpec(memory_space=pl.ANY)]


def after(value, *others):
    return pl.pallas_call(
        lambda *refs: None,
        out_shape=jax.ShapeDtypeStruct(value.shape, value.dtype),
        in_specs=any_spec() * (1 + len(others)),
        out_specs=any_spec()[0],
        input_output_aliases={0: 0},
        name="after",
    )(value, *others)


def sync(*values):
    return pl.pallas_call(
        lambda *refs: None,
        out_shape=tuple(jax.ShapeDtypeStruct(v.shape, v.dtype) for v in values),
        in_specs=any_spec() * len(values),
        out_specs=tuple(any_spec() * len(values)),
        input_output_aliases={i: i for i in range(len(values))},
        name="sync",
    )(*values)


def bits_of(size):
    return [1 << i for i in range(size.bit_length() - 1)]


def plane_order(flip):
    bits = bits_of(lax.axis_size("head"))
    order = [0]
    for bit in bits[::-1] if flip else bits:
        order = order + [i | bit for i in order]
    return order


class Spread:
    def __init__(self, name, value):
        self.name, self.held, self.rest = name, value[None], self.plan()

    def send(self):
        with jax.named_scope(self.name):
            self.got = swap(self.held, self.axis, self.rest[0])
        return [self.got]

    def take(self, got):
        self.rest = self.rest[1:]
        with jax.named_scope(self.name):
            self.held = self.join(self.held, got[0])
        return self

    @property
    def more(self):
        return bool(self.rest)


class Line(Spread):
    axis = "seq"

    def plan(self):
        return [2 * bit for bit in bits_of(depth())[::-1]]

    def join(self, held, got):
        return jnp.stack([held, got], axis=1).reshape((-1,) + held.shape[1:])


class Plane:
    def __init__(self, name, first, second):
        self.name, self.held = name, [first[None], second[None]]
        self.rest = bits_of(lax.axis_size("head"))

    def send(self):
        count = len(self.rest)
        with jax.named_scope(self.name):
            masks = (self.rest[0], bits_of(lax.axis_size("head"))[count - 1])
            return [swap(v, "head", m) for v, m in zip(self.held, masks)]

    def take(self, got):
        self.rest = self.rest[1:]
        if not self.rest:
            self.held = [v for pair in zip(self.held, got) for v in pair]
            return self
        with jax.named_scope(self.name):
            self.held = [jnp.concatenate([v, g], axis=0) for v, g in zip(self.held, got)]
        return self

    @property
    def more(self):
        return bool(self.rest)


def add_halves(first, second):
    half = first.shape[0] // 2
    return [
        (first[i].astype(F32) + second[i].astype(F32)).astype(BF16)
        for i in (slice(0, half), slice(half, None))
    ]


class PlaneSum:
    def __init__(self, name, *halves):
        self.name, self.held, self.left = name, halves, len(bits_of(lax.axis_size("head")))

    def send(self):
        bits = bits_of(lax.axis_size("head"))
        masks = (bits[self.left - 1], bits[len(bits) - self.left])
        with jax.named_scope(self.name):
            return [swap(sent, "head", m) for (_, sent), m in zip(self.held, masks)]

    def take(self, got):
        self.left -= 1
        with jax.named_scope(self.name):
            if self.left:
                self.held = [add_halves(kept, g) for (kept, _), g in zip(self.held, got)]
            else:
                self.held = [
                    (kept.astype(F32) + g.astype(F32)).astype(BF16)[0]
                    for (kept, _), g in zip(self.held, got)
                ]
        return self

    @property
    def more(self):
        return self.left > 0


class LineSum:
    def __init__(self, name, value):
        self.name, self.held, self.rest = name, value, bits_of(depth())

    def send(self):
        pairs = self.held.reshape((-1, 2) + self.held.shape[1:])
        self.kept = pairs[:, 0]
        with jax.named_scope(self.name):
            return [swap(pairs[:, 1], "seq", 2 * self.rest[0])]

    def take(self, got):
        self.rest = self.rest[1:]
        with jax.named_scope(self.name):
            self.held = self.kept.astype(F32) + got[0].astype(F32)
            if self.rest:
                self.held = self.held.astype(BF16)
            else:
                self.held = self.held[0]
        return self

    @property
    def more(self):
        return bool(self.rest)


class Sends:
    def __init__(self, name, values, axis, masks):
        self.name, self.values, self.axis, self.masks = name, values, axis, masks
        self.more = True

    def send(self):
        with jax.named_scope(self.name):
            return [swap(v, self.axis, m) for v, m in zip(self.values, self.masks)]

    def take(self, got):
        self.more = False
        self.held = list(got)
        return self


def core_send(name, values):
    return Sends(name, values, "seq", [1] * len(values))


def head_send(name, values):
    return Sends(name, values, "head", list(range(1, lax.axis_size("head"))))


class Phase:
    def __init__(self, *flows):
        self.flows = [flow for flow in flows if flow is not None and flow.more]
        self.sent = [flow.send() for flow in self.flows]

    def end(self, *others):
        flat = [v for got in self.sent for v in got] + list(others)
        flat = list(sync(*flat))
        for flow, got in zip(self.flows, self.sent):
            flow.take([flat.pop(0) for _ in got])
        return flat


def run(*flows):
    while any(flow.more for flow in flows):
        Phase(*flows).end()
    return [flow.held for flow in flows]


def take(refs, count):
    return [refs.pop(0) for _ in range(count)]


def part_places(here, own, other, size):
    return [
        ((ref, line), pl.multiple_of((here ^ (2 * line + core)) * size, size))
        for core, ref in enumerate((own, other))
        for line in range(ref.shape[0])
    ]


class Pack:
    def __init__(self, size, heads, seq_count):
        self.size, self.rank = size, RANK // seq_count
        self.query_parts = heads * QDIM // size
        self.expand_parts = 2 * heads * HDIM // size
        self.expand_at = self.query_parts * size
        self.out_at = self.expand_at + self.expand_parts * self.rank
        self.out_rows = heads * HDIM
        self.rows = self.out_at + self.out_rows

    def query(self, ref, part):
        array, line = ref
        return array[line, part * self.size : (part + 1) * self.size, :]

    def expand(self, ref, part):
        array, line = ref
        at = part * self.rank
        return array[line, at : at + self.rank, :]

    def out(self, ref):
        array, line = ref
        return array[line, : self.out_rows, :]


def latent_kernel(plane, s_ref, x_ref, cos, sin, *refs):
    refs = list(refs)
    own, other = take(refs, plane), take(refs, plane)
    keys_out, lat_out, gattn_out, gffn_out, glat_out, wide_out, full = refs
    here, column = s_ref[0], s_ref[1]
    rows = RANK + RDIM
    lines, each, size = own[0].shape
    for core, group in enumerate((own, other)):
        for line in range(lines):
            place = pl.multiple_of((here ^ (2 * line + core)) * size, size)
            for r, ref in enumerate(group):
                top = pl.multiple_of((column ^ r) * each, 16)
                full[pl.ds(top, each), pl.ds(place, size)] = ref[line]
    x = x_ref[...].astype(F32)
    gains = full[rows : rows + 16, :].astype(F32)
    gattn_out[...] = gains[0:1]
    gffn_out[...] = gains[1:2]
    spread = gains[2 : 2 + RANK // size]
    glat = spread[:, :size]
    for i in range(1, 2 * lines):
        glat = glat + spread[:, i * size : (i + 1) * size]
    glat = jnp.concatenate([glat[i : i + 1] for i in range(RANK // size)], axis=1)
    glat_out[...] = glat
    normed = (x * rms_inverse(x) * gains[0:1]).astype(BF16)
    wide_out[...] = full[:rows, :]
    low = dot_nt(normed, wide_out[...]).astype(BF16)
    lat_out[...] = low
    low = low.astype(F32)
    comp = low[:, :RANK]
    comp = comp * rms_inverse(comp) * glat
    first, second = low[:, RANK : RANK + HALF], low[:, RANK + HALF :]
    keys_out[...] = jnp.concatenate(
        [
            comp,
            first * cos[...] - second * sin[...],
            first * sin[...] + second * cos[...],
            jnp.zeros((x.shape[0], WIDE - RANK - RDIM), F32),
        ],
        axis=1,
    ).astype(BF16)


def block_scores(query, keys, masks):
    scores = dot_nt(query, keys)
    if masks is not None:
        scores = jnp.where(masks, scores, NEG_LARGE)
    return scores


def entry(pair, order, r):
    half, j = divmod(order.index(r), len(order) // 2)
    return pair[half], j


def load_keys(pair, order, line):
    found = [entry(pair, order, r) for r in range(len(order))]
    return jnp.concatenate([ref[j, line] for ref, j in found], axis=0)


def fill_expand(here, own, other, wexp, pack):
    for ref, place in part_places(here, own, other, pack.rank):
        for part in range(pack.expand_parts):
            columns = slice(part * pack.size, (part + 1) * pack.size)
            wexp[pl.ds(place, pack.rank), columns] = pack.expand(ref, part)


def attend_masked(here, heads, order, lines, key_refs, wexp, q_out, state, qblk_ref, kblk_ref):
    acc, mx, sm = state
    group = q_out.shape[1]
    for core, ref in enumerate(key_refs):

        def step(line, carry, core=core, ref=ref):
            @pl.when((here ^ (2 * line + core)) <= here)
            def _():
                latent = load_keys(ref, order, line)
                expanded = dot(latent[:, :RANK], wexp[...]).astype(BF16)
                rope_key = latent[:, RANK : RANK + RDIM]
                allowed = kblk_ref[pl.ds(2 * line + core, 1), :] <= qblk_ref[...]
                for h in range(heads):
                    keys = jnp.concatenate(
                        [expanded[:, 2 * h * HDIM : (2 * h + 1) * HDIM], rope_key], axis=1
                    )
                    vals = expanded[:, (2 * h + 1) * HDIM : (2 * h + 2) * HDIM]
                    scores = block_scores(q_out[h], keys, allowed)
                    old = mx[h][:, :1]
                    new = jnp.maximum(old, jnp.max(scores, axis=1, keepdims=True))
                    weights = jnp.exp2((scores - new) * (SCALE * LOG2E))
                    weights = jnp.where(allowed, weights, 0.0)
                    rescale = jnp.exp2((old - new) * (SCALE * LOG2E))
                    sm[h] = sm[h] * rescale + jnp.sum(weights, axis=1, keepdims=True)
                    acc[h] = acc[h] * rescale + dot(weights.astype(BF16), vals)
                    mx[h] = jnp.broadcast_to(new, (group, HDIM))

            return carry

        lax.fori_loop(0, lines, step, 0)


def attend_whole(here, heads, order, lines, key_refs, wexp, q_out, state, all_scores, all_vals):
    acc, mx, sm = state
    wide = mx.shape[2]

    def each_block(body):
        for core, ref in enumerate(key_refs):

            def step(line, carry, core=core, ref=ref):
                @pl.when((here ^ (2 * line + core)) <= here)
                def _():
                    body(2 * line + core, ref, line)

                return carry

            lax.fori_loop(0, lines, step, 0)

    def score(place, ref, line):
        latent = load_keys(ref, order, line)
        expanded = dot(latent[:, :RANK], wexp[...]).astype(BF16)
        rope_key = latent[:, RANK : RANK + RDIM]
        for h in range(heads):
            keys = jnp.concatenate(
                [expanded[:, 2 * h * HDIM : (2 * h + 1) * HDIM], rope_key], axis=1
            )
            all_vals[place, :, h * HDIM : (h + 1) * HDIM] = expanded[
                :, (2 * h + 1) * HDIM : (2 * h + 2) * HDIM
            ]
            scores = dot_nt(q_out[h], keys)
            all_scores[h, place] = scores
            top = mx[h]
            for i in range(scores.shape[1] // wide):
                top = jnp.maximum(top, scores[:, i * wide : (i + 1) * wide])
            mx[h] = top

    each_block(score)
    for h in range(heads):
        mx[h] = jnp.broadcast_to(jnp.max(mx[h], axis=1, keepdims=True), mx.shape[1:])

    def weigh(place, ref, line):
        for h in range(heads):
            weights = jnp.exp2((all_scores[h, place] - mx[h][:, :1]) * (SCALE * LOG2E))
            total = sm[h]
            for i in range(weights.shape[1] // wide):
                total = total + weights[:, i * wide : (i + 1) * wide]
            sm[h] = total
            vals = all_vals[place, :, h * HDIM : (h + 1) * HDIM]
            acc[h] = acc[h] + dot(weights.astype(BF16), vals)

    each_block(weigh)
    for h in range(heads):
        sm[h] = jnp.broadcast_to(jnp.sum(sm[h], axis=1, keepdims=True), sm.shape[1:])


def attend_kernel(pack, heads, masked, order, tokens, *refs):
    refs = list(refs)
    (s_ref,) = take(refs, 1)
    qblk_ref, kblk_ref = take(refs, 2) if masked else (None, None)
    x, own, other = take(refs, 2), take(refs, 2), take(refs, 2)
    gain, cos, sin, w_own, w_other, e_own, e_other = take(refs, 7)
    take(refs, tokens)
    lines = own[0].shape[1]
    normed_out, q_out, att_out, lse_out = take(refs, 4)
    acc, mx, sm, wexp, *kept = refs
    group = normed_out.shape[0]
    nope = heads * HDIM
    wide = heads * HALF
    size = pack.size
    here = s_ref[0]
    fill_expand(here, e_own, e_other, wexp, pack)
    found = [entry(x, order, r) for r in range(len(order))]
    rows = jnp.concatenate([ref[j] for ref, j in found], axis=0).astype(F32)
    normed_out[...] = (rows * rms_inverse(rows) * gain[...]).astype(BF16)
    qlin = [jnp.zeros((group, size), F32) for _ in range(pack.query_parts)]
    for ref, place in part_places(here, w_own, w_other, size):
        block = normed_out[:, pl.ds(place, size)]
        qlin = [q + dot(block, pack.query(ref, part)) for part, q in enumerate(qlin)]
    qlin = jnp.concatenate(qlin, axis=1)
    first = qlin[:, nope : nope + wide]
    second = qlin[:, nope + wide :]
    turned_a = first * cos[...] - second * sin[...]
    turned_b = first * sin[...] + second * cos[...]
    for h in range(heads):
        q_out[h] = jnp.concatenate(
            [
                qlin[:, h * HDIM : (h + 1) * HDIM],
                turned_a[:, h * HALF : (h + 1) * HALF],
                turned_b[:, h * HALF : (h + 1) * HALF],
            ],
            axis=1,
        ).astype(BF16)
    acc[...] = jnp.zeros_like(acc)
    mx[...] = jnp.full_like(mx, NEG_LARGE)
    sm[...] = jnp.zeros_like(sm)
    if masked:
        attend_masked(
            here, heads, order, lines, (own, other), wexp, q_out, (acc, mx, sm), qblk_ref, kblk_ref
        )
    else:
        attend_whole(here, heads, order, lines, (own, other), wexp, q_out, (acc, mx, sm), *kept)
    for h in range(heads):
        att_out[:, h * HDIM : (h + 1) * HDIM] = (acc[h] / sm[h]).astype(BF16)
        lse_out[h] = mx[h] * (SCALE * LOG2E) + jnp.log2(sm[h])


def out_kernel(pack, tokens, *refs):
    refs = list(refs)
    s_ref, att, w_own, w_other = take(refs, 4)
    take(refs, tokens)
    each = refs[0].shape[0]
    for ref, place in part_places(s_ref[0], w_own, w_other, pack.size):
        block = dot(att[...], pack.out(ref)).astype(BF16)
        for r, out in enumerate(refs):
            out[:, pl.ds(place, pack.size)] = block[r * each : (r + 1) * each]


def project(pack, here, att, weights, plane, tokens):
    width = 2 * weights[0].shape[0] * pack.size
    return pl.pallas_call(
        functools.partial(out_kernel, pack, len(tokens)),
        out_shape=tuple(
            [jax.ShapeDtypeStruct((att.shape[0] // plane, width), BF16)] * plane
        ),
        in_specs=smem_spec() + vmem_specs(3) + any_spec() * len(tokens),
        out_specs=tuple(vmem_specs(plane)),
        compiler_params=pltpu.CompilerParams(vmem_limit_bytes=40 * MIB),
        cost_estimate=pl.CostEstimate(
            flops=1_000_000_000, bytes_accessed=5_000_000, transcendentals=0
        ),
        name="project",
    )(here, att, *weights, *tokens)


def attend_back_kernel(pack, heads, masked, orders, *refs):
    refs = list(refs)
    (s_ref,) = take(refs, 1)
    qblk_ref, kblk_ref = take(refs, 2) if masked else (None, None)
    cos, sin, w_own, w_other, e_own, e_other, o_own, o_other = take(refs, 8)
    per_batch = [
        (take(refs, 2), take(refs, 2), take(refs, 2), *take(refs, 4)) for _ in orders
    ]
    take(refs, 1)
    batches, plane = len(orders), len(orders[0])
    lines = w_own.shape[0]
    gpart_outs = [take(refs, 2) for _ in orders]
    own_out, other_out, dw_own, dw_other = take(refs, 4)
    gq_acc, gqlin, gatt, wexp, dwexp, dwq, dwo = refs
    group = gqlin.shape[0]
    each = group // plane
    nope = heads * HDIM
    wide = heads * HALF
    size = pack.size
    here = s_ref[0]
    fill_expand(here, e_own, e_other, wexp, pack)
    dwexp[...] = jnp.zeros_like(dwexp)
    places = part_places(here, w_own, w_other, size)
    for b, order in enumerate(orders):
        gres, own, other, normed, q_ref, att, lse = per_batch[b]
        total = jnp.zeros((group, nope), F32)
        for i, (ref, place) in enumerate(part_places(here, o_own, o_other, size)):
            found = [entry(gres, order, r) for r in range(plane)]
            block = jnp.concatenate([g[j, :, pl.ds(place, size)] for g, j in found], axis=0)
            total = total + dot_nt(block, pack.out(ref))
            term = dot_tn(att[...], block)
            dwo[i] = term if b == 0 else dwo[i] + term
        gatt[...] = total.astype(BF16)
        gq_acc[...] = jnp.zeros_like(gq_acc)
        deltas = [
            jnp.sum(
                gatt[:, h * HDIM : (h + 1) * HDIM].astype(F32)
                * att[:, h * HDIM : (h + 1) * HDIM].astype(F32),
                axis=1,
                keepdims=True,
            )
            for h in range(heads)
        ]
        for core, (ref, out) in enumerate(((own, own_out), (other, other_out))):

            def step(
                line, carry, core=core, key_ref=ref, out=out, b=b, q_ref=q_ref, lse=lse,
                deltas=deltas, order=order,
            ):
                live = (here ^ (2 * line + core)) <= here

                @pl.when(jnp.logical_not(live))
                def _():
                    out[line, b] = jnp.zeros((group, WIDE), BF16)

                @pl.when(live)
                def _():
                    latent = load_keys(key_ref, order, line)
                    expanded = dot(latent[:, :RANK], wexp[...]).astype(BF16)
                    rope_key = latent[:, RANK : RANK + RDIM]
                    allowed = None
                    if masked:
                        allowed = kblk_ref[pl.ds(2 * line + core, 1), :] <= qblk_ref[...]
                    grads = []
                    grad_rope = jnp.zeros((group, RDIM), F32)
                    for h in range(heads):
                        keys = jnp.concatenate(
                            [expanded[:, 2 * h * HDIM : (2 * h + 1) * HDIM], rope_key], axis=1
                        )
                        vals = expanded[:, (2 * h + 1) * HDIM : (2 * h + 2) * HDIM]
                        query = q_ref[h]
                        gout = gatt[:, h * HDIM : (h + 1) * HDIM]
                        scores = block_scores(query, keys, allowed)
                        probs = jnp.exp2(scores * (SCALE * LOG2E) - lse[h][:, :1])
                        if masked:
                            probs = jnp.where(allowed, probs, 0.0)
                        gprobs = dot_nt(gout, vals)
                        gscores = (probs * (gprobs - deltas[h])).astype(BF16)
                        gq_acc[h] = gq_acc[h] + dot(gscores, keys)
                        gkeys = dot_tn(gscores, query) * SCALE
                        gvals = dot_tn(probs.astype(BF16), gout)
                        grads.append(gkeys[:, :HDIM].astype(BF16))
                        grads.append(gvals.astype(BF16))
                        grad_rope = grad_rope + gkeys[:, HDIM:]
                    gexp = jnp.concatenate(grads, axis=1)
                    dwexp[...] = dwexp[...] + dot_tn(latent[:, :RANK], gexp)
                    gcomp = dot_nt(gexp, wexp[...])
                    blank = jnp.zeros((group, WIDE - RANK - RDIM), F32)
                    out[line, b] = jnp.concatenate([gcomp, grad_rope, blank], axis=1).astype(BF16)

                return carry

            lax.fori_loop(0, lines, step, 0)
        firsts, seconds = [], []
        for h in range(heads):
            value = gq_acc[h] * SCALE
            gqlin[:, h * HDIM : (h + 1) * HDIM] = value[:, :HDIM].astype(BF16)
            firsts.append(value[:, HDIM : HDIM + HALF])
            seconds.append(value[:, HDIM + HALF :])
        first = jnp.concatenate(firsts, axis=1)
        second = jnp.concatenate(seconds, axis=1)
        gqlin[:, nope : nope + wide] = (first * cos[...] + second * sin[...]).astype(BF16)
        gqlin[:, nope + wide :] = (second * cos[...] - first * sin[...]).astype(BF16)
        for i, (ref, place) in enumerate(places):
            weight = jnp.concatenate(
                [pack.query(ref, part) for part in range(pack.query_parts)], axis=1
            )
            block = dot_nt(gqlin[...], weight).astype(BF16)
            for r in range(plane):
                half, j = divmod(order.index(r), plane // 2)
                gpart_outs[b][half][j, :, pl.ds(place, size)] = block[r * each : (r + 1) * each]
            term = dot_tn(normed[:, pl.ds(place, size)], gqlin[...])
            dwq[i] = term if b == 0 else dwq[i] + term
    for core, out in enumerate((dw_own, dw_other)):
        for line in range(lines):
            i = core * lines + line
            term = dwq[i].astype(BF16)
            for part in range(pack.query_parts):
                out[line, part * size : (part + 1) * size] = term[
                    :, part * size : (part + 1) * size
                ]
            place = pl.multiple_of((here ^ (2 * line + core)) * pack.rank, pack.rank)
            term = dwexp[pl.ds(place, pack.rank), :].astype(BF16)
            for part in range(pack.expand_parts):
                at = pack.expand_at + part * pack.rank
                out[line, at : at + pack.rank] = term[:, part * size : (part + 1) * size]
            out[line, pack.out_at : pack.rows] = dwo[i].astype(BF16)


def vmem_specs(count):
    return [pl.BlockSpec(memory_space=pltpu.VMEM)] * count


def smem_spec():
    return [pl.BlockSpec(memory_space=pltpu.SMEM)]


def own_latents(place, x, cos, sin, own, other):
    rows, width = x.shape
    total = len(own) * own[0].shape[1]
    return pl.pallas_call(
        functools.partial(latent_kernel, len(own)),
        out_shape=(
            jax.ShapeDtypeStruct((rows, WIDE), BF16),
            jax.ShapeDtypeStruct((rows, RANK + RDIM), BF16),
            jax.ShapeDtypeStruct((1, width), F32),
            jax.ShapeDtypeStruct((1, width), F32),
            jax.ShapeDtypeStruct((1, RANK), F32),
            jax.ShapeDtypeStruct((RANK + RDIM, width), BF16),
        ),
        in_specs=smem_spec() + vmem_specs(3 + len(own) + len(other)),
        out_specs=tuple(vmem_specs(6)),
        scratch_shapes=[pltpu.VMEM((total, width), BF16)],
        compiler_params=pltpu.CompilerParams(vmem_limit_bytes=40 * MIB),
        cost_estimate=pl.CostEstimate(
            flops=1_000_000_000, bytes_accessed=6_000_000, transcendentals=1_000
        ),
        name="own_latents",
    )(place, x, cos, sin, *own, *other)


def whole(value):
    rank = len(value.shape)
    return pl.BlockSpec(value.shape, lambda i: (0,) * rank)


def attend(pack, here, marks, order, x, gain, cos, sin, keys, weights, heads, tokens):
    plane, each, width = x[0].shape
    group = 2 * plane * each
    lines = keys[0].shape[1]
    inputs = [*marks, *x, *keys, gain, cos, sin, *weights]
    return pl.pallas_call(
        functools.partial(attend_kernel, pack, heads, bool(marks), order, len(tokens)),
        out_shape=(
            jax.ShapeDtypeStruct((group, width), BF16),
            jax.ShapeDtypeStruct((heads, group, QDIM), BF16),
            jax.ShapeDtypeStruct((group, heads * HDIM), BF16),
            jax.ShapeDtypeStruct((heads, group, HDIM), F32),
        ),
        in_specs=smem_spec() + vmem_specs(len(inputs)) + any_spec() * len(tokens),
        out_specs=tuple(vmem_specs(4)),
        scratch_shapes=[pltpu.VMEM((heads, group, HDIM), F32)] * 3
        + [pltpu.VMEM((RANK, 2 * heads * HDIM), BF16)]
        + (
            []
            if marks
            else [
                pltpu.VMEM((heads, 2 * lines, group, group), F32),
                pltpu.VMEM((2 * lines, group, heads * HDIM), BF16),
            ]
        ),
        compiler_params=pltpu.CompilerParams(vmem_limit_bytes=60 * MIB),
        cost_estimate=pl.CostEstimate(
            flops=16_000_000_000, bytes_accessed=16_000_000, transcendentals=4_000_000
        ),
        name="attend",
    )(here, *inputs, *tokens)


def attend_back(pack, here, marks, orders, cos, sin, weights, out_weights, per_batch, token):
    batches, plane = len(orders), len(orders[0])
    lines = weights[0].shape[0]
    heads, group = per_batch[0][7].shape[:2]
    each, width = per_batch[0][0].shape[1:]
    size = pack.size
    outs = [jax.ShapeDtypeStruct((plane // 2, each, width), BF16)] * (2 * batches)
    outs += [jax.ShapeDtypeStruct((lines, batches, group, WIDE), BF16)] * 2
    outs += [jax.ShapeDtypeStruct((lines, pack.rows, size), BF16)] * 2
    inputs = [*marks, cos, sin, *weights, *out_weights]
    inputs += [v for args in per_batch for v in args]
    res = pl.pallas_call(
        functools.partial(attend_back_kernel, pack, heads, bool(marks), orders),
        out_shape=tuple(outs),
        in_specs=smem_spec() + vmem_specs(len(inputs)) + any_spec(),
        out_specs=tuple(vmem_specs(len(outs))),
        scratch_shapes=[
            pltpu.VMEM((heads, group, QDIM), F32),
            pltpu.VMEM((group, heads * QDIM), BF16),
            pltpu.VMEM((group, heads * HDIM), BF16),
            pltpu.VMEM((RANK, 2 * heads * HDIM), BF16),
            pltpu.VMEM((RANK, 2 * heads * HDIM), F32),
            pltpu.VMEM((2 * lines, size, heads * QDIM), F32),
            pltpu.VMEM((2 * lines, heads * HDIM, size), F32),
        ],
        compiler_params=pltpu.CompilerParams(vmem_limit_bytes=63 * MIB),
        cost_estimate=pl.CostEstimate(
            flops=32_000_000_000, bytes_accessed=30_000_000, transcendentals=8_000_000
        ),
        name="attend_back",
    )(here, *inputs, token)
    return res[: 2 * batches], res[2 * batches : 2 * batches + 2], res[2 * batches + 2 :]


def shared_kernel(s_ref, *refs):
    *pieces, gates_out, down_out = refs
    here = s_ref[0]
    _, kinds, rows, size = pieces[0].shape
    pad = down_out.shape[0]
    gates_out[...] = jnp.zeros_like(gates_out)
    down_out[...] = jnp.zeros_like(down_out)
    for k, ref in enumerate(pieces):
        for core in range(2):
            place = pl.multiple_of(((here // 2) ^ k) * (2 * size) + core * size, size)
            for kind in range(2):
                gates_out[kind * pad : kind * pad + rows, pl.ds(place, size)] = ref[core, kind]
            down_out[:rows, pl.ds(place, size)] = ref[core, 2]


def shared_whole(here, pieces, pad):
    width = 2 * len(pieces) * pieces[0].shape[-1]
    return pl.pallas_call(
        shared_kernel,
        out_shape=(
            jax.ShapeDtypeStruct((2 * pad, width), BF16),
            jax.ShapeDtypeStruct((pad, width), BF16),
        ),
        in_specs=smem_spec() + vmem_specs(len(pieces)),
        out_specs=tuple(vmem_specs(2)),
        cost_estimate=pl.CostEstimate(flops=0, bytes_accessed=4_000_000, transcendentals=0),
        name="shared_whole",
    )(here, *pieces)


def key_back_kernel(got, low_ref, gain, cos, sin, grad_out, gain_out):
    value = got[...]
    comp = low_ref[:, :RANK].astype(F32)
    inverse = rms_inverse(comp)
    hat = comp * inverse
    grad = value[:, :RANK]
    gain_out[...] = jnp.sum(grad * hat, axis=0, keepdims=True)
    scaled = grad * gain[...]
    grad = inverse * (scaled - hat * jnp.mean(scaled * hat, axis=-1, keepdims=True))
    first, second = value[:, RANK : RANK + HALF], value[:, RANK + HALF : RANK + RDIM]
    grad_out[...] = jnp.concatenate(
        [
            grad,
            first * cos[...] + second * sin[...],
            second * cos[...] - first * sin[...],
            jnp.zeros((value.shape[0], WIDE - RANK - RDIM), F32),
        ],
        axis=1,
    ).astype(BF16)


def key_back(got, low, gain, cos, sin):
    return pl.pallas_call(
        key_back_kernel,
        out_shape=(
            jax.ShapeDtypeStruct(got.shape, BF16),
            jax.ShapeDtypeStruct((1, RANK), F32),
        ),
        in_specs=vmem_specs(5),
        out_specs=tuple(vmem_specs(2)),
        name="key_back",
    )(got, low, gain, cos, sin)


def inputs_back_kernel(first, second, grad_latent, latent_t, x_ref, gain, residual, out, gain_out):
    grad = jnp.concatenate([first[...], second[...]], axis=0).astype(F32)
    grad = grad + dot(grad_latent[:, : RANK + RDIM], latent_t[...])
    x = x_ref[...].astype(F32)
    inverse = rms_inverse(x)
    hat = x * inverse
    gain_out[...] = jnp.sum(grad * hat, axis=0, keepdims=True)
    scaled = grad * gain[...]
    grad = inverse * (scaled - hat * jnp.mean(scaled * hat, axis=-1, keepdims=True))
    out[...] = (grad + residual[...]).astype(BF16)


def inputs_back(first, second, grad_latent, latent_t, x, gain, residual):
    return pl.pallas_call(
        inputs_back_kernel,
        out_shape=(
            jax.ShapeDtypeStruct(x.shape, BF16),
            jax.ShapeDtypeStruct(gain.shape, F32),
        ),
        in_specs=vmem_specs(7),
        out_specs=tuple(vmem_specs(2)),
        compiler_params=pltpu.CompilerParams(vmem_limit_bytes=40 * MIB),
        name="inputs_back",
    )(first, second, grad_latent, latent_t, x, gain, residual)


def latent_back_kernel(batches, plane, share, s_ref, *refs):
    refs = list(refs)
    grads, normed = take(refs, plane), take(refs, batches)
    gattn, gffn, glat, own_out, other_out, full = refs
    here, column = s_ref[0], s_ref[1]
    lines, rows, size = own_out.shape
    for b in range(batches):
        mine = jnp.concatenate([g[b, :, : RANK + RDIM] for g in grads], axis=0)
        term = dot_tn(mine, normed[b][...])
        full[...] = term if b == 0 else full[...] + term
    top = pl.multiple_of(column * share, 8)
    parts = RANK // size
    lat = [glat[:, i * size : (i + 1) * size] for i in range(parts)]
    blank = jnp.zeros((rows - share - 2 - parts, size), F32)
    for core, out in enumerate((own_out, other_out)):
        for line in range(lines):
            place = pl.multiple_of((here ^ (2 * line + core)) * size, size)
            columns = pl.ds(place, size)
            out[line] = jnp.concatenate(
                [full[pl.ds(top, share), columns], gattn[:, columns], gffn[:, columns], *lat, blank],
                axis=0,
            ).astype(BF16)


def latent_back(here, grads, normed, gains, lines, share):
    width = normed[0].shape[1]
    out = jax.ShapeDtypeStruct((lines, share + 16, width // (2 * lines)), BF16)
    return pl.pallas_call(
        functools.partial(latent_back_kernel, len(normed), len(grads), share),
        out_shape=(out, out),
        in_specs=smem_spec() + vmem_specs(len(grads) + len(normed) + 3),
        out_specs=tuple(vmem_specs(2)),
        scratch_shapes=[pltpu.VMEM((RANK + RDIM, width), F32)],
        compiler_params=pltpu.CompilerParams(vmem_limit_bytes=40 * MIB),
        cost_estimate=pl.CostEstimate(
            flops=2_000_000_000, bytes_accessed=5_000_000, transcendentals=0
        ),
        name="latent_back",
    )(here, *grads, *normed, *gains)


def feed_kernel(orders, per, side, aliased, *refs):
    refs = list(refs)
    slot, gate = take(refs, 2)
    xa, xb, ca, cb = [take(refs, 2) for _ in range(4)]
    wg, wu, wd, sgut, sd = take(refs, 5)
    came = take(refs, 2) if side == 0 else None
    take(refs, aliased + 1)
    rows_out, grows_out, act_out, gpre_out, gup_out, dsgut, dsd = take(refs, 7)
    pieces = refs
    plane, _, half, width = xa[0].shape
    plane = 2 * plane
    each = 2 * half
    group = plane * each
    cap = rows_out.shape[2]
    pad = sd.shape[0]

    @pl.when(pl.program_id(0) == 0)
    def _():
        dsgut[...] = jnp.zeros_like(dsgut)
        dsd[...] = jnp.zeros_like(dsd)

    picks, gates = [], []
    for i in range(per):
        chosen = lax.broadcasted_iota(jnp.int32, (cap, group), 0) == slot[i]
        gates.append(jnp.sum(jnp.where(chosen, gate[i], 0.0), axis=1, keepdims=True))
        picks.append(chosen.astype(F32))
    at_a, at_b = [[order.index(r) for r in range(plane)] for order in orders]

    def tokens_of(*pairs):
        found = [
            (i, *entry(pair, order, r))
            for i in range(per)
            for r in range(plane)
            for pair, order in zip(pairs, orders)
        ]
        return jnp.concatenate([ref[j, i] for i, ref, j in found], axis=0)

    x, cot = tokens_of(xa, xb), tokens_of(ca, cb)
    gates = jnp.concatenate(gates, axis=0)
    rows = jnp.concatenate(
        [
            dot(picks[i].astype(BF16), x[i * group : (i + 1) * group]).astype(BF16)
            for i in range(per)
        ],
        axis=0,
    )
    grows = jnp.concatenate(
        [dot(picks[i].astype(BF16), cot[i * group : (i + 1) * group]) for i in range(per)],
        axis=0,
    )
    grows = (grows * gates).astype(BF16)
    pre = dot_nt(rows, wg[...])
    upp = dot_nt(rows, wu[...])
    sig = 1.0 / (1.0 + jnp.exp(-pre))
    silu = pre * sig
    act = (silu * upp).astype(BF16)
    geact = dot_nt(grows, wd[...])
    gpre = (geact * upp * (sig * (1.0 + pre * (1.0 - sig)))).astype(BF16)
    gup = (geact * silu).astype(BF16)
    for i in range(per):
        part = slice(i * cap, (i + 1) * cap)
        rows_out[0, i] = rows[part]
        grows_out[0, i] = grows[part]
        act_out[0, i] = act[part]
        gpre_out[0, i] = gpre[part]
        gup_out[0, i] = gup[part]
    made = (dot(act, wd[...]) * gates).astype(BF16)
    gmade = (dot(gpre, wg[...]) + dot(gup, wu[...])).astype(BF16)
    both = dot_nt(x, sgut[...])
    spre, supp = both[:, :pad], both[:, pad:]
    ssig = 1.0 / (1.0 + jnp.exp(-spre))
    ssilu = spre * ssig
    sact = (ssilu * supp).astype(BF16)
    gsact = dot_nt(cot, sd[...])
    gspre = (gsact * supp * (ssig * (1.0 + spre * (1.0 - ssig)))).astype(BF16)
    gsupp = (gsact * ssilu).astype(BF16)
    gsboth = jnp.concatenate([gspre, gsupp], axis=1)
    dsgut[...] = dsgut[...] + dot_tn(gsboth, x)
    dsd[...] = dsd[...] + dot_tn(sact, cot)
    for i in range(per):
        back = picks[i].T.astype(BF16)
        toks = slice(i * group, (i + 1) * group)
        part = slice(i * cap, (i + 1) * cap)
        out = dot(
            jnp.concatenate([back, sact[toks]], axis=1),
            jnp.concatenate([made[part], sd[...]], axis=0),
        )
        gx = dot(
            jnp.concatenate([back, gsboth[toks]], axis=1),
            jnp.concatenate([gmade[part], sgut[...]], axis=0),
        )
        if side == 1:
            pieces[0][i] = out.astype(BF16)
            pieces[1][i] = gx.astype(BF16)
            continue
        out = (out + came[0][i].astype(F32)).astype(BF16)
        gx = (gx + came[1][i].astype(F32)).astype(BF16)
        for value, (keep_a, send_a, keep_b, send_b) in ((out, pieces[:4]), (gx, pieces[4:])):
            for r in range(plane):
                for part_of, at, both in ((0, at_a, (keep_a, send_a)), (1, at_b, (keep_b, send_b))):
                    top = r * each + part_of * half
                    ref = both[at[r] // (plane // 2)]
                    ref[at[r] % (plane // 2), i] = value[top : top + half]


def feed(
    here, orders, b, side, batches, cap, slot, gate, rows, cots, weights, came, earlier, token
):
    plane, lines, half, width = rows[0].shape
    plane = 2 * plane
    group = 2 * plane * half
    per = 2 if group <= 256 and lines % 2 == 0 else 1
    steps = lines // per
    hidden = weights[0].shape[0]
    pad = weights[-1].shape[0]

    def fixed(shape):
        return pl.BlockSpec(shape, lambda i: (0,) * len(shape), pipeline_mode=pl.Buffered(1))

    def block(count, size):
        return pl.BlockSpec((count, per, size, width), lambda i: (0, i, 0, 0))

    def saved(size):
        return pl.BlockSpec((1, per, cap, size), lambda i: (b, side * steps + i, 0, 0))

    mark = pl.BlockSpec((per, 1, group), lambda i: (i, 0, 0))
    flat = pl.BlockSpec((per, group, width), lambda i: (i, 0, 0))
    keep = [width, width, hidden, hidden, hidden]
    shapes = [jax.ShapeDtypeStruct((batches, 2 * lines, cap, size), BF16) for size in keep]
    shapes += [
        jax.ShapeDtypeStruct((2 * pad, width), F32),
        jax.ShapeDtypeStruct((pad, width), F32),
    ]
    out_specs = [saved(size) for size in keep] + [fixed((2 * pad, width)), fixed((pad, width))]
    if side == 1:
        shapes += [jax.ShapeDtypeStruct((lines, group, width), BF16)] * 2
        out_specs += [flat] * 2
    else:
        shapes += [jax.ShapeDtypeStruct((plane // 2, lines, half, width), BF16)] * 8
        out_specs += [block(plane // 2, half)] * 8
    in_specs = [mark, mark] + [block(plane // 2, half)] * 8
    in_specs += [fixed(w.shape) for w in weights]
    inputs = [slot, gate, *rows, *cots, *weights]
    if side == 0:
        in_specs += [flat] * 2
        inputs += list(came)
    aliases = {}
    for value, place in earlier:
        aliases[len(inputs)] = place
        inputs.append(value)
        in_specs += any_spec()
    inputs.append(token)
    in_specs += any_spec()
    return pl.pallas_call(
        functools.partial(feed_kernel, orders, per, side, len(earlier)),
        grid=(steps,),
        out_shape=tuple(shapes),
        in_specs=in_specs,
        out_specs=tuple(out_specs),
        input_output_aliases=aliases,
        compiler_params=pltpu.CompilerParams(vmem_limit_bytes=63 * MIB),
        cost_estimate=pl.CostEstimate(
            flops=24_000_000_000, bytes_accessed=40_000_000, transcendentals=1_000_000
        ),
        name="feed",
    )(*inputs)


def local(
    inputs,
    cotangent,
    routes,
    gate_weights,
    attn_gain,
    latent_gain,
    ffn_gain,
    query_proj,
    latent_proj,
    expand_proj,
    out_proj,
    shared_gate,
    shared_up,
    shared_down,
    expert_gate,
    expert_up_weight,
    expert_down,
):
    seq_count = lax.axis_size("seq")
    head_count = lax.axis_size("head")
    seq_index = lax.axis_index("seq")
    head_index = lax.axis_index("head")
    lines = depth()
    line, core = seq_index // 2, seq_index % 2
    batches, each, width = inputs.shape
    group = each * head_count
    heads = out_proj.shape[0] // HDIM
    serial = group > BLOCK
    here = jnp.stack([seq_index, head_index])
    positions = seq_index * group + jnp.arange(group, dtype=jnp.int32)
    away = jnp.arange(head_count, dtype=jnp.int32) ^ head_index

    shard = latent_proj.shape[0]
    pack = Pack(shard, heads, seq_count)
    n_lat = latent_gain.shape[0]
    lat_gain = lax.dynamic_update_slice_in_dim(
        jnp.zeros((RANK,), BF16), latent_gain, seq_index * n_lat, 0
    )
    unit = 16 * head_count
    lat_rows = -(-(RANK + RDIM + 16) // unit) * unit
    gain_part = jnp.concatenate(
        [attn_gain[None], ffn_gain[None], lat_gain.reshape(RANK // shard, shard)], axis=0
    )
    gain_part = jnp.pad(gain_part, ((0, lat_rows - RANK - RDIM - gain_part.shape[0]), (0, 0)))
    lat_mine = jnp.concatenate([jnp.transpose(latent_proj), gain_part], axis=0)
    lat_each = lat_rows // head_count
    lat_mine = lax.dynamic_slice_in_dim(lat_mine, head_index * lat_each, lat_each, 0)
    orders = [plane_order(False), plane_order(True)]
    lat_line = Sends("latent_weights", [lat_mine] * (lines - 1), "seq", [2 * k for k in range(1, lines)])
    xs_flow = Plane("inputs", inputs[0], inputs[1])
    phase = Phase(lat_line, xs_flow)

    pair = head_count // 2
    expert_ids = jnp.arange(seq_count, dtype=jnp.int32) * pair + head_index // 2
    hits = routes[None] == expert_ids[:, None, None, None]
    gate_of = jnp.sum(jnp.where(hits, gate_weights[None], 0.0), axis=-1)
    named = jnp.any(hits, axis=-1).astype(F32)
    both = jnp.stack([gate_of, named]).reshape(2, seq_count, batches, head_count, each)
    gate_of, named = jnp.take(both, away, axis=3).reshape(2, seq_count, batches, group)
    ahead = jnp.arange(group)[:, None] < jnp.arange(group)[None, :]
    rank = lax.dot_general(
        named.astype(BF16), ahead.astype(BF16), (((2,), (0,)), ((), ())), preferred_element_type=F32
    )
    gate_high = gate_of.astype(BF16)
    mark_mine = jnp.stack(
        [
            jnp.where(named > 0.0, jnp.minimum(rank, 255.0), -1.0).astype(BF16),
            gate_high,
            (gate_of - gate_high.astype(F32)).astype(BF16),
        ],
        axis=1,
    )
    mark_size = mark_mine.size
    mark_rows = -(-mark_size // (16 * shard)) * 16
    mark_mine = jnp.pad(mark_mine.reshape(-1), (0, mark_rows * shard - mark_size)).reshape(
        mark_rows, shard
    )

    cols = query_proj.reshape(query_proj.shape[0], heads, QDIM)
    query_mine = jnp.concatenate(
        [
            cols[..., :HDIM].reshape(-1, heads * HDIM),
            cols[..., HDIM : HDIM + HALF].reshape(-1, heads * HALF),
            cols[..., HDIM + HALF :].reshape(-1, heads * HALF),
        ],
        axis=1,
    )
    blocks = [query_mine[:, i * shard : (i + 1) * shard] for i in range(pack.query_parts)]
    blocks += [expand_proj[:, i * shard : (i + 1) * shard] for i in range(pack.expand_parts)]
    query_mine = jnp.concatenate(blocks[: pack.query_parts], axis=0)
    expand_mine = jnp.concatenate(blocks[pack.query_parts :], axis=0)
    out_mine = jnp.concatenate([out_proj, mark_mine], axis=0)

    lat_mine, query_mine = phase.end(lat_mine, query_mine)
    lat_stack = jnp.stack([lat_mine] + lat_line.held)
    lat_plane = head_send("latent_weights", [lat_stack] * (head_count - 1))
    query_flow = Line("query_weights", query_mine)
    lat_stack, out_mine = Phase(lat_plane, query_flow).end(lat_stack, out_mine)
    lat_own = [lat_stack] + lat_plane.held
    lat_core = core_send("latent_weights", lat_own)
    cot_lines = [None, None]
    if not serial:
        (cot_mine,) = sync(after(cotangent, lat_stack))
        cot_lines = [Line("cotangents", cot_mine[b]) for b in range(batches)]
    cot_phase = Phase(cot_lines[0])
    Phase(lat_core).end()
    lat_other = lat_core.held

    cos_all, sin_all = rope_tables(positions)
    own_cos, own_sin = [
        lax.dynamic_slice_in_dim(t, head_index * each, each, 0) for t in (cos_all, sin_all)
    ]
    own_keys, own_latent, gain_attn, gain_ffn, gain_lat, latent_t = own_latents(
        here,
        inputs.reshape(batches * each, width),
        jnp.tile(own_cos, (batches, 1)),
        jnp.tile(own_sin, (batches, 1)),
        lat_own,
        lat_other,
    )
    own_keys = own_keys.reshape(batches, each, WIDE)
    key_flow = Line("keys", own_keys)
    (own_keys,) = cot_phase.end(own_keys)
    key_flow = Line("keys", own_keys)
    (expand_mine,) = Phase(key_flow, query_flow, xs_flow).end(expand_mine)
    expand_flow = Line("expand_weights", expand_mine)
    run(query_flow)
    query_core = core_send("query_weights", [query_flow.held])
    Phase(key_flow, expand_flow, query_core).end()
    run(key_flow)
    run(query_flow)
    key_plane = Plane("keys", key_flow.held[:, 0], key_flow.held[:, 1])
    shared_mine = jnp.stack(
        [
            jnp.transpose(shared_gate).reshape(seq_count, -1, shard),
            jnp.transpose(shared_up).reshape(seq_count, -1, shard),
            shared_down.reshape(seq_count, -1, shard),
        ],
        axis=1,
    ).reshape(lines, 2, 3, -1, shard)
    out_mine, shared_mine = Phase(key_plane, expand_flow, cot_lines[0]).end(out_mine, shared_mine)
    out_flow = Line("output_weights", out_mine)
    run(expand_flow)
    expand_core = core_send("expand_weights", [expand_flow.held])
    shared_kept = pick(shared_mine, core, 1)
    shared_core = core_send("shared_weights", [pick(shared_mine, core ^ 1, 1)])
    Phase(key_plane, out_flow, expand_core, shared_core).end()
    while key_plane.more:
        Phase(key_plane).end()
    key_core = core_send("keys", key_plane.held)
    first_weights = (query_flow.held, query_core.held[0], expand_flow.held, expand_core.held[0])
    Phase(key_core).end()
    keys = [(*key_plane.held[2 * b : 2 * b + 2], *key_core.held[2 * b : 2 * b + 2]) for b in range(2)]
    xs = run(xs_flow)[0]
    xs = [xs[:2], xs[2:]]

    own_rows = inputs.astype(F32)
    own_inverse = rms_inverse(own_rows)
    own_hat = own_rows * own_inverse
    cos_b, sin_b = [
        jnp.tile(
            jnp.take(t.reshape(head_count, each, HALF), away, axis=0).reshape(group, HALF),
            (1, heads),
        )
        for t in (cos_all, sin_all)
    ]
    marks = ()
    if group > BLOCK:
        place = (away[:, None] * each + jnp.arange(each, dtype=jnp.int32)[None, :]).reshape(group)
        own_block = (seq_index * group + place) // BLOCK
        offsets = jnp.arange(seq_count, dtype=jnp.int32) ^ seq_index
        key_block = (offsets[:, None] * group + place[None, :]) // BLOCK
        marks = (jnp.broadcast_to(own_block[:, None], (group, group)), key_block)
    half = each // 2
    saved, residual, ffn_hat, ffn_inverse = [], [], [], []

    def attend_batch(b, tokens):
        saved.append(
            attend(
                pack, here, marks, orders[b], xs[b], gain_attn, cos_b, sin_b, keys[b],
                first_weights, heads, tokens,
            )
        )
        return saved[-1][2]

    def ffn_rows(b, parts, got):
        total = parts[0].astype(F32)
        for value in got:
            total = total + value.astype(F32)
        residual_b = own_rows[b] + total
        inverse_b = rms_inverse(residual_b)
        hat_b = residual_b * inverse_b
        residual.append(residual_b)
        ffn_inverse.append(inverse_b)
        ffn_hat.append(hat_b)
        return Line("ffn_rows", (hat_b * gain_ffn).astype(BF16))

    def halves_of(name, value):
        return Plane(name, value[:, :half], value[:, half:])

    def keep(b, att):
        saved[b] = (*saved[b][:2], att, saved[b][3])
        return att

    cots = [None, None]
    if not serial:
        cots[0] = halves_of("cotangents", run(cot_lines[0])[0])
    window = Phase(out_flow, cots[0], cot_lines[1])
    att0 = attend_batch(0, [key_core.held[0]])
    att0 = keep(0, window.end(att0)[0])
    run(out_flow)
    out_core = core_send("output_weights", [out_flow.held])
    att0 = keep(0, Phase(out_core).end(att0)[0])
    out_weights = (out_flow.held, out_core.held[0])
    parts0 = project(pack, here, att0, out_weights, head_count, [])
    sum0 = head_send("attention_sum", parts0[1:])
    window = Phase(sum0, cots[0])
    att1 = attend_batch(1, [parts0[0]])
    att1, own0 = window.end(att1, parts0[0])
    keep(1, att1)
    parts1 = project(pack, here, att1, out_weights, head_count, [])
    rows = [ffn_rows(0, [own0], sum0.held)]
    sum1 = head_send("attention_sum", parts1[1:])
    came = shared_core.held[0]
    paired = jnp.where(
        core == 0, jnp.stack([shared_kept, came], 1), jnp.stack([came, shared_kept], 1)
    )
    cot_held = [] if serial else run(cots[0])[0]
    own1, paired, *cot_held = Phase(sum1, rows[0], cot_lines[1]).end(parts1[0], paired, *cot_held)
    rows.append(ffn_rows(1, [own1], sum1.held))

    def moves_of(paired):
        return Sends(
            "shared_weights",
            [pick(paired, line ^ k) for k in range(1, lines)],
            "seq",
            [2 * k for k in range(1, lines)],
        )

    if serial:
        run(rows[0])
        shared_moves = moves_of(paired)
        run(shared_moves)
    else:
        cots[0].held = cot_held
        cot_core = [core_send("cotangents", cots[0].held), None]
        cot_late = run(cot_lines[1])[0]
        cot_late, paired = Phase(rows[0], rows[1], cot_core[0]).end(cot_late, paired)
        row_planes = [halves_of("ffn_rows", run(rows[0])[0]), None]
        cot_late, paired = Phase(row_planes[0], rows[1]).end(cot_late, paired)
        row_late = run(rows[1])[0]
        shared_moves = moves_of(paired)
        cot_late, row_late = Phase(row_planes[0], shared_moves).end(cot_late, row_late)
        run(row_planes[0])
        row_core = [core_send("ffn_rows", row_planes[0].held), None]
        cot_late, row_late = Phase(row_core[0]).end(cot_late, row_late)
        cots[1] = halves_of("cotangents", cot_late)
        row_planes[1] = halves_of("ffn_rows", row_late)
    hidden_each = shared_gate.shape[1] // seq_count
    hidden_pad = -(-hidden_each // 128) * 128
    sgut, sdown = shared_whole(here, [pick(paired, line)] + shared_moves.held, hidden_pad)
    weights = (
        jnp.transpose(expert_gate[0]),
        jnp.transpose(expert_up_weight[0]),
        expert_down[0],
        sgut,
        sdown,
    )

    def marks_from(parts):
        flat = parts[:, pack.out_rows :].reshape(lines, -1)
        flat = flat[:, :mark_size]
        return pick(flat.reshape(lines, seq_count, 3, batches, 1, group), seq_index, 1).astype(F32)

    marks_mine = [marks_from(parts) for parts in out_weights]
    slots = [m[:, 0].astype(jnp.int32) for m in marks_mine]
    gates = [m[:, 1] + m[:, 2] for m in marks_mine]
    most_rows = 4 * group * TOPK // (3 * seq_count * pair)
    state = {"kept": [], "dsgut": 0.0, "dsd": 0.0}

    def run_feed(b, side, rows_b, cots_b, came, token):
        earlier = [(v, i) for i, v in enumerate(state["kept"])]
        res = feed(
            here, orders, b, side, batches, most_rows, slots[side][:, b], gates[side][:, b],
            rows_b, cots_b, weights, came, earlier, token,
        )
        state["kept"] = res[:5]
        state["dsgut"] = state["dsgut"] + res[5]
        state["dsd"] = state["dsd"] + res[6]
        return res[7:]

    def collect(name, values):
        return PlaneSum(name, values[:2], values[2:])

    def lines_of(name, flow):
        return LineSum(name, jnp.concatenate(flow.held, axis=1))

    def whole_sum(name, values):
        flow = collect(name, values)
        run(flow)
        return run(lines_of(name, flow))[0]

    if serial:
        grad_ffn, outs = [], []
        for b in range(batches):
            tokens = [grad_ffn[b - 1], outs[b - 1]] if b else []
            row_line = run(rows[b])[0]
            line_b = cotangent[b]
            if b:
                row_line, line_b = after(row_line, *tokens), after(line_b, *tokens)
            line_b = run(Line("cotangents", line_b))[0]
            row_plane, cot_plane = halves_of("ffn_rows", row_line), halves_of("cotangents", line_b)
            row_own, cot_own = run(row_plane, cot_plane)
            row_other = run(core_send("ffn_rows", row_own))[0]
            cot_other = run(core_send("cotangents", cot_own))[0]
            made = run_feed(b, 1, row_other, cot_other, None, row_own[0])
            came = run(core_send("feed_other", made))[0]
            made = run_feed(b, 0, row_own, cot_own, came, row_own[0])
            grad_ffn.append(whole_sum("ffn_grads", made[4:]))
            outs.append(whole_sum("outputs", made[:4]))
        kept = state["kept"]
        rows, grows, act, gpre, gup = [v.reshape(-1, v.shape[-1]) for v in kept]
        exgate_grad = dot_tn(gpre, rows)
        exup_grad = dot_tn(gup, rows)
        exdown_grad = dot_tn(act, grows)
    else:
        phase = Phase(cots[1], row_planes[1])
        made = run_feed(0, 1, row_core[0].held, cot_core[0].held, None, row_core[0].held[0])
        made = phase.end(*made)
        other = core_send("feed_other", made)
        phase = Phase(cots[1])
        Phase(other).end()
        late = Phase(row_planes[1])
        made0 = run_feed(0, 0, row_planes[0].held, cots[0].held, other.held, other.held[0])
        made0 = phase.end(*made0)
        made0 = late.end(*made0)
        run(cots[1], row_planes[1])
        cot_core[1] = core_send("cotangents", cots[1].held)
        row_core[1] = core_send("ffn_rows", row_planes[1].held)
        grads = [collect("ffn_grads", made0[4:]), None]
        phase = Phase(grads[0])
        Phase(cot_core[1], row_core[1]).end()
        made = run_feed(1, 1, row_core[1].held, cot_core[1].held, None, row_core[1].held[0])
        made = phase.end(*made)
        other = core_send("feed_other", made)
        outs = [collect("outputs", made0[:4]), None]
        phase = Phase(grads[0])
        Phase(other).end()
        out_phase = Phase(outs[0])
        made1 = run_feed(1, 0, row_planes[1].held, cots[1].held, other.held, other.held[0])
        made1 = phase.end(*made1)
        run(grads[0])
        grad_line = [lines_of("ffn_grads", grads[0]), None]
        grads[1] = collect("ffn_grads", made1[4:])
        phase = Phase(grad_line[0], grads[1])
        kept = state["kept"]
        rows, grows, act, gpre, gup = [v.reshape(-1, v.shape[-1]) for v in kept]
        exgate_grad = dot_tn(after(gpre, made1[0]), rows)
        exgate_grad, gup = phase.end(exgate_grad, gup)
        phase = Phase(grad_line[0], grads[1])
        exup_grad = dot_tn(gup, rows)
        exup_grad, act = phase.end(exup_grad, act)
        run(grads[1], grad_line[0])
        grad_line[1] = lines_of("ffn_grads", grads[1])
        (grows,) = out_phase.end(grows)
        phase = Phase(grad_line[1], outs[0])
        exdown_grad = dot_tn(act, grows)
        (exdown_grad,) = phase.end(exdown_grad)
        run(grad_line[1])
        grad_ffn = [flow.held for flow in grad_line]
        outs[1] = collect("outputs", made1[:4])
    exgate_grad = jnp.transpose(exgate_grad)[None]
    exup_grad = jnp.transpose(exup_grad)[None]
    exdown_grad = exdown_grad[None]
    dsgut, dsd = state["dsgut"], state["dsd"]

    ffn_hat, ffn_inverse = jnp.stack(ffn_hat), jnp.stack(ffn_inverse)
    grad_two, ffngain_term = norm_back(jnp.stack(grad_ffn), ffn_hat, ffn_inverse, gain_ffn)
    grad_residual = cotangent.astype(F32) + grad_two
    grad_attention = grad_residual.astype(BF16)
    shared_term = jnp.concatenate([dsgut.reshape(2, hidden_pad, width), dsd[None]], axis=0)
    shared_term = shared_term[:, :hidden_each].astype(BF16)
    shared_term = jnp.transpose(
        shared_term.reshape(3, hidden_each, lines, 2, shard), (2, 3, 0, 1, 4)
    )

    gres_flow = Plane("attention_grads", grad_attention[0], grad_attention[1])
    if serial:
        run(gres_flow)
    else:
        Phase(gres_flow).end()
        run(outs[0])
        out_line = [lines_of("outputs", outs[0]), None]
        Phase(gres_flow, out_line[0]).end()
        run(gres_flow)
    gres = gres_flow.held
    token = gres[0]
    if not serial:
        shared_sent = Sends(
            "shared_grads",
            [pick(shared_term, line ^ k) for k in range(1, lines)],
            "seq",
            [2 * k for k in range(1, lines)],
        )
        window = Phase(outs[1], shared_sent)

    per_batch = [(*gres[2 * b : 2 * b + 2], *keys[b], *saved[b]) for b in range(batches)]
    groups = [[b] for b in range(batches)] if serial else [list(range(batches))]
    calls = [
        attend_back(
            pack, here, marks, [orders[b] for b in g], cos_b, sin_b, first_weights, out_weights,
            [per_batch[b] for b in g], token,
        )
        for g in groups
    ]
    if serial:
        gparts = [v for c in calls for v in c[0]]
        gkeys = [jnp.concatenate(v, axis=1) for v in zip(*[c[1] for c in calls])]
        dweights = [
            sum(v.astype(F32) for v in t).astype(BF16) for t in zip(*[c[2] for c in calls])
        ]
        shared_sent = Sends(
            "shared_grads",
            [pick(shared_term, line ^ k) for k in range(1, lines)],
            "seq",
            [2 * k for k in range(1, lines)],
        )
        run(shared_sent)
    else:
        made = window.end(*[v for group_of in calls[0] for v in group_of])
        gparts, gkeys, dweights = made[: 2 * batches], made[-4:-2], made[-2:]
    weight_core = core_send("weight_grads", [dweights[1]])
    key_core = core_send("key_grads", [gkeys[1]])
    late = None if serial else outs[1]
    gkey, dweight_own = Phase(key_core, weight_core).end(gkeys[0], dweights[0])
    both = [
        (
            gkey[:, :, r * each : (r + 1) * each].astype(F32)
            + key_core.held[0][:, :, r * each : (r + 1) * each].astype(F32)
        ).astype(BF16)
        for r in range(head_count)
    ]
    key_plane = head_send("key_grads", both[1:])
    weight_both = (dweight_own.astype(F32) + weight_core.held[0].astype(F32)).astype(BF16)
    weight_line = LineSum("weight_grads", weight_both)
    ends = [both[0], *gparts]
    if late is not None and late.more:
        ends += [v for pair in late.held for v in pair]
    both0, *ends = Phase(key_plane, weight_line).end(*ends)
    gparts = ends[: 2 * batches]
    if late is not None and late.more:
        late.held = [ends[-4:-2], ends[-2:]]
    total = both0.astype(F32)
    for value in key_plane.held:
        total = total + value.astype(F32)
    key_line = LineSum("key_grads", total.astype(BF16))
    normed_sum = PlaneSum("normed_grads", gparts[:2], gparts[2:])
    Phase(key_line, normed_sum, late).end()
    while key_line.more:
        Phase(key_line, normed_sum, None if serial else out_line[0]).end()
    run(normed_sum)
    own_tiled = [jnp.tile(t, (batches, 1)) for t in (own_cos, own_sin)]
    grad_latent, latgain_term = key_back(
        key_line.held.reshape(batches * each, WIDE), own_latent, gain_lat, *own_tiled
    )
    latent_send = head_send(
        "latent_grads", [grad_latent.reshape(batches, each, WIDE)] * (head_count - 1)
    )
    if serial:
        run(latent_send)
    else:
        run(outs[1])
        out_line[1] = lines_of("outputs", outs[1])
        Phase(latent_send).end()
    weights_phase = Phase(weight_line)
    inputs_grad, attngain_term = inputs_back(
        *normed_sum.held, grad_latent, latent_t, inputs.reshape(batches * each, width),
        gain_attn, grad_residual.reshape(batches * each, width),
    )
    inputs_grad = inputs_grad.reshape(batches, each, width)

    share = (RANK + RDIM) // head_count
    latent_own, latent_other = latent_back(
        here,
        [grad_latent.reshape(batches, each, WIDE)] + latent_send.held,
        [kept_b[0] for kept_b in saved],
        (attngain_term, ffngain_term.reshape(1, width), latgain_term),
        lines,
        share,
    )
    latent_core = core_send("latent_grads", [latent_other])
    shared_held = jnp.stack([pick(shared_term, line)] + shared_sent.held)
    shared_core = core_send("shared_grads", [pick(shared_held, core ^ 1, 1)])
    (latent_own,) = Phase(latent_core, shared_core).end(latent_own)
    (latent_own,) = weights_phase.end(latent_own)
    both = (latent_own.astype(F32) + latent_core.held[0].astype(F32)).astype(BF16)
    latent_line = LineSum("latent_grads", both)
    Phase(latent_line, None if serial else out_line[1]).end()
    (latent_mine,) = run(latent_line)
    latent_mine = latent_mine.astype(BF16)
    latent_last = head_send("latent_grads", [latent_mine] * (head_count - 1))
    (latent_mine,) = Phase(latent_last).end(latent_mine)
    if serial:
        run(weight_line)
    else:
        run(weight_line, out_line[0], out_line[1])
    latent_parts = [latent_mine] + latent_last.held
    dweight = weight_line.held
    query_grad = jnp.concatenate(
        [dweight[i * shard : (i + 1) * shard] for i in range(pack.query_parts)], axis=1
    )
    nope = heads * HDIM
    query_grad = jnp.concatenate(
        [
            query_grad[:, :nope].reshape(-1, heads, HDIM),
            query_grad[:, nope : nope + heads * HALF].reshape(-1, heads, HALF),
            query_grad[:, nope + heads * HALF :].reshape(-1, heads, HALF),
        ],
        axis=-1,
    ).reshape(-1, heads * QDIM)
    expand_grad = jnp.concatenate(
        [
            dweight[pack.expand_at + i * pack.rank : pack.expand_at + (i + 1) * pack.rank]
            for i in range(pack.expand_parts)
        ],
        axis=1,
    )
    outproj_grad = dweight[pack.out_at :]

    latent_grad = jnp.zeros((head_count, share, shard), BF16)
    gain_grad = 0.0
    for k in range(head_count):
        latent_grad = lax.dynamic_update_slice_in_dim(
            latent_grad, latent_parts[k][None, :share], head_index ^ k, 0
        )
        gain_grad = gain_grad + latent_parts[k][share:].astype(F32)
    latent_grad = jnp.transpose(latent_grad.reshape(RANK + RDIM, shard)).astype(F32)
    attngain_grad = gain_grad[0]
    ffngain_grad = gain_grad[1]
    lat_grads = gain_grad[2 : 2 + RANK // shard].reshape(RANK)
    latgain_grad = lax.dynamic_slice_in_dim(lat_grads, seq_index * n_lat, n_lat)

    kept, came = pick(shared_held, core, 1), shared_core.held[0]
    paired = jnp.where(core == 0, jnp.stack([kept, came], 1), jnp.stack([came, kept], 1))
    shared_grad = jnp.zeros(paired.shape, BF16)
    for k in range(lines):
        shared_grad = lax.dynamic_update_slice_in_dim(shared_grad, paired[k : k + 1], line ^ k, 0)
    shared_grad = jnp.transpose(shared_grad, (2, 0, 1, 3, 4)).reshape(3, -1, shard).astype(F32)
    shgate_grad = jnp.transpose(shared_grad[0])
    shup_grad = jnp.transpose(shared_grad[1])
    shdown_grad = shared_grad[2]

    if not serial:
        outs = [flow.held for flow in out_line]
    output = (jnp.stack(residual) + jnp.stack(outs)).astype(BF16)

    return (
        output,
        inputs_grad,
        query_grad,
        latent_grad,
        expand_grad,
        outproj_grad,
        shgate_grad,
        shup_grad,
        shdown_grad,
        exgate_grad,
        exup_grad,
        exdown_grad,
        attngain_grad,
        latgain_grad,
        ffngain_grad,
    )


def solution(mesh):
    own = P(None, ("seq", "head"), None)
    stack = P(("seq", "head"), None, None)
    return jax.shard_map(
        local,
        mesh=mesh,
        in_specs=(
            own,
            own,
            P(None, "seq", None),
            P(None, "seq", None),
            P("seq"),
            P("seq"),
            P("seq"),
            P("seq", "head"),
            P("seq", None),
            P("seq", "head"),
            P("head", "seq"),
            P("seq", "head"),
            P("seq", "head"),
            P("head", "seq"),
            stack,
            stack,
            stack,
        ),
        out_specs=(
            own,
            own,
            P("seq", "head"),
            P("seq", None),
            P("seq", "head"),
            P("head", "seq"),
            P("seq", "head"),
            P("seq", "head"),
            P("head", "seq"),
            stack,
            stack,
            stack,
            P("seq"),
            P("seq"),
            P("seq"),
        ),
        check_vma=False,
    )
```

```python
import functools

import jax
import jax.numpy as jnp
from jax import lax
from jax.experimental import pallas as pl
from jax.experimental.pallas import tpu as pltpu
from jax.sharding import PartitionSpec as P

HDIM = 128
RDIM = 64
RANK = 512
TOPK = 6
BLOCK = 256
QDIM = 192
HALF = RDIM // 2
EPSILON = 1e-06
ROPE_BASE = 10000.0
NEG_LARGE = -1e30
LOG2E = 1.4426950408889634
SCALE = QDIM ** (-0.5)
WIDE = -(-(RANK + RDIM) // 128) * 128
F32 = jnp.float32
BF16 = jnp.bfloat16
MIB = 1024 * 1024


def dot(a, b):
    return lax.dot_general(a, b, (((1,), (0,)), ((), ())), preferred_element_type=F32)


def dot_nt(a, b):
    return lax.dot_general(a, b, (((1,), (1,)), ((), ())), preferred_element_type=F32)


def dot_tn(a, b):
    return lax.dot_general(a, b, (((0,), (0,)), ((), ())), preferred_element_type=F32)


def rms_inverse(values):
    return lax.rsqrt(jnp.mean(values * values, axis=-1, keepdims=True) + EPSILON)


def rope_tables(positions):
    frequency = ROPE_BASE ** (-jnp.arange(HALF, dtype=F32) / HALF)
    angles = positions.astype(F32)[:, None] * frequency[None, :]
    return (jnp.cos(angles), jnp.sin(angles))


def norm_back(grad_normed, hat_rows, inverse, gain_vec):
    scaled = grad_normed * gain_vec
    gain_term = jnp.sum(grad_normed * hat_rows, axis=(0, 1))
    grad_rows = inverse * (scaled - hat_rows * jnp.mean(scaled * hat_rows, axis=-1, keepdims=True))
    return (grad_rows, gain_term)


def swap(value, axis, mask):
    size = lax.axis_size(axis)
    return lax.ppermute(value, axis, [(i, i ^ mask) for i in range(size)])


def depth():
    return lax.axis_size("seq") // 2


def line_pieces(value):
    return [value] + [swap(value, "seq", 2 * k) for k in range(1, depth())]


def plane_pieces(value):
    return [value] + [swap(value, "head", r) for r in range(1, lax.axis_size("head"))]


def core_pieces(values):
    return values, [swap(v, "seq", 1) for v in values]


def line_sum(values):
    total = values[0].astype(F32)
    for k in range(1, depth()):
        total = total + swap(values[k], "seq", 2 * k).astype(F32)
    return total


def plane_sum(values):
    total = values[0].astype(F32)
    for r in range(1, lax.axis_size("head")):
        total = total + swap(values[r], "head", r).astype(F32)
    return total


def pick(value, index, axis=0):
    return lax.dynamic_index_in_dim(value, index, axis, keepdims=False)


def any_spec():
    return [pl.BlockSpec(memory_space=pl.ANY)]


def after(value, *others):
    return pl.pallas_call(
        lambda *refs: None,
        out_shape=jax.ShapeDtypeStruct(value.shape, value.dtype),
        in_specs=any_spec() * (1 + len(others)),
        out_specs=any_spec()[0],
        input_output_aliases={0: 0},
        name="after",
    )(value, *others)


def sync(*values):
    return pl.pallas_call(
        lambda *refs: None,
        out_shape=tuple(jax.ShapeDtypeStruct(v.shape, v.dtype) for v in values),
        in_specs=any_spec() * len(values),
        out_specs=tuple(any_spec() * len(values)),
        input_output_aliases={i: i for i in range(len(values))},
        name="sync",
    )(*values)


def bits_of(size):
    return [1 << i for i in range(size.bit_length() - 1)]


def plane_order(flip):
    bits = bits_of(lax.axis_size("head"))
    order = [0]
    for bit in bits[::-1] if flip else bits:
        order = order + [i | bit for i in order]
    return order


class Spread:
    def __init__(self, name, value):
        self.name, self.held, self.rest = name, value[None], self.plan()

    def send(self):
        with jax.named_scope(self.name):
            self.got = swap(self.held, self.axis, self.rest[0])
        return [self.got]

    def take(self, got):
        self.rest = self.rest[1:]
        with jax.named_scope(self.name):
            self.held = self.join(self.held, got[0])
        return self

    @property
    def more(self):
        return bool(self.rest)


class Line(Spread):
    axis = "seq"

    def plan(self):
        return [2 * bit for bit in bits_of(depth())[::-1]]

    def join(self, held, got):
        return jnp.stack([held, got], axis=1).reshape((-1,) + held.shape[1:])


class Plane:
    def __init__(self, name, first, second, hold=False):
        self.name, self.held, self.hold = name, [first[None], second[None]], hold
        self.rest = bits_of(lax.axis_size("head"))

    def send(self):
        count = len(self.rest)
        with jax.named_scope(self.name):
            masks = (self.rest[0], bits_of(lax.axis_size("head"))[count - 1])
            return [swap(v, "head", m) for v, m in zip(self.held, masks)]

    def take(self, got):
        self.rest = self.rest[1:]
        if not self.rest:
            self.held = [v for pair in zip(self.held, got) for v in pair]
            return self
        with jax.named_scope(self.name):
            self.held = [jnp.concatenate([v, g], axis=0) for v, g in zip(self.held, got)]
        return self

    @property
    def more(self):
        return bool(self.rest)


def add_halves(first, second):
    half = first.shape[0] // 2
    return [
        (first[i].astype(F32) + second[i].astype(F32)).astype(BF16)
        for i in (slice(0, half), slice(half, None))
    ]


class PlaneSum:
    def __init__(self, name, *halves):
        self.name, self.held, self.left = name, halves, len(bits_of(lax.axis_size("head")))

    def send(self):
        bits = bits_of(lax.axis_size("head"))
        masks = (bits[self.left - 1], bits[len(bits) - self.left])
        with jax.named_scope(self.name):
            return [swap(sent, "head", m) for (_, sent), m in zip(self.held, masks)]

    def take(self, got):
        self.left -= 1
        with jax.named_scope(self.name):
            if self.left:
                self.held = [add_halves(kept, g) for (kept, _), g in zip(self.held, got)]
            else:
                self.held = [
                    (kept.astype(F32) + g.astype(F32)).astype(BF16)[0]
                    for (kept, _), g in zip(self.held, got)
                ]
        return self

    @property
    def more(self):
        return self.left > 0


class LineSum:
    def __init__(self, name, value):
        self.name, self.held, self.rest = name, value, bits_of(depth())

    def send(self):
        pairs = self.held.reshape((-1, 2) + self.held.shape[1:])
        self.kept = pairs[:, 0]
        with jax.named_scope(self.name):
            return [swap(pairs[:, 1], "seq", 2 * self.rest[0])]

    def take(self, got):
        self.rest = self.rest[1:]
        with jax.named_scope(self.name):
            self.held = self.kept.astype(F32) + got[0].astype(F32)
            if self.rest:
                self.held = self.held.astype(BF16)
            else:
                self.held = self.held[0]
        return self

    @property
    def more(self):
        return bool(self.rest)


class Sends:
    def __init__(self, name, values, axis, masks):
        self.name, self.values, self.axis, self.masks = name, values, axis, masks
        self.more = True

    def send(self):
        with jax.named_scope(self.name):
            return [swap(v, self.axis, m) for v, m in zip(self.values, self.masks)]

    def take(self, got):
        self.more = False
        self.held = list(got)
        return self


def core_send(name, values):
    return Sends(name, values, "seq", [1] * len(values))


def head_send(name, values):
    return Sends(name, values, "head", list(range(1, lax.axis_size("head"))))


class Phase:
    def __init__(self, *flows):
        self.flows = [flow for flow in flows if flow is not None and flow.more]
        self.sent = [flow.send() for flow in self.flows]

    def end(self, *others):
        planes = [f for f in self.flows if isinstance(f, Plane) and f.hold and len(f.rest) == 1]
        flat = [v for got in self.sent for v in got]
        flat += [v for flow in planes for v in flow.held] + list(others)
        flat = list(sync(*flat))
        sent = [[flat.pop(0) for _ in got] for got in self.sent]
        for flow in planes:
            flow.held = [flat.pop(0) for _ in flow.held]
        for flow, got in zip(self.flows, sent):
            flow.take(got)
        return flat


def run(*flows):
    while any(flow.more for flow in flows):
        Phase(*flows).end()
    return [flow.held for flow in flows]


def take(refs, count):
    return [refs.pop(0) for _ in range(count)]


def part_places(here, own, other, size):
    return [
        ((ref, line), pl.multiple_of((here ^ (2 * line + core)) * size, size))
        for core, ref in enumerate((own, other))
        for line in range(ref.shape[0])
    ]


class Pack:
    def __init__(self, size, heads, seq_count):
        self.size, self.rank = size, RANK // seq_count
        self.query_parts = heads * QDIM // size
        self.expand_parts = 2 * heads * HDIM // size
        self.expand_at = self.query_parts * size
        self.out_at = self.expand_at + self.expand_parts * self.rank
        self.out_rows = heads * HDIM
        self.rows = self.out_at + self.out_rows

    def query(self, ref, part):
        array, line = ref
        return array[line, part * self.size : (part + 1) * self.size, :]

    def expand(self, ref, part):
        array, line = ref
        at = part * self.rank
        return array[line, at : at + self.rank, :]

    def out(self, ref):
        array, line = ref
        return array[line, : self.out_rows, :]


def latent_kernel(plane, s_ref, x_ref, cos, sin, *refs):
    refs = list(refs)
    own, other = take(refs, plane), take(refs, plane)
    keys_out, lat_out, gattn_out, gffn_out, glat_out, wide_out, full = refs
    here, column = s_ref[0], s_ref[1]
    rows = RANK + RDIM
    lines, each, size = own[0].shape
    for core, group in enumerate((own, other)):
        for line in range(lines):
            place = pl.multiple_of((here ^ (2 * line + core)) * size, size)
            for r, ref in enumerate(group):
                top = pl.multiple_of((column ^ r) * each, 16)
                full[pl.ds(top, each), pl.ds(place, size)] = ref[line]
    x = x_ref[...].astype(F32)
    gains = full[rows : rows + 16, :].astype(F32)
    gattn_out[...] = gains[0:1]
    gffn_out[...] = gains[1:2]
    spread = gains[2 : 2 + RANK // size]
    glat = spread[:, :size]
    for i in range(1, 2 * lines):
        glat = glat + spread[:, i * size : (i + 1) * size]
    glat = jnp.concatenate([glat[i : i + 1] for i in range(RANK // size)], axis=1)
    glat_out[...] = glat
    normed = (x * rms_inverse(x) * gains[0:1]).astype(BF16)
    wide_out[...] = full[:rows, :]
    low = dot_nt(normed, wide_out[...]).astype(BF16)
    lat_out[...] = low
    low = low.astype(F32)
    comp = low[:, :RANK]
    comp = comp * rms_inverse(comp) * glat
    first, second = low[:, RANK : RANK + HALF], low[:, RANK + HALF :]
    keys_out[...] = jnp.concatenate(
        [
            comp,
            first * cos[...] - second * sin[...],
            first * sin[...] + second * cos[...],
            jnp.zeros((x.shape[0], WIDE - RANK - RDIM), F32),
        ],
        axis=1,
    ).astype(BF16)


def block_scores(query, keys, masks):
    scores = dot_nt(query, keys)
    if masks is not None:
        scores = jnp.where(masks, scores, NEG_LARGE)
    return scores


def entry(pair, order, r):
    half, j = divmod(order.index(r), len(order) // 2)
    return pair[half], j


def load_keys(pair, order, line):
    found = [entry(pair, order, r) for r in range(len(order))]
    return jnp.concatenate([ref[j, line] for ref, j in found], axis=0)


def fill_expand(here, own, other, wexp, pack):
    for ref, place in part_places(here, own, other, pack.rank):
        for part in range(pack.expand_parts):
            columns = slice(part * pack.size, (part + 1) * pack.size)
            wexp[pl.ds(place, pack.rank), columns] = pack.expand(ref, part)


def attend_masked(here, heads, order, lines, key_refs, wexp, q_out, state, qblk_ref, kblk_ref):
    acc, mx, sm = state
    group = q_out.shape[1]
    for core, ref in enumerate(key_refs):

        def step(line, carry, core=core, ref=ref):
            @pl.when((here ^ (2 * line + core)) <= here)
            def _():
                latent = load_keys(ref, order, line)
                expanded = dot(latent[:, :RANK], wexp[...]).astype(BF16)
                rope_key = latent[:, RANK : RANK + RDIM]
                allowed = kblk_ref[pl.ds(2 * line + core, 1), :] <= qblk_ref[...]
                for h in range(heads):
                    keys = jnp.concatenate(
                        [expanded[:, 2 * h * HDIM : (2 * h + 1) * HDIM], rope_key], axis=1
                    )
                    vals = expanded[:, (2 * h + 1) * HDIM : (2 * h + 2) * HDIM]
                    scores = block_scores(q_out[h], keys, allowed)
                    old = mx[h][:, :1]
                    new = jnp.maximum(old, jnp.max(scores, axis=1, keepdims=True))
                    weights = jnp.exp2((scores - new) * (SCALE * LOG2E))
                    weights = jnp.where(allowed, weights, 0.0)
                    rescale = jnp.exp2((old - new) * (SCALE * LOG2E))
                    sm[h] = sm[h] * rescale + jnp.sum(weights, axis=1, keepdims=True)
                    acc[h] = acc[h] * rescale + dot(weights.astype(BF16), vals)
                    mx[h] = jnp.broadcast_to(new, (group, HDIM))

            return carry

        lax.fori_loop(0, lines, step, 0)


def attend_whole(here, heads, order, lines, key_refs, wexp, q_out, state, all_scores, all_vals):
    acc, mx, sm = state
    wide = mx.shape[2]

    def each_block(body):
        for core, ref in enumerate(key_refs):

            def step(line, carry, core=core, ref=ref):
                @pl.when((here ^ (2 * line + core)) <= here)
                def _():
                    body(2 * line + core, ref, line)

                return carry

            lax.fori_loop(0, lines, step, 0)

    def score(place, ref, line):
        latent = load_keys(ref, order, line)
        expanded = dot(latent[:, :RANK], wexp[...]).astype(BF16)
        rope_key = latent[:, RANK : RANK + RDIM]
        for h in range(heads):
            keys = jnp.concatenate(
                [expanded[:, 2 * h * HDIM : (2 * h + 1) * HDIM], rope_key], axis=1
            )
            all_vals[place, :, h * HDIM : (h + 1) * HDIM] = expanded[
                :, (2 * h + 1) * HDIM : (2 * h + 2) * HDIM
            ]
            scores = dot_nt(q_out[h], keys)
            all_scores[h, place] = scores
            top = mx[h]
            for i in range(scores.shape[1] // wide):
                top = jnp.maximum(top, scores[:, i * wide : (i + 1) * wide])
            mx[h] = top

    each_block(score)
    for h in range(heads):
        mx[h] = jnp.broadcast_to(jnp.max(mx[h], axis=1, keepdims=True), mx.shape[1:])

    def weigh(place, ref, line):
        for h in range(heads):
            weights = jnp.exp2((all_scores[h, place] - mx[h][:, :1]) * (SCALE * LOG2E))
            total = sm[h]
            for i in range(weights.shape[1] // wide):
                total = total + weights[:, i * wide : (i + 1) * wide]
            sm[h] = total
            vals = all_vals[place, :, h * HDIM : (h + 1) * HDIM]
            acc[h] = acc[h] + dot(weights.astype(BF16), vals)

    each_block(weigh)
    for h in range(heads):
        sm[h] = jnp.broadcast_to(jnp.sum(sm[h], axis=1, keepdims=True), sm.shape[1:])


def attend_kernel(pack, heads, masked, order, tokens, *refs):
    refs = list(refs)
    (s_ref,) = take(refs, 1)
    qblk_ref, kblk_ref = take(refs, 2) if masked else (None, None)
    x, own, other = take(refs, 2), take(refs, 2), take(refs, 2)
    gain, cos, sin, w_own, w_other, e_own, e_other = take(refs, 7)
    take(refs, tokens)
    lines = own[0].shape[1]
    normed_out, q_out, att_out, lse_out = take(refs, 4)
    acc, mx, sm, wexp, *kept = refs
    group = normed_out.shape[0]
    nope = heads * HDIM
    wide = heads * HALF
    size = pack.size
    here = s_ref[0]
    fill_expand(here, e_own, e_other, wexp, pack)
    found = [entry(x, order, r) for r in range(len(order))]
    rows = jnp.concatenate([ref[j] for ref, j in found], axis=0).astype(F32)
    normed_out[...] = (rows * rms_inverse(rows) * gain[...]).astype(BF16)
    qlin = [jnp.zeros((group, size), F32) for _ in range(pack.query_parts)]
    for ref, place in part_places(here, w_own, w_other, size):
        block = normed_out[:, pl.ds(place, size)]
        qlin = [q + dot(block, pack.query(ref, part)) for part, q in enumerate(qlin)]
    qlin = jnp.concatenate(qlin, axis=1)
    first = qlin[:, nope : nope + wide]
    second = qlin[:, nope + wide :]
    turned_a = first * cos[...] - second * sin[...]
    turned_b = first * sin[...] + second * cos[...]
    for h in range(heads):
        q_out[h] = jnp.concatenate(
            [
                qlin[:, h * HDIM : (h + 1) * HDIM],
                turned_a[:, h * HALF : (h + 1) * HALF],
                turned_b[:, h * HALF : (h + 1) * HALF],
            ],
            axis=1,
        ).astype(BF16)
    acc[...] = jnp.zeros_like(acc)
    mx[...] = jnp.full_like(mx, NEG_LARGE)
    sm[...] = jnp.zeros_like(sm)
    if masked:
        attend_masked(
            here, heads, order, lines, (own, other), wexp, q_out, (acc, mx, sm), qblk_ref, kblk_ref
        )
    else:
        attend_whole(here, heads, order, lines, (own, other), wexp, q_out, (acc, mx, sm), *kept)
    for h in range(heads):
        att_out[:, h * HDIM : (h + 1) * HDIM] = (acc[h] / sm[h]).astype(BF16)
        lse_out[h] = mx[h] * (SCALE * LOG2E) + jnp.log2(sm[h])


def out_kernel(pack, tokens, *refs):
    refs = list(refs)
    s_ref, att, w_own, w_other = take(refs, 4)
    take(refs, tokens)
    each = refs[0].shape[0]
    for ref, place in part_places(s_ref[0], w_own, w_other, pack.size):
        block = dot(att[...], pack.out(ref)).astype(BF16)
        for r, out in enumerate(refs):
            out[:, pl.ds(place, pack.size)] = block[r * each : (r + 1) * each]


def project(pack, here, att, weights, plane, tokens):
    width = 2 * weights[0].shape[0] * pack.size
    return pl.pallas_call(
        functools.partial(out_kernel, pack, len(tokens)),
        out_shape=tuple(
            [jax.ShapeDtypeStruct((att.shape[0] // plane, width), BF16)] * plane
        ),
        in_specs=smem_spec() + vmem_specs(3) + any_spec() * len(tokens),
        out_specs=tuple(vmem_specs(plane)),
        compiler_params=pltpu.CompilerParams(vmem_limit_bytes=40 * MIB),
        cost_estimate=pl.CostEstimate(
            flops=1_000_000_000, bytes_accessed=5_000_000, transcendentals=0
        ),
        name="project",
    )(here, att, *weights, *tokens)


def attend_back_kernel(pack, heads, masked, orders, *refs):
    refs = list(refs)
    (s_ref,) = take(refs, 1)
    qblk_ref, kblk_ref = take(refs, 2) if masked else (None, None)
    cos, sin, w_own, w_other, e_own, e_other, o_own, o_other = take(refs, 8)
    per_batch = [
        (take(refs, 2), take(refs, 2), take(refs, 2), *take(refs, 4)) for _ in orders
    ]
    take(refs, 1)
    batches, plane = len(orders), len(orders[0])
    lines = w_own.shape[0]
    gpart_outs = [take(refs, 2) for _ in orders]
    own_out, other_out, dw_own, dw_other = take(refs, 4)
    gq_acc, gqlin, gatt, wexp, dwexp, dwq, dwo = refs
    group = gqlin.shape[0]
    each = group // plane
    nope = heads * HDIM
    wide = heads * HALF
    size = pack.size
    here = s_ref[0]
    fill_expand(here, e_own, e_other, wexp, pack)
    dwexp[...] = jnp.zeros_like(dwexp)
    places = part_places(here, w_own, w_other, size)
    for b, order in enumerate(orders):
        gres, own, other, normed, q_ref, att, lse = per_batch[b]
        total = jnp.zeros((group, nope), F32)
        for i, (ref, place) in enumerate(part_places(here, o_own, o_other, size)):
            found = [entry(gres, order, r) for r in range(plane)]
            block = jnp.concatenate([g[j, :, pl.ds(place, size)] for g, j in found], axis=0)
            total = total + dot_nt(block, pack.out(ref))
            term = dot_tn(att[...], block)
            dwo[i] = term if b == 0 else dwo[i] + term
        gatt[...] = total.astype(BF16)
        gq_acc[...] = jnp.zeros_like(gq_acc)
        deltas = [
            jnp.sum(
                gatt[:, h * HDIM : (h + 1) * HDIM].astype(F32)
                * att[:, h * HDIM : (h + 1) * HDIM].astype(F32),
                axis=1,
                keepdims=True,
            )
            for h in range(heads)
        ]
        for core, (ref, out) in enumerate(((own, own_out), (other, other_out))):

            def step(
                line, carry, core=core, key_ref=ref, out=out, b=b, q_ref=q_ref, lse=lse,
                deltas=deltas, order=order,
            ):
                live = (here ^ (2 * line + core)) <= here

                @pl.when(jnp.logical_not(live))
                def _():
                    out[line, b] = jnp.zeros((group, WIDE), BF16)

                @pl.when(live)
                def _():
                    latent = load_keys(key_ref, order, line)
                    expanded = dot(latent[:, :RANK], wexp[...]).astype(BF16)
                    rope_key = latent[:, RANK : RANK + RDIM]
                    allowed = None
                    if masked:
                        allowed = kblk_ref[pl.ds(2 * line + core, 1), :] <= qblk_ref[...]
                    grads = []
                    grad_rope = jnp.zeros((group, RDIM), F32)
                    for h in range(heads):
                        keys = jnp.concatenate(
                            [expanded[:, 2 * h * HDIM : (2 * h + 1) * HDIM], rope_key], axis=1
                        )
                        vals = expanded[:, (2 * h + 1) * HDIM : (2 * h + 2) * HDIM]
                        query = q_ref[h]
                        gout = gatt[:, h * HDIM : (h + 1) * HDIM]
                        scores = block_scores(query, keys, allowed)
                        probs = jnp.exp2(scores * (SCALE * LOG2E) - lse[h][:, :1])
                        if masked:
                            probs = jnp.where(allowed, probs, 0.0)
                        gprobs = dot_nt(gout, vals)
                        gscores = (probs * (gprobs - deltas[h])).astype(BF16)
                        gq_acc[h] = gq_acc[h] + dot(gscores, keys)
                        gkeys = dot_tn(gscores, query) * SCALE
                        gvals = dot_tn(probs.astype(BF16), gout)
                        grads.append(gkeys[:, :HDIM].astype(BF16))
                        grads.append(gvals.astype(BF16))
                        grad_rope = grad_rope + gkeys[:, HDIM:]
                    gexp = jnp.concatenate(grads, axis=1)
                    dwexp[...] = dwexp[...] + dot_tn(latent[:, :RANK], gexp)
                    gcomp = dot_nt(gexp, wexp[...])
                    blank = jnp.zeros((group, WIDE - RANK - RDIM), F32)
                    out[line, b] = jnp.concatenate([gcomp, grad_rope, blank], axis=1).astype(BF16)

                return carry

            lax.fori_loop(0, lines, step, 0)
        firsts, seconds = [], []
        for h in range(heads):
            value = gq_acc[h] * SCALE
            gqlin[:, h * HDIM : (h + 1) * HDIM] = value[:, :HDIM].astype(BF16)
            firsts.append(value[:, HDIM : HDIM + HALF])
            seconds.append(value[:, HDIM + HALF :])
        first = jnp.concatenate(firsts, axis=1)
        second = jnp.concatenate(seconds, axis=1)
        gqlin[:, nope : nope + wide] = (first * cos[...] + second * sin[...]).astype(BF16)
        gqlin[:, nope + wide :] = (second * cos[...] - first * sin[...]).astype(BF16)
        for i, (ref, place) in enumerate(places):
            weight = jnp.concatenate(
                [pack.query(ref, part) for part in range(pack.query_parts)], axis=1
            )
            block = dot_nt(gqlin[...], weight).astype(BF16)
            for r in range(plane):
                half, j = divmod(order.index(r), plane // 2)
                gpart_outs[b][half][j, :, pl.ds(place, size)] = block[r * each : (r + 1) * each]
            term = dot_tn(normed[:, pl.ds(place, size)], gqlin[...])
            dwq[i] = term if b == 0 else dwq[i] + term
    for core, out in enumerate((dw_own, dw_other)):
        for line in range(lines):
            i = core * lines + line
            term = dwq[i].astype(BF16)
            for part in range(pack.query_parts):
                out[line, part * size : (part + 1) * size] = term[
                    :, part * size : (part + 1) * size
                ]
            place = pl.multiple_of((here ^ (2 * line + core)) * pack.rank, pack.rank)
            term = dwexp[pl.ds(place, pack.rank), :].astype(BF16)
            for part in range(pack.expand_parts):
                at = pack.expand_at + part * pack.rank
                out[line, at : at + pack.rank] = term[:, part * size : (part + 1) * size]
            out[line, pack.out_at : pack.rows] = dwo[i].astype(BF16)


def vmem_specs(count):
    return [pl.BlockSpec(memory_space=pltpu.VMEM)] * count


def smem_spec():
    return [pl.BlockSpec(memory_space=pltpu.SMEM)]


def own_latents(place, x, cos, sin, own, other):
    rows, width = x.shape
    total = len(own) * own[0].shape[1]
    return pl.pallas_call(
        functools.partial(latent_kernel, len(own)),
        out_shape=(
            jax.ShapeDtypeStruct((rows, WIDE), BF16),
            jax.ShapeDtypeStruct((rows, RANK + RDIM), BF16),
            jax.ShapeDtypeStruct((1, width), F32),
            jax.ShapeDtypeStruct((1, width), F32),
            jax.ShapeDtypeStruct((1, RANK), F32),
            jax.ShapeDtypeStruct((RANK + RDIM, width), BF16),
        ),
        in_specs=smem_spec() + vmem_specs(3 + len(own) + len(other)),
        out_specs=tuple(vmem_specs(6)),
        scratch_shapes=[pltpu.VMEM((total, width), BF16)],
        compiler_params=pltpu.CompilerParams(vmem_limit_bytes=40 * MIB),
        cost_estimate=pl.CostEstimate(
            flops=1_000_000_000, bytes_accessed=6_000_000, transcendentals=1_000
        ),
        name="own_latents",
    )(place, x, cos, sin, *own, *other)


def whole(value):
    rank = len(value.shape)
    return pl.BlockSpec(value.shape, lambda i: (0,) * rank)


def attend(pack, here, marks, order, x, gain, cos, sin, keys, weights, heads, tokens):
    plane, each, width = x[0].shape
    group = 2 * plane * each
    lines = keys[0].shape[1]
    inputs = [*marks, *x, *keys, gain, cos, sin, *weights]
    return pl.pallas_call(
        functools.partial(attend_kernel, pack, heads, bool(marks), order, len(tokens)),
        out_shape=(
            jax.ShapeDtypeStruct((group, width), BF16),
            jax.ShapeDtypeStruct((heads, group, QDIM), BF16),
            jax.ShapeDtypeStruct((group, heads * HDIM), BF16),
            jax.ShapeDtypeStruct((heads, group, HDIM), F32),
        ),
        in_specs=smem_spec() + vmem_specs(len(inputs)) + any_spec() * len(tokens),
        out_specs=tuple(vmem_specs(4)),
        scratch_shapes=[pltpu.VMEM((heads, group, HDIM), F32)] * 3
        + [pltpu.VMEM((RANK, 2 * heads * HDIM), BF16)]
        + (
            []
            if marks
            else [
                pltpu.VMEM((heads, 2 * lines, group, group), F32),
                pltpu.VMEM((2 * lines, group, heads * HDIM), BF16),
            ]
        ),
        compiler_params=pltpu.CompilerParams(vmem_limit_bytes=60 * MIB),
        cost_estimate=pl.CostEstimate(
            flops=16_000_000_000, bytes_accessed=16_000_000, transcendentals=4_000_000
        ),
        name="attend",
    )(here, *inputs, *tokens)


def attend_back(pack, here, marks, orders, cos, sin, weights, out_weights, per_batch, token):
    batches, plane = len(orders), len(orders[0])
    lines = weights[0].shape[0]
    heads, group = per_batch[0][7].shape[:2]
    each, width = per_batch[0][0].shape[1:]
    size = pack.size
    outs = [jax.ShapeDtypeStruct((plane // 2, each, width), BF16)] * (2 * batches)
    outs += [jax.ShapeDtypeStruct((lines, batches, group, WIDE), BF16)] * 2
    outs += [jax.ShapeDtypeStruct((lines, pack.rows, size), BF16)] * 2
    inputs = [*marks, cos, sin, *weights, *out_weights]
    inputs += [v for args in per_batch for v in args]
    res = pl.pallas_call(
        functools.partial(attend_back_kernel, pack, heads, bool(marks), orders),
        out_shape=tuple(outs),
        in_specs=smem_spec() + vmem_specs(len(inputs)) + any_spec(),
        out_specs=tuple(vmem_specs(len(outs))),
        scratch_shapes=[
            pltpu.VMEM((heads, group, QDIM), F32),
            pltpu.VMEM((group, heads * QDIM), BF16),
            pltpu.VMEM((group, heads * HDIM), BF16),
            pltpu.VMEM((RANK, 2 * heads * HDIM), BF16),
            pltpu.VMEM((RANK, 2 * heads * HDIM), F32),
            pltpu.VMEM((2 * lines, size, heads * QDIM), F32),
            pltpu.VMEM((2 * lines, heads * HDIM, size), F32),
        ],
        compiler_params=pltpu.CompilerParams(vmem_limit_bytes=63 * MIB),
        cost_estimate=pl.CostEstimate(
            flops=32_000_000_000, bytes_accessed=30_000_000, transcendentals=8_000_000
        ),
        name="attend_back",
    )(here, *inputs, token)
    return res[: 2 * batches], res[2 * batches : 2 * batches + 2], res[2 * batches + 2 :]


def shared_kernel(s_ref, *refs):
    *pieces, gates_out, down_out = refs
    here = s_ref[0]
    _, kinds, rows, size = pieces[0].shape
    pad = down_out.shape[0]
    gates_out[...] = jnp.zeros_like(gates_out)
    down_out[...] = jnp.zeros_like(down_out)
    for k, ref in enumerate(pieces):
        for core in range(2):
            place = pl.multiple_of(((here // 2) ^ k) * (2 * size) + core * size, size)
            for kind in range(2):
                gates_out[kind * pad : kind * pad + rows, pl.ds(place, size)] = ref[core, kind]
            down_out[:rows, pl.ds(place, size)] = ref[core, 2]


def shared_whole(here, pieces, pad):
    width = 2 * len(pieces) * pieces[0].shape[-1]
    return pl.pallas_call(
        shared_kernel,
        out_shape=(
            jax.ShapeDtypeStruct((2 * pad, width), BF16),
            jax.ShapeDtypeStruct((pad, width), BF16),
        ),
        in_specs=smem_spec() + vmem_specs(len(pieces)),
        out_specs=tuple(vmem_specs(2)),
        cost_estimate=pl.CostEstimate(flops=0, bytes_accessed=4_000_000, transcendentals=0),
        name="shared_whole",
    )(here, *pieces)


def key_back_kernel(got, low_ref, gain, cos, sin, grad_out, gain_out):
    value = got[...]
    comp = low_ref[:, :RANK].astype(F32)
    inverse = rms_inverse(comp)
    hat = comp * inverse
    grad = value[:, :RANK]
    gain_out[...] = jnp.sum(grad * hat, axis=0, keepdims=True)
    scaled = grad * gain[...]
    grad = inverse * (scaled - hat * jnp.mean(scaled * hat, axis=-1, keepdims=True))
    first, second = value[:, RANK : RANK + HALF], value[:, RANK + HALF : RANK + RDIM]
    grad_out[...] = jnp.concatenate(
        [
            grad,
            first * cos[...] + second * sin[...],
            second * cos[...] - first * sin[...],
            jnp.zeros((value.shape[0], WIDE - RANK - RDIM), F32),
        ],
        axis=1,
    ).astype(BF16)


def key_back(got, low, gain, cos, sin):
    return pl.pallas_call(
        key_back_kernel,
        out_shape=(
            jax.ShapeDtypeStruct(got.shape, BF16),
            jax.ShapeDtypeStruct((1, RANK), F32),
        ),
        in_specs=vmem_specs(5),
        out_specs=tuple(vmem_specs(2)),
        name="key_back",
    )(got, low, gain, cos, sin)


def inputs_back_kernel(first, second, grad_latent, latent_t, x_ref, gain, residual, out, gain_out):
    grad = jnp.concatenate([first[...], second[...]], axis=0).astype(F32)
    grad = grad + dot(grad_latent[:, : RANK + RDIM], latent_t[...])
    x = x_ref[...].astype(F32)
    inverse = rms_inverse(x)
    hat = x * inverse
    gain_out[...] = jnp.sum(grad * hat, axis=0, keepdims=True)
    scaled = grad * gain[...]
    grad = inverse * (scaled - hat * jnp.mean(scaled * hat, axis=-1, keepdims=True))
    out[...] = (grad + residual[...]).astype(BF16)


def inputs_back(first, second, grad_latent, latent_t, x, gain, residual):
    return pl.pallas_call(
        inputs_back_kernel,
        out_shape=(
            jax.ShapeDtypeStruct(x.shape, BF16),
            jax.ShapeDtypeStruct(gain.shape, F32),
        ),
        in_specs=vmem_specs(7),
        out_specs=tuple(vmem_specs(2)),
        compiler_params=pltpu.CompilerParams(vmem_limit_bytes=40 * MIB),
        name="inputs_back",
    )(first, second, grad_latent, latent_t, x, gain, residual)


def latent_back_kernel(batches, plane, share, s_ref, *refs):
    refs = list(refs)
    grads, normed = take(refs, plane), take(refs, batches)
    gattn, gffn, glat, own_out, other_out, full = refs
    here, column = s_ref[0], s_ref[1]
    lines, rows, size = own_out.shape
    for b in range(batches):
        mine = jnp.concatenate([g[b, :, : RANK + RDIM] for g in grads], axis=0)
        term = dot_tn(mine, normed[b][...])
        full[...] = term if b == 0 else full[...] + term
    top = pl.multiple_of(column * share, 8)
    parts = RANK // size
    lat = [glat[:, i * size : (i + 1) * size] for i in range(parts)]
    blank = jnp.zeros((rows - share - 2 - parts, size), F32)
    for core, out in enumerate((own_out, other_out)):
        for line in range(lines):
            place = pl.multiple_of((here ^ (2 * line + core)) * size, size)
            columns = pl.ds(place, size)
            out[line] = jnp.concatenate(
                [full[pl.ds(top, share), columns], gattn[:, columns], gffn[:, columns], *lat, blank],
                axis=0,
            ).astype(BF16)


def latent_back(here, grads, normed, gains, lines, share):
    width = normed[0].shape[1]
    out = jax.ShapeDtypeStruct((lines, share + 16, width // (2 * lines)), BF16)
    return pl.pallas_call(
        functools.partial(latent_back_kernel, len(normed), len(grads), share),
        out_shape=(out, out),
        in_specs=smem_spec() + vmem_specs(len(grads) + len(normed) + 3),
        out_specs=tuple(vmem_specs(2)),
        scratch_shapes=[pltpu.VMEM((RANK + RDIM, width), F32)],
        compiler_params=pltpu.CompilerParams(vmem_limit_bytes=40 * MIB),
        cost_estimate=pl.CostEstimate(
            flops=2_000_000_000, bytes_accessed=5_000_000, transcendentals=0
        ),
        name="latent_back",
    )(here, *grads, *normed, *gains)


def feed_kernel(orders, per, side, aliased, *refs):
    refs = list(refs)
    slot, gate = take(refs, 2)
    xa, xb, ca, cb = [take(refs, 2) for _ in range(4)]
    wg, wu, wd, sgut, sd = take(refs, 5)
    came = take(refs, 2) if side == 0 else None
    take(refs, aliased + 1)
    rows_out, grows_out, act_out, gpre_out, gup_out, dsgut, dsd = take(refs, 7)
    pieces = refs
    plane, _, half, width = xa[0].shape
    plane = 2 * plane
    each = 2 * half
    group = plane * each
    cap = rows_out.shape[2]
    pad = sd.shape[0]

    @pl.when(pl.program_id(0) == 0)
    def _():
        dsgut[...] = jnp.zeros_like(dsgut)
        dsd[...] = jnp.zeros_like(dsd)

    picks, gates = [], []
    for i in range(per):
        chosen = lax.broadcasted_iota(jnp.int32, (cap, group), 0) == slot[i]
        gates.append(jnp.sum(jnp.where(chosen, gate[i], 0.0), axis=1, keepdims=True))
        picks.append(chosen.astype(F32))
    at_a, at_b = [[order.index(r) for r in range(plane)] for order in orders]

    def tokens_of(*pairs):
        found = [
            (i, *entry(pair, order, r))
            for i in range(per)
            for r in range(plane)
            for pair, order in zip(pairs, orders)
        ]
        return jnp.concatenate([ref[j, i] for i, ref, j in found], axis=0)

    x, cot = tokens_of(xa, xb), tokens_of(ca, cb)
    gates = jnp.concatenate(gates, axis=0)
    rows = jnp.concatenate(
        [
            dot(picks[i].astype(BF16), x[i * group : (i + 1) * group]).astype(BF16)
            for i in range(per)
        ],
        axis=0,
    )
    grows = jnp.concatenate(
        [dot(picks[i].astype(BF16), cot[i * group : (i + 1) * group]) for i in range(per)],
        axis=0,
    )
    grows = (grows * gates).astype(BF16)
    pre = dot_nt(rows, wg[...])
    upp = dot_nt(rows, wu[...])
    sig = 1.0 / (1.0 + jnp.exp(-pre))
    silu = pre * sig
    act = (silu * upp).astype(BF16)
    geact = dot_nt(grows, wd[...])
    gpre = (geact * upp * (sig * (1.0 + pre * (1.0 - sig)))).astype(BF16)
    gup = (geact * silu).astype(BF16)
    for i in range(per):
        part = slice(i * cap, (i + 1) * cap)
        rows_out[0, i] = rows[part]
        grows_out[0, i] = grows[part]
        act_out[0, i] = act[part]
        gpre_out[0, i] = gpre[part]
        gup_out[0, i] = gup[part]
    made = (dot(act, wd[...]) * gates).astype(BF16)
    gmade = (dot(gpre, wg[...]) + dot(gup, wu[...])).astype(BF16)
    both = dot_nt(x, sgut[...])
    spre, supp = both[:, :pad], both[:, pad:]
    ssig = 1.0 / (1.0 + jnp.exp(-spre))
    ssilu = spre * ssig
    sact = (ssilu * supp).astype(BF16)
    gsact = dot_nt(cot, sd[...])
    gspre = (gsact * supp * (ssig * (1.0 + spre * (1.0 - ssig)))).astype(BF16)
    gsupp = (gsact * ssilu).astype(BF16)
    gsboth = jnp.concatenate([gspre, gsupp], axis=1)
    dsgut[...] = dsgut[...] + dot_tn(gsboth, x)
    dsd[...] = dsd[...] + dot_tn(sact, cot)
    for i in range(per):
        back = picks[i].T.astype(BF16)
        toks = slice(i * group, (i + 1) * group)
        part = slice(i * cap, (i + 1) * cap)
        out = dot(
            jnp.concatenate([back, sact[toks]], axis=1),
            jnp.concatenate([made[part], sd[...]], axis=0),
        )
        gx = dot(
            jnp.concatenate([back, gsboth[toks]], axis=1),
            jnp.concatenate([gmade[part], sgut[...]], axis=0),
        )
        if side == 1:
            pieces[0][i] = out.astype(BF16)
            pieces[1][i] = gx.astype(BF16)
            continue
        out = (out + came[0][i].astype(F32)).astype(BF16)
        gx = (gx + came[1][i].astype(F32)).astype(BF16)
        for value, (keep_a, send_a, keep_b, send_b) in ((out, pieces[:4]), (gx, pieces[4:])):
            for r in range(plane):
                for part_of, at, both in ((0, at_a, (keep_a, send_a)), (1, at_b, (keep_b, send_b))):
                    top = r * each + part_of * half
                    ref = both[at[r] // (plane // 2)]
                    ref[at[r] % (plane // 2), i] = value[top : top + half]


def feed(
    here, orders, b, side, batches, cap, slot, gate, rows, cots, weights, came, earlier, token
):
    plane, lines, half, width = rows[0].shape
    plane = 2 * plane
    group = 2 * plane * half
    per = 2 if group <= 256 and lines % 2 == 0 else 1
    steps = lines // per
    hidden = weights[0].shape[0]
    pad = weights[-1].shape[0]

    def fixed(shape):
        return pl.BlockSpec(shape, lambda i: (0,) * len(shape), pipeline_mode=pl.Buffered(1))

    def block(count, size):
        return pl.BlockSpec((count, per, size, width), lambda i: (0, i, 0, 0))

    def saved(size):
        return pl.BlockSpec((1, per, cap, size), lambda i: (b, side * steps + i, 0, 0))

    mark = pl.BlockSpec((per, 1, group), lambda i: (i, 0, 0))
    flat = pl.BlockSpec((per, group, width), lambda i: (i, 0, 0))
    keep = [width, width, hidden, hidden, hidden]
    shapes = [jax.ShapeDtypeStruct((batches, 2 * lines, cap, size), BF16) for size in keep]
    shapes += [
        jax.ShapeDtypeStruct((2 * pad, width), F32),
        jax.ShapeDtypeStruct((pad, width), F32),
    ]
    out_specs = [saved(size) for size in keep] + [fixed((2 * pad, width)), fixed((pad, width))]
    if side == 1:
        shapes += [jax.ShapeDtypeStruct((lines, group, width), BF16)] * 2
        out_specs += [flat] * 2
    else:
        shapes += [jax.ShapeDtypeStruct((plane // 2, lines, half, width), BF16)] * 8
        out_specs += [block(plane // 2, half)] * 8
    in_specs = [mark, mark] + [block(plane // 2, half)] * 8
    in_specs += [fixed(w.shape) for w in weights]
    inputs = [slot, gate, *rows, *cots, *weights]
    if side == 0:
        in_specs += [flat] * 2
        inputs += list(came)
    aliases = {}
    for value, place in earlier:
        aliases[len(inputs)] = place
        inputs.append(value)
        in_specs += any_spec()
    inputs.append(token)
    in_specs += any_spec()
    return pl.pallas_call(
        functools.partial(feed_kernel, orders, per, side, len(earlier)),
        grid=(steps,),
        out_shape=tuple(shapes),
        in_specs=in_specs,
        out_specs=tuple(out_specs),
        input_output_aliases=aliases,
        compiler_params=pltpu.CompilerParams(vmem_limit_bytes=63 * MIB),
        cost_estimate=pl.CostEstimate(
            flops=24_000_000_000, bytes_accessed=40_000_000, transcendentals=1_000_000
        ),
        name="feed",
    )(*inputs)


def local(
    inputs,
    cotangent,
    routes,
    gate_weights,
    attn_gain,
    latent_gain,
    ffn_gain,
    query_proj,
    latent_proj,
    expand_proj,
    out_proj,
    shared_gate,
    shared_up,
    shared_down,
    expert_gate,
    expert_up_weight,
    expert_down,
):
    seq_count = lax.axis_size("seq")
    head_count = lax.axis_size("head")
    seq_index = lax.axis_index("seq")
    head_index = lax.axis_index("head")
    lines = depth()
    line, core = seq_index // 2, seq_index % 2
    batches, each, width = inputs.shape
    group = each * head_count
    heads = out_proj.shape[0] // HDIM
    serial = group > BLOCK
    here = jnp.stack([seq_index, head_index])
    positions = seq_index * group + jnp.arange(group, dtype=jnp.int32)
    away = jnp.arange(head_count, dtype=jnp.int32) ^ head_index

    shard = latent_proj.shape[0]
    pack = Pack(shard, heads, seq_count)
    n_lat = latent_gain.shape[0]
    lat_gain = lax.dynamic_update_slice_in_dim(
        jnp.zeros((RANK,), BF16), latent_gain, seq_index * n_lat, 0
    )
    unit = 16 * head_count
    lat_rows = -(-(RANK + RDIM + 16) // unit) * unit
    gain_part = jnp.concatenate(
        [attn_gain[None], ffn_gain[None], lat_gain.reshape(RANK // shard, shard)], axis=0
    )
    gain_part = jnp.pad(gain_part, ((0, lat_rows - RANK - RDIM - gain_part.shape[0]), (0, 0)))
    lat_mine = jnp.concatenate([jnp.transpose(latent_proj), gain_part], axis=0)
    lat_each = lat_rows // head_count
    lat_mine = lax.dynamic_slice_in_dim(lat_mine, head_index * lat_each, lat_each, 0)
    orders = [plane_order(False), plane_order(True)]
    lat_line = Sends("latent_weights", [lat_mine] * (lines - 1), "seq", [2 * k for k in range(1, lines)])
    xs_flow = Plane("inputs", inputs[0], inputs[1])
    phase = Phase(lat_line, xs_flow)

    pair = head_count // 2
    expert_ids = jnp.arange(seq_count, dtype=jnp.int32) * pair + head_index // 2
    hits = routes[None] == expert_ids[:, None, None, None]
    gate_of = jnp.sum(jnp.where(hits, gate_weights[None], 0.0), axis=-1)
    named = jnp.any(hits, axis=-1).astype(F32)
    both = jnp.stack([gate_of, named]).reshape(2, seq_count, batches, head_count, each)
    gate_of, named = jnp.take(both, away, axis=3).reshape(2, seq_count, batches, group)
    ahead = jnp.arange(group)[:, None] < jnp.arange(group)[None, :]
    rank = lax.dot_general(
        named.astype(BF16), ahead.astype(BF16), (((2,), (0,)), ((), ())), preferred_element_type=F32
    )
    gate_high = gate_of.astype(BF16)
    mark_mine = jnp.stack(
        [
            jnp.where(named > 0.0, jnp.minimum(rank, 255.0), -1.0).astype(BF16),
            gate_high,
            (gate_of - gate_high.astype(F32)).astype(BF16),
        ],
        axis=1,
    )
    mark_size = mark_mine.size
    mark_rows = -(-mark_size // (16 * shard)) * 16
    mark_mine = jnp.pad(mark_mine.reshape(-1), (0, mark_rows * shard - mark_size)).reshape(
        mark_rows, shard
    )

    cols = query_proj.reshape(query_proj.shape[0], heads, QDIM)
    query_mine = jnp.concatenate(
        [
            cols[..., :HDIM].reshape(-1, heads * HDIM),
            cols[..., HDIM : HDIM + HALF].reshape(-1, heads * HALF),
            cols[..., HDIM + HALF :].reshape(-1, heads * HALF),
        ],
        axis=1,
    )
    blocks = [query_mine[:, i * shard : (i + 1) * shard] for i in range(pack.query_parts)]
    blocks += [expand_proj[:, i * shard : (i + 1) * shard] for i in range(pack.expand_parts)]
    query_mine = jnp.concatenate(blocks[: pack.query_parts], axis=0)
    expand_mine = jnp.concatenate(blocks[pack.query_parts :], axis=0)
    out_mine = jnp.concatenate([out_proj, mark_mine], axis=0)

    lat_mine, query_mine = phase.end(lat_mine, query_mine)
    lat_stack = jnp.stack([lat_mine] + lat_line.held)
    lat_plane = head_send("latent_weights", [lat_stack] * (head_count - 1))
    query_flow = Line("query_weights", query_mine)
    lat_stack, out_mine = Phase(lat_plane, query_flow).end(lat_stack, out_mine)
    lat_own = [lat_stack] + lat_plane.held
    lat_core = core_send("latent_weights", lat_own)
    cot_lines = [None, None]
    if not serial:
        (cot_mine,) = sync(after(cotangent, lat_stack))
        cot_lines = [Line("cotangents", cot_mine[b]) for b in range(batches)]
    cot_phase = Phase(cot_lines[0])
    Phase(lat_core).end()
    lat_other = lat_core.held

    cos_all, sin_all = rope_tables(positions)
    own_cos, own_sin = [
        lax.dynamic_slice_in_dim(t, head_index * each, each, 0) for t in (cos_all, sin_all)
    ]
    own_keys, own_latent, gain_attn, gain_ffn, gain_lat, latent_t = own_latents(
        here,
        inputs.reshape(batches * each, width),
        jnp.tile(own_cos, (batches, 1)),
        jnp.tile(own_sin, (batches, 1)),
        lat_own,
        lat_other,
    )
    own_keys = own_keys.reshape(batches, each, WIDE)
    key_flow = Line("keys", own_keys)
    (own_keys,) = cot_phase.end(own_keys)
    key_flow = Line("keys", own_keys)
    (expand_mine,) = Phase(key_flow, query_flow, xs_flow).end(expand_mine)
    expand_flow = Line("expand_weights", expand_mine)
    run(query_flow)
    query_core = core_send("query_weights", [query_flow.held])
    Phase(key_flow, expand_flow, query_core).end()
    run(key_flow)
    run(query_flow)
    key_plane = Plane("keys", key_flow.held[:, 0], key_flow.held[:, 1])
    shared_mine = jnp.stack(
        [
            jnp.transpose(shared_gate).reshape(seq_count, -1, shard),
            jnp.transpose(shared_up).reshape(seq_count, -1, shard),
            shared_down.reshape(seq_count, -1, shard),
        ],
        axis=1,
    ).reshape(lines, 2, 3, -1, shard)
    out_mine, shared_mine = Phase(key_plane, expand_flow, cot_lines[0]).end(out_mine, shared_mine)
    out_flow = Line("output_weights", out_mine)
    run(expand_flow)
    expand_core = core_send("expand_weights", [expand_flow.held])
    shared_kept = pick(shared_mine, core, 1)
    shared_core = core_send("shared_weights", [pick(shared_mine, core ^ 1, 1)])
    Phase(key_plane, out_flow, expand_core, shared_core).end()
    while key_plane.more:
        Phase(key_plane).end()
    key_core = core_send("keys", key_plane.held)
    first_weights = (query_flow.held, query_core.held[0], expand_flow.held, expand_core.held[0])
    Phase(key_core).end()
    keys = [(*key_plane.held[2 * b : 2 * b + 2], *key_core.held[2 * b : 2 * b + 2]) for b in range(2)]
    xs = run(xs_flow)[0]
    xs = [xs[:2], xs[2:]]

    own_rows = inputs.astype(F32)
    own_inverse = rms_inverse(own_rows)
    own_hat = own_rows * own_inverse
    cos_b, sin_b = [
        jnp.tile(
            jnp.take(t.reshape(head_count, each, HALF), away, axis=0).reshape(group, HALF),
            (1, heads),
        )
        for t in (cos_all, sin_all)
    ]
    marks = ()
    if group > BLOCK:
        place = (away[:, None] * each + jnp.arange(each, dtype=jnp.int32)[None, :]).reshape(group)
        own_block = (seq_index * group + place) // BLOCK
        offsets = jnp.arange(seq_count, dtype=jnp.int32) ^ seq_index
        key_block = (offsets[:, None] * group + place[None, :]) // BLOCK
        marks = (jnp.broadcast_to(own_block[:, None], (group, group)), key_block)
    half = each // 2
    saved, residual, ffn_hat, ffn_inverse = [], [], [], []

    def attend_batch(b, tokens):
        saved.append(
            attend(
                pack, here, marks, orders[b], xs[b], gain_attn, cos_b, sin_b, keys[b],
                first_weights, heads, tokens,
            )
        )
        return saved[-1][2]

    def ffn_rows(b, parts, got):
        total = parts[0].astype(F32)
        for value in got:
            total = total + value.astype(F32)
        residual_b = own_rows[b] + total
        inverse_b = rms_inverse(residual_b)
        hat_b = residual_b * inverse_b
        residual.append(residual_b)
        ffn_inverse.append(inverse_b)
        ffn_hat.append(hat_b)
        return Line("ffn_rows", (hat_b * gain_ffn).astype(BF16))

    def halves_of(name, value, hold=False):
        return Plane(name, value[:, :half], value[:, half:], hold)

    def keep(b, att):
        saved[b] = (*saved[b][:2], att, saved[b][3])
        return att

    cots = [None, None]
    if not serial:
        cots[0] = halves_of("cotangents", run(cot_lines[0])[0])
    window = Phase(out_flow, cots[0], cot_lines[1])
    att0 = attend_batch(0, [key_core.held[0]])
    att0 = keep(0, window.end(att0)[0])
    run(out_flow)
    out_core = core_send("output_weights", [out_flow.held])
    att0 = keep(0, Phase(out_core).end(att0)[0])
    out_weights = (out_flow.held, out_core.held[0])
    parts0 = project(pack, here, att0, out_weights, head_count, [])
    sum0 = head_send("attention_sum", parts0[1:])
    window = Phase(sum0, cots[0])
    att1 = attend_batch(1, [parts0[0]])
    att1, own0 = window.end(att1, parts0[0])
    keep(1, att1)
    parts1 = project(pack, here, att1, out_weights, head_count, [])
    rows = [ffn_rows(0, [own0], sum0.held)]
    sum1 = head_send("attention_sum", parts1[1:])
    came = shared_core.held[0]
    paired = jnp.where(
        core == 0, jnp.stack([shared_kept, came], 1), jnp.stack([came, shared_kept], 1)
    )
    cot_held = [] if serial else run(cots[0])[0]
    own1, paired, *cot_held = Phase(sum1, rows[0], cot_lines[1]).end(parts1[0], paired, *cot_held)
    rows.append(ffn_rows(1, [own1], sum1.held))

    def moves_of(paired):
        return Sends(
            "shared_weights",
            [pick(paired, line ^ k) for k in range(1, lines)],
            "seq",
            [2 * k for k in range(1, lines)],
        )

    if serial:
        run(rows[0])
        shared_moves = moves_of(paired)
        run(shared_moves)
    else:
        cots[0].held = cot_held
        cot_core = [core_send("cotangents", cots[0].held), None]
        cot_late = run(cot_lines[1])[0]
        cot_late, paired = Phase(rows[0], rows[1], cot_core[0]).end(cot_late, paired)
        row_planes = [halves_of("ffn_rows", run(rows[0])[0]), None]
        cot_late, paired = Phase(row_planes[0], rows[1]).end(cot_late, paired)
        row_late = run(rows[1])[0]
        shared_moves = moves_of(paired)
        cot_late, row_late = Phase(row_planes[0], shared_moves).end(cot_late, row_late)
        run(row_planes[0])
        row_core = [core_send("ffn_rows", row_planes[0].held), None]
        cot_late, row_late = Phase(row_core[0]).end(cot_late, row_late)
        cots[1] = halves_of("cotangents", cot_late, True)
        row_planes[1] = halves_of("ffn_rows", row_late, True)
    hidden_each = shared_gate.shape[1] // seq_count
    hidden_pad = -(-hidden_each // 128) * 128
    sgut, sdown = shared_whole(here, [pick(paired, line)] + shared_moves.held, hidden_pad)
    weights = (
        jnp.transpose(expert_gate[0]),
        jnp.transpose(expert_up_weight[0]),
        expert_down[0],
        sgut,
        sdown,
    )

    def marks_from(parts):
        flat = parts[:, pack.out_rows :].reshape(lines, -1)
        flat = flat[:, :mark_size]
        return pick(flat.reshape(lines, seq_count, 3, batches, 1, group), seq_index, 1).astype(F32)

    marks_mine = [marks_from(parts) for parts in out_weights]
    slots = [m[:, 0].astype(jnp.int32) for m in marks_mine]
    gates = [m[:, 1] + m[:, 2] for m in marks_mine]
    most_rows = 4 * group * TOPK // (3 * seq_count * pair)
    state = {"kept": [], "dsgut": 0.0, "dsd": 0.0}

    def run_feed(b, side, rows_b, cots_b, came, token):
        earlier = [(v, i) for i, v in enumerate(state["kept"])]
        res = feed(
            here, orders, b, side, batches, most_rows, slots[side][:, b], gates[side][:, b],
            rows_b, cots_b, weights, came, earlier, token,
        )
        state["kept"] = res[:5]
        state["dsgut"] = state["dsgut"] + res[5]
        state["dsd"] = state["dsd"] + res[6]
        return res[7:]

    def collect(name, values):
        return PlaneSum(name, values[:2], values[2:])

    def lines_of(name, flow):
        return LineSum(name, jnp.concatenate(flow.held, axis=1))

    def whole_sum(name, values):
        flow = collect(name, values)
        run(flow)
        return run(lines_of(name, flow))[0]

    if serial:
        grad_ffn, outs = [], []
        for b in range(batches):
            tokens = [grad_ffn[b - 1], outs[b - 1]] if b else []
            row_line = run(rows[b])[0]
            line_b = cotangent[b]
            if b:
                row_line, line_b = after(row_line, *tokens), after(line_b, *tokens)
            line_b = run(Line("cotangents", line_b))[0]
            row_plane, cot_plane = halves_of("ffn_rows", row_line), halves_of("cotangents", line_b)
            row_own, cot_own = run(row_plane, cot_plane)
            row_other = run(core_send("ffn_rows", row_own))[0]
            cot_other = run(core_send("cotangents", cot_own))[0]
            made = run_feed(b, 1, row_other, cot_other, None, row_own[0])
            came = run(core_send("feed_other", made))[0]
            made = run_feed(b, 0, row_own, cot_own, came, row_own[0])
            grad_ffn.append(whole_sum("ffn_grads", made[4:]))
            outs.append(whole_sum("outputs", made[:4]))
        kept = state["kept"]
        rows, grows, act, gpre, gup = [v.reshape(-1, v.shape[-1]) for v in kept]
        exgate_grad = dot_tn(gpre, rows)
        exup_grad = dot_tn(gup, rows)
        exdown_grad = dot_tn(act, grows)
    else:
        phase = Phase(cots[1], row_planes[1])
        made = run_feed(0, 1, row_core[0].held, cot_core[0].held, None, row_core[0].held[0])
        made = phase.end(*made)
        other = core_send("feed_other", made)
        phase = Phase(cots[1])
        Phase(other).end()
        late = Phase(row_planes[1])
        made0 = run_feed(0, 0, row_planes[0].held, cots[0].held, other.held, other.held[0])
        made0 = phase.end(*made0)
        made0 = late.end(*made0)
        run(cots[1], row_planes[1])
        cot_core[1] = core_send("cotangents", cots[1].held)
        row_core[1] = core_send("ffn_rows", row_planes[1].held)
        grads = [collect("ffn_grads", made0[4:]), None]
        phase = Phase(grads[0])
        Phase(cot_core[1], row_core[1]).end()
        made = run_feed(1, 1, row_core[1].held, cot_core[1].held, None, row_core[1].held[0])
        made = phase.end(*made)
        other = core_send("feed_other", made)
        outs = [collect("outputs", made0[:4]), None]
        phase = Phase(grads[0])
        Phase(other).end()
        out_phase = Phase(outs[0])
        made1 = run_feed(1, 0, row_planes[1].held, cots[1].held, other.held, other.held[0])
        made1 = phase.end(*made1)
        run(grads[0])
        grad_line = [lines_of("ffn_grads", grads[0]), None]
        grads[1] = collect("ffn_grads", made1[4:])
        phase = Phase(grad_line[0], grads[1])
        kept = state["kept"]
        rows, grows, act, gpre, gup = [v.reshape(-1, v.shape[-1]) for v in kept]
        exgate_grad = dot_tn(after(gpre, made1[0]), rows)
        exgate_grad, gup = phase.end(exgate_grad, gup)
        phase = Phase(grad_line[0], grads[1])
        exup_grad = dot_tn(gup, rows)
        exup_grad, act = phase.end(exup_grad, act)
        run(grads[1], grad_line[0])
        grad_line[1] = lines_of("ffn_grads", grads[1])
        (grows,) = out_phase.end(grows)
        phase = Phase(grad_line[1], outs[0])
        exdown_grad = dot_tn(act, grows)
        (exdown_grad,) = phase.end(exdown_grad)
        run(grad_line[1])
        grad_ffn = [flow.held for flow in grad_line]
        outs[1] = collect("outputs", made1[:4])
    exgate_grad = jnp.transpose(exgate_grad)[None]
    exup_grad = jnp.transpose(exup_grad)[None]
    exdown_grad = exdown_grad[None]
    dsgut, dsd = state["dsgut"], state["dsd"]

    ffn_hat, ffn_inverse = jnp.stack(ffn_hat), jnp.stack(ffn_inverse)
    grad_two, ffngain_term = norm_back(jnp.stack(grad_ffn), ffn_hat, ffn_inverse, gain_ffn)
    grad_residual = cotangent.astype(F32) + grad_two
    grad_attention = grad_residual.astype(BF16)
    shared_term = jnp.concatenate([dsgut.reshape(2, hidden_pad, width), dsd[None]], axis=0)
    shared_term = shared_term[:, :hidden_each].astype(BF16)
    shared_term = jnp.transpose(
        shared_term.reshape(3, hidden_each, lines, 2, shard), (2, 3, 0, 1, 4)
    )

    gres_flow = Plane("attention_grads", grad_attention[0], grad_attention[1])
    if serial:
        run(gres_flow)
    else:
        Phase(gres_flow).end()
        run(outs[0])
        out_line = [lines_of("outputs", outs[0]), None]
        Phase(gres_flow, out_line[0]).end()
        run(gres_flow)
    gres = gres_flow.held
    token = gres[0]
    if not serial:
        shared_sent = Sends(
            "shared_grads",
            [pick(shared_term, line ^ k) for k in range(1, lines)],
            "seq",
            [2 * k for k in range(1, lines)],
        )
        window = Phase(outs[1], shared_sent)

    per_batch = [(*gres[2 * b : 2 * b + 2], *keys[b], *saved[b]) for b in range(batches)]
    groups = [[b] for b in range(batches)] if serial else [list(range(batches))]
    calls = [
        attend_back(
            pack, here, marks, [orders[b] for b in g], cos_b, sin_b, first_weights, out_weights,
            [per_batch[b] for b in g], token,
        )
        for g in groups
    ]
    if serial:
        gparts = [v for c in calls for v in c[0]]
        gkeys = [jnp.concatenate(v, axis=1) for v in zip(*[c[1] for c in calls])]
        dweights = [
            sum(v.astype(F32) for v in t).astype(BF16) for t in zip(*[c[2] for c in calls])
        ]
        shared_sent = Sends(
            "shared_grads",
            [pick(shared_term, line ^ k) for k in range(1, lines)],
            "seq",
            [2 * k for k in range(1, lines)],
        )
        run(shared_sent)
    else:
        made = window.end(*[v for group_of in calls[0] for v in group_of])
        gparts, gkeys, dweights = made[: 2 * batches], made[-4:-2], made[-2:]
    weight_core = core_send("weight_grads", [dweights[1]])
    key_core = core_send("key_grads", [gkeys[1]])
    late = None if serial else outs[1]
    gkey, dweight_own = Phase(key_core, weight_core).end(gkeys[0], dweights[0])
    both = [
        (
            gkey[:, :, r * each : (r + 1) * each].astype(F32)
            + key_core.held[0][:, :, r * each : (r + 1) * each].astype(F32)
        ).astype(BF16)
        for r in range(head_count)
    ]
    key_plane = head_send("key_grads", both[1:])
    weight_both = (dweight_own.astype(F32) + weight_core.held[0].astype(F32)).astype(BF16)
    weight_line = LineSum("weight_grads", weight_both)
    ends = [both[0], *gparts]
    if late is not None and late.more:
        ends += [v for pair in late.held for v in pair]
    both0, *ends = Phase(key_plane, weight_line).end(*ends)
    gparts = ends[: 2 * batches]
    if late is not None and late.more:
        late.held = [ends[-4:-2], ends[-2:]]
    total = both0.astype(F32)
    for value in key_plane.held:
        total = total + value.astype(F32)
    key_line = LineSum("key_grads", total.astype(BF16))
    normed_sum = PlaneSum("normed_grads", gparts[:2], gparts[2:])
    Phase(key_line, normed_sum, None if serial else out_line[0]).end()
    while key_line.more:
        Phase(key_line, normed_sum, late).end()
    run(normed_sum)
    own_tiled = [jnp.tile(t, (batches, 1)) for t in (own_cos, own_sin)]
    grad_latent, latgain_term = key_back(
        key_line.held.reshape(batches * each, WIDE), own_latent, gain_lat, *own_tiled
    )
    latent_send = head_send(
        "latent_grads", [grad_latent.reshape(batches, each, WIDE)] * (head_count - 1)
    )
    if serial:
        run(latent_send)
    else:
        run(outs[1])
        out_line[1] = lines_of("outputs", outs[1])
        Phase(latent_send).end()
    weights_phase = Phase(weight_line)
    inputs_grad, attngain_term = inputs_back(
        *normed_sum.held, grad_latent, latent_t, inputs.reshape(batches * each, width),
        gain_attn, grad_residual.reshape(batches * each, width),
    )
    inputs_grad = inputs_grad.reshape(batches, each, width)

    share = (RANK + RDIM) // head_count
    latent_own, latent_other = latent_back(
        here,
        [grad_latent.reshape(batches, each, WIDE)] + latent_send.held,
        [kept_b[0] for kept_b in saved],
        (attngain_term, ffngain_term.reshape(1, width), latgain_term),
        lines,
        share,
    )
    latent_core = core_send("latent_grads", [latent_other])
    shared_held = jnp.stack([pick(shared_term, line)] + shared_sent.held)
    shared_core = core_send("shared_grads", [pick(shared_held, core ^ 1, 1)])
    (latent_own,) = Phase(latent_core, shared_core).end(latent_own)
    (latent_own,) = weights_phase.end(latent_own)
    both = (latent_own.astype(F32) + latent_core.held[0].astype(F32)).astype(BF16)
    latent_line = LineSum("latent_grads", both)
    Phase(latent_line, None if serial else out_line[1]).end()
    (latent_mine,) = run(latent_line)
    latent_mine = latent_mine.astype(BF16)
    latent_last = head_send("latent_grads", [latent_mine] * (head_count - 1))
    (latent_mine,) = Phase(latent_last).end(latent_mine)
    if serial:
        run(weight_line)
    else:
        run(weight_line, out_line[0], out_line[1])
    latent_parts = [latent_mine] + latent_last.held
    dweight = weight_line.held
    query_grad = jnp.concatenate(
        [dweight[i * shard : (i + 1) * shard] for i in range(pack.query_parts)], axis=1
    )
    nope = heads * HDIM
    query_grad = jnp.concatenate(
        [
            query_grad[:, :nope].reshape(-1, heads, HDIM),
            query_grad[:, nope : nope + heads * HALF].reshape(-1, heads, HALF),
            query_grad[:, nope + heads * HALF :].reshape(-1, heads, HALF),
        ],
        axis=-1,
    ).reshape(-1, heads * QDIM)
    expand_grad = jnp.concatenate(
        [
            dweight[pack.expand_at + i * pack.rank : pack.expand_at + (i + 1) * pack.rank]
            for i in range(pack.expand_parts)
        ],
        axis=1,
    )
    outproj_grad = dweight[pack.out_at :]

    latent_grad = jnp.zeros((head_count, share, shard), BF16)
    gain_grad = 0.0
    for k in range(head_count):
        latent_grad = lax.dynamic_update_slice_in_dim(
            latent_grad, latent_parts[k][None, :share], head_index ^ k, 0
        )
        gain_grad = gain_grad + latent_parts[k][share:].astype(F32)
    latent_grad = jnp.transpose(latent_grad.reshape(RANK + RDIM, shard)).astype(F32)
    attngain_grad = gain_grad[0]
    ffngain_grad = gain_grad[1]
    lat_grads = gain_grad[2 : 2 + RANK // shard].reshape(RANK)
    latgain_grad = lax.dynamic_slice_in_dim(lat_grads, seq_index * n_lat, n_lat)

    kept, came = pick(shared_held, core, 1), shared_core.held[0]
    paired = jnp.where(core == 0, jnp.stack([kept, came], 1), jnp.stack([came, kept], 1))
    shared_grad = jnp.zeros(paired.shape, BF16)
    for k in range(lines):
        shared_grad = lax.dynamic_update_slice_in_dim(shared_grad, paired[k : k + 1], line ^ k, 0)
    shared_grad = jnp.transpose(shared_grad, (2, 0, 1, 3, 4)).reshape(3, -1, shard).astype(F32)
    shgate_grad = jnp.transpose(shared_grad[0])
    shup_grad = jnp.transpose(shared_grad[1])
    shdown_grad = shared_grad[2]

    if not serial:
        outs = [flow.held for flow in out_line]
    output = (jnp.stack(residual) + jnp.stack(outs)).astype(BF16)

    return (
        output,
        inputs_grad,
        query_grad,
        latent_grad,
        expand_grad,
        outproj_grad,
        shgate_grad,
        shup_grad,
        shdown_grad,
        exgate_grad,
        exup_grad,
        exdown_grad,
        attngain_grad,
        latgain_grad,
        ffngain_grad,
    )


def solution(mesh):
    own = P(None, ("seq", "head"), None)
    stack = P(("seq", "head"), None, None)
    return jax.shard_map(
        local,
        mesh=mesh,
        in_specs=(
            own,
            own,
            P(None, "seq", None),
            P(None, "seq", None),
            P("seq"),
            P("seq"),
            P("seq"),
            P("seq", "head"),
            P("seq", None),
            P("seq", "head"),
            P("head", "seq"),
            P("seq", "head"),
            P("seq", "head"),
            P("head", "seq"),
            stack,
            stack,
            stack,
        ),
        out_specs=(
            own,
            own,
            P("seq", "head"),
            P("seq", None),
            P("seq", "head"),
            P("head", "seq"),
            P("seq", "head"),
            P("seq", "head"),
            P("head", "seq"),
            stack,
            stack,
            stack,
            P("seq"),
            P("seq"),
            P("seq"),
        ),
        check_vma=False,
    )
```
